32 devices in a mesh: section: 2 (over x), dp: 16 (over z, y, core).
Axes of the slice: x: 2, y: 2, z: 4, core: 2. Of those that a mesh axis runs over, the one named last changes fastest.
Arguments:
- entering: bfloat16 [2, 2, 6144, 1280], P('section', None, 'dp'), may hold values from -6 to 6
- deal: int32 [2, 6144], P(None, 'dp'), may hold values from 0 to 6143, as said below
- seq_lens: int32 [2, 16, 3], P(None, 'dp'), may hold values from 1 to 256, 384 in all within a row
- mats: float32 [2, 7680, 1280], P('section', 'dp')
- gains: float32 [2, 2560], P('section', 'dp'), may hold values from 0.1 to 1.9
- biases: float32 [2, 2560], P('section', 'dp'), may hold values from -3 to 3
Outputs:
- results: bfloat16 [2, 2, 6144, 1280], P('section', None, 'dp')
- mats_grad: float32 [2, 7680, 1280], P('section', 'dp')
- gains_grad: float32 [2, 2560], P('section', 'dp')
- biases_grad: float32 [2, 2560], P('section', 'dp')
The draws below stay inside these ranges and needn't reach their ends.
Inputs may be any that keep to these rules, and one draw needn't show every extreme that they name: `deal`: for each micro-batch a permutation of the rows; the dealt rows of each block of 384 take exactly 24 = 24 rows from each block of 384 arrival rows. `seq_lens`: each device's 3 lengths of a micro-batch sum to 384.
All inputs are finite; a program needn't handle non-finite values.
Results may differ from the reference program's by a relative error of at most 0.018.
Values may be sent and summed in bfloat16 or wider, within the bound.
A program may use at most 384 MiB of HBM per device.

```python
import math
import jax
import jax.numpy as jnp
import numpy as np
from jax import lax

D = 1280
HEADS = 16
TOK_DEV = 384
MB = 2
SLOTS = 3
SEQ_MAX = 256
TOKENS = 6144
N_SECTION = 2
N_DP = 16


def draw_deal(key, part):
    key = jax.random.fold_in(key, 11)
    per_peer = TOK_DEV // N_DP

    def one_batch(batch_key):
        slot_key, row_key = jax.random.split(batch_key)
        orders = jax.vmap(lambda member: jax.random.permutation(member, TOK_DEV))(jax.random.split(slot_key, N_DP))
        picks = jax.vmap(lambda member: jax.random.permutation(member, TOK_DEV))(jax.random.split(row_key, N_DP))
        entries = jnp.arange(TOK_DEV, dtype=jnp.int32)
        source_dev = entries // per_peer
        offsets = entries % per_peer
        targets = jnp.arange(N_DP, dtype=jnp.int32)
        source_row = picks[source_dev[None, :], targets[:, None] * per_peer + offsets[None, :]]
        global_src = (source_dev[None, :] * TOK_DEV + source_row).astype(jnp.int32)
        placed = jax.vmap(lambda order, value: jnp.zeros((TOK_DEV,), jnp.int32).at[order].set(value))(orders, global_src)
        return placed.reshape(N_DP * TOK_DEV)
    return jax.vmap(one_batch)(jax.random.split(key, MB)).astype(jnp.int32)


def draw_mats(key, part):
    key = jax.random.fold_in(key, 7)
    base = jax.random.normal(key, (N_SECTION, 6, D, D), jnp.float32)
    boost = jnp.array([1.0, 1.0, 1.0, 4.0, 1.0, 1.0], jnp.float32)
    return (base * boost[None, :, None, None] * D ** (-0.5)).reshape(N_SECTION, 6 * D, D)


def block_levels(stream_key, extent, cuts, least, top_value):
    level = 1.0
    for axis_at, parts in cuts:
        heights = jax.random.uniform(jax.random.fold_in(jax.random.fold_in(stream_key, 6), axis_at), (parts,), jnp.float32, least / len(cuts), top_value / len(cuts))
        level = level * jnp.repeat(jnp.exp(heights), extent[axis_at] // parts).reshape((-1,) + (1,) * (len(extent) - 1 - axis_at))
    return level


def length_profile(amount, total, limit, lean):
    loads = [(1 << 20) // math.isqrt(rank ** lean) + 1 for rank in range(2, amount + 1)]
    spare, given = total - limit - (amount - 1), [1] * (amount - 1)
    while spare > 0:
        candidates = [i for i in range(amount - 1) if given[i] < limit]
        whole, left = sum([loads[i] for i in candidates]), spare
        for i in candidates:
            extra = min(limit - given[i], max(1, left * loads[i] // whole), spare)
            given[i] = given[i] + extra
            spare = spare - extra
    return np.array([limit] + given)


def ragged_sizes(own_key, count, total, limit, skew):
    if count == 2:
        one = jax.random.randint(own_key, (), max(1, total - limit), min(limit, total - 1) + 1)
        return jnp.stack([one, total - one])
    tallies = jnp.asarray(length_profile(count, total, limit, skew), jnp.int32)
    twos = (count - 1) // 2
    source_of, receiver = tallies[1:1 + 2 * twos:2], tallies[2:2 + 2 * twos:2]
    margin = jnp.minimum(source_of - 1, limit - receiver)
    moved = jax.random.randint(jax.random.fold_in(own_key, 1), (twos,), 0, 1 << 20) % (margin + 1)
    tallies = tallies.at[1:1 + 2 * twos:2].set(source_of - moved).at[2:2 + 2 * twos:2].set(receiver + moved)
    return tallies[jax.random.permutation(jax.random.fold_in(own_key, 2), count)]


def gaussian(key, extent, deviation, limit, cuts=(), held_as=jnp.bfloat16):
    values = jax.random.normal(key, extent, jnp.float32) * deviation
    if len(cuts) > 0:
        values = block_levels(key, extent, cuts, -0.22, 0.18) * values
    return jnp.clip(values, min=-limit, max=limit).astype(held_as)


def setup_inputs(seed: int = 0) -> dict:
    streams_of = jax.random.split(jax.random.key(seed), 7)
    entering = gaussian(streams_of[0], (N_SECTION, MB, TOKENS, D), 1.0, 6.0, ((0, 2), (2, 16)))
    deal = draw_deal(jax.random.fold_in(streams_of[6], 71), 0)
    seq_lens = jax.vmap(lambda own: ragged_sizes(own, SLOTS, TOK_DEV, SEQ_MAX, 2))(jax.random.split(streams_of[2], MB * N_DP)).reshape((MB, N_DP, SLOTS)).astype(jnp.int32)
    mats = draw_mats(jax.random.fold_in(streams_of[6], 71), 0)
    gains = jnp.clip(1.0 + 0.18 * jax.random.normal(streams_of[4], (N_SECTION, 2 * D), jnp.float32), 0.1, 1.9)
    biases = gaussian(streams_of[5], (N_SECTION, 2 * D), 0.5, 3.0, ((0, 2), (1, 16)), jnp.float32)
    return {"entering": entering, "deal": deal, "seq_lens": seq_lens, "mats": mats, "gains": gains, "biases": biases}


@jax.custom_vjp
def low(v):
    return lax.optimization_barrier(v.astype(jnp.bfloat16)).astype(jnp.float32)

@jax.custom_vjp
def low_back(v):
    return v

def low_keep(v):
    return (low(v), None)

def low_pass(kept, grad):
    return (grad,)

def back_keep(v):
    return (v, None)

def back_low(kept, grad):
    return (low(grad),)
low.defvjp(low_keep, low_pass)
low_back.defvjp(back_keep, back_low)
EPS = 1e-06
NEG = -1000000000.0

def normed(value, gain):
    return value * lax.rsqrt(lax.optimization_barrier(jnp.mean(value * value, axis=-1, keepdims=True)) + EPS) * gain

def mul_high(left, right):
    return jnp.dot(left, right, precision=lax.Precision.HIGHEST)

def block_layer(hidden, segment, weights):
    w_query, w_key, w_value, w_mix, w_inner, w_outer, gain_one, gain_two, bias_inner, bias_outer = weights
    row_count = hidden.shape[0]
    depth = D // HEADS
    scale = depth ** (-0.5)
    first = low(normed(hidden, gain_one))
    query = low_back(low(mul_high(first, w_query))).reshape(row_count, HEADS, depth)
    keys = low_back(low(mul_high(first, w_key))).reshape(row_count, HEADS, depth)
    values = low_back(low(mul_high(first, w_value))).reshape(row_count, HEADS, depth)
    scores = low_back(jnp.einsum('qhd,khd->hqk', query, keys, precision=lax.Precision.HIGHEST) * scale)
    positions = jnp.arange(row_count, dtype=jnp.int32)
    allowed = (segment[:, None] == segment[None, :]) & (positions[None, :] <= positions[:, None])
    scores = jnp.where(allowed[None], scores, NEG)
    top_score = lax.optimization_barrier(jnp.max(scores, axis=-1, keepdims=True))
    expd = jnp.exp(scores - top_score)
    probs = low(expd / lax.optimization_barrier(jnp.sum(expd, axis=-1, keepdims=True)))
    attended = jnp.einsum('hqk,khd->qhd', probs, values, precision=lax.Precision.HIGHEST).reshape(row_count, D)
    attended = low_back(low(attended))
    middle = hidden + low_back(mul_high(attended, w_mix))
    second = low(normed(middle, gain_two))
    inner = low_back(mul_high(second, w_inner) + bias_inner)
    active = low(jax.nn.gelu(inner, approximate=True))
    return middle + low_back(mul_high(active, w_outer) + bias_outer)

def reference(entering, deal, seq_lens, mats, gains, biases):
    inputs = entering[0].astype(jnp.float32)
    cotangent = entering[1].astype(jnp.float32)
    seg_ends = jnp.cumsum(seq_lens, axis=-1).astype(jnp.int32)
    positions = jnp.arange(TOK_DEV, dtype=jnp.int32)
    segments = lax.optimization_barrier(jnp.sum((positions[None, None, :, None] >= seg_ends[:, :, None, :]).astype(jnp.int32), axis=-1))
    segments = segments.reshape(MB * N_DP, TOK_DEV).astype(jnp.int32)
    batch_index = jnp.arange(MB, dtype=jnp.int32)[:, None]
    deal_index = deal.astype(jnp.int32)

    def forward(inputs, mats, gains, biases):
        state = jnp.take_along_axis(inputs, deal_index[:, :, None], axis=1)
        state = state.reshape(MB * N_DP, TOK_DEV, D)
        for section_number in range(N_SECTION):
            if section_number > 0:
                state = low_back(low(state))
            section_mats = mats[section_number].reshape(6, D, D)
            section_gains = gains[section_number].reshape(2, D)
            section_biases = biases[section_number].reshape(2, D)
            weights = tuple((low(section_mats[index]) for index in range(6))) + (low(section_gains[0]), low(section_gains[1]), low(section_biases[0]), low(section_biases[1]))

            def one_block(pair, weights=weights):
                return block_layer(pair[0], pair[1], weights)
            state = lax.map(jax.checkpoint(one_block), (state, segments))
        outcome = state.reshape(MB, TOKENS, D)
        return jnp.zeros_like(outcome).at[batch_index, deal_index].set(outcome)
    outputs, pull_back = jax.vjp(forward, inputs, mats, gains, biases)
    grad_inputs, grad_mats, grad_gains, grad_biases = pull_back(cotangent)
    results = jnp.stack([grad_inputs, outputs]).astype(jnp.bfloat16)
    return (results, grad_mats, grad_gains, grad_biases)
```

```python
import functools

import jax
import jax.numpy as jnp
from jax import lax
from jax.experimental import pallas as pl
from jax.experimental.pallas import tpu as pltpu
from jax.sharding import PartitionSpec as P

HEADS = 16
EPS = 1e-06
NEG = -1000000000.0
BOTH = ("section", "dp")
MESH = pl.DeviceIdType.MESH
PARTS = ((0, 112, "zxy"), (112, 112, "zyx"), (224, 128, "xzy"), (352, 128, "yzx"))


def coords():
    s=lax.axis_index("section"); d=lax.axis_index("dp")
    return s,d,d//4,(d//2)%2,d%2

def items():
    out=[]
    for bx in (0,1):
        for by in (0,1):
            for dz in (0,-1,1,-2,2,-3,3):
                out.append((bx,by,dz))
    return out
def hops(it): return it[0]+it[1]+abs(it[2])
def arrival(order,it):
    diff={"x":it[0]!=0,"y":it[1]!=0,"z":it[2]!=0}
    last=None
    for k,dim in enumerate(order):
        if diff[dim]: last=k
    return last

def neighbours(s,d,z,y,c,zn):
    return [(None,(1-s,d)),(None,(s,(z*2+1-y)*2+c)),(None,(s,(z*2+y)*2+1-c)),(z>0,(s,d-4)),(z<zn-1,(s,d+4))]

def ag_kernel(parts,zn,x_ref,w_ref,ssem,rsem,cs,cr,lsem):
    s,d,z,y,c=coords()
    bar=pltpu.get_barrier_semaphore()
    for cond,dev in neighbours(s,d,z,y,c,zn):
        def sig(dev=dev): pl.semaphore_signal(bar,inc=1,device_id=dev,device_id_type=MESH)
        sig() if cond is None else pl.when(cond)(sig)
    inner=jnp.logical_and(z>0,z<zn-1)
    pl.when(inner)(lambda: pl.semaphore_wait(bar,5))
    pl.when(jnp.logical_not(inner))(lambda: pl.semaphore_wait(bar,4))
    lc=pltpu.make_async_copy(x_ref,w_ref.at[s,d],lsem)
    lc.start()
    KIND={"x":0,"y":1,"l":2,"r":3}
    def where(it):
        s2=1-s if it[0] else s
        y2=1-y if it[1] else y
        z2=z+it[2]
        return s2,z2,y2
    def dsc(p,it,kind):
        r0,rn,order=parts[p]
        s2,z2,y2=where(it)
        idx=s2*(2*zn)+z2*2+y2
        own=it==(0,0,0)
        src=x_ref.at[pl.ds(r0,rn)] if own else w_ref.at[s2,(z2*2+y2)*2+c,pl.ds(r0,rn)]
        dst=w_ref.at[s2,(z2*2+y2)*2+c,pl.ds(r0,rn)]
        if kind=="core":
            dev=(s,(z*2+y)*2+1-c)
            return pltpu.make_async_remote_copy(src,dst,cs.at[p,idx],cr.at[p,idx],device_id=dev,device_id_type=MESH)
        dev={"x":(1-s,d),"y":(s,(z*2+1-y)*2+c),"l":(s,d-4),"r":(s,d+4)}[kind]
        return pltpu.make_async_remote_copy(src,dst,ssem.at[KIND[kind],p,idx],rsem.at[p,idx],device_id=dev,device_id_type=MESH)
    def cdsc(p,it):
        r0,rn,order=parts[p]
        s2,z2,y2=where(it)
        idx=s2*(2*zn)+z2*2+y2
        dst=w_ref.at[s2,(z2*2+y2)*2+1-c,pl.ds(r0,rn)]
        return pltpu.make_async_remote_copy(dst,dst,cs.at[p,idx],cr.at[p,idx],device_id=(s,(z*2+y)*2+1-c),device_id_type=MESH)
    def conds(it,kind):
        cs_=[]
        if it[2]<0: cs_.append(z+it[2]>=0)
        if it[2]>0: cs_.append(z+it[2]<=zn-1)
        if kind=="l": cs_.append(z>0)
        if kind=="r": cs_.append(z<zn-1)
        return cs_
    def guarded(cl,fn):
        if not cl: fn(); return
        e=cl[0]
        for q in cl[1:]: e=jnp.logical_and(e,q)
        pl.when(e)(fn)
    def sends(p,it):
        order=parts[p][2]
        a=arrival(order,it)
        ks=[]
        if a is not None and order[a]=="z": ks.append("l" if it[2]>0 else "r")
        for dim in order[(a+1) if a is not None else 0:]:
            ks += ["r","l"] if dim=="z" else [dim]
        ks.append("core")
        return ks
    evs=[]
    for p in range(len(parts)):
        for it in items(): evs.append((hops(it),p,it))
    evs.sort(key=lambda e:e[0])
    todo=[]
    for h,p,it in evs:
        if abs(it[2])>zn-1: continue
        def ev(p=p,it=it):
            if it!=(0,0,0): dsc(p,it,"x").wait_recv()
            for k in sends(p,it):
                guarded([q for q in conds((0,0,0),k)], lambda k=k: dsc(p,it,k).start())
        guarded(conds(it,None),ev)
        todo.append((p,it))
    for p,it in todo:
        def fin(p=p,it=it):
            cdsc(p,it).wait_recv()
            for k in sends(p,it):
                guarded(conds((0,0,0),k), lambda k=k: dsc(p,it,k).wait_send())
        guarded(conds(it,None),fin)
    lc.wait()

def ag(x,parts,zn,cid=0):
    n=len(parts)
    return pl.pallas_call(functools.partial(ag_kernel,parts,zn),
        out_shape=jax.ShapeDtypeStruct((2,4*zn,480,1280),jnp.bfloat16),
        in_specs=[pl.BlockSpec(memory_space=pl.ANY)],out_specs=pl.BlockSpec(memory_space=pl.ANY),
        scratch_shapes=[pltpu.SemaphoreType.DMA((4,n,4*zn)),pltpu.SemaphoreType.DMA((n,4*zn)),
          pltpu.SemaphoreType.DMA((n,4*zn)),pltpu.SemaphoreType.DMA((n,4*zn)),pltpu.SemaphoreType.DMA],
        compiler_params=pltpu.CompilerParams(collective_id=cid,has_side_effects=True))(x)


def rs_kernel(parts,zn,g_ref,o_ref,land,buf,obuf,*rest):
    nP=len(parts)
    lks=rest[:nP]
    ssem,rsem,cs,cr,lsem,osem=rest[nP:]
    s,d,z,y,c=coords()
    bar=pltpu.get_barrier_semaphore()
    for cond,dev in neighbours(s,d,z,y,c,zn):
        def sig(dev=dev): pl.semaphore_signal(bar,inc=1,device_id=dev,device_id_type=MESH)
        sig() if cond is None else pl.when(cond)(sig)
    inner=jnp.logical_and(z>0,z<zn-1)
    pl.when(inner)(lambda: pl.semaphore_wait(bar,5))
    pl.when(jnp.logical_not(inner))(lambda: pl.semaphore_wait(bar,4))
    sib=(s,(z*2+y)*2+1-c)
    def where(it):
        s2=1-s if it[0] else s
        y2=1-y if it[1] else y
        return s2,z+it[2],y2
    def conds(it):
        cl=[]
        if it[2]<0: cl.append(z+it[2]>=0)
        if it[2]>0: cl.append(z+it[2]<=zn-1)
        return cl
    def guarded(cl,fn):
        if not cl: fn(); return
        e=cl[0]
        for q in cl[1:]: e=jnp.logical_and(e,q)
        pl.when(e)(fn)
    def slot_base(order):
        sizes={"x":2,"y":2,"z":zn}
        base={};cur=0
        for k,dim in enumerate(order):
            n=1
            for q in order[k+1:]: n*=sizes[q]
            if dim=="z": n*=2*zn
            base[dim]=cur; cur+=n
        return base,cur
    def slot(p,dim,side,dest):
        order=parts[p][2][::-1]
        base,_=slot_base(order)
        k=order.index(dim)
        v={"x":dest[0],"z":dest[1],"y":dest[2]}
        idx=0
        for q in order[k+1:]:
            idx=idx*(zn if q=="z" else 2)+v[q]
        if dim=="z": idx=(idx*zn+dest[1])*2+side
        return base[dim]+idx
    evs=[]
    for p in range(nP):
        for it in items():
            if abs(it[2])<=zn-1: evs.append((-hops(it),p,it))
    evs.sort(key=lambda e:e[0])
    seq=[(p,it) for _,p,it in evs]
    def core_dsc(p,it,mine):
        r0,rn,_=parts[p]
        s2,z2,y2=where(it)
        idx=(s2*zn+z2)*2+y2
        cc=c if mine else 1-c
        return pltpu.make_async_remote_copy(g_ref.at[s2,(z2*2+y2)*2+cc,pl.ds(r0,rn)],land.at[idx,pl.ds(r0,rn)],cs.at[p,idx],cr.at[p,idx],device_id=sib,device_id_type=MESH)
    for p,it in seq:
        guarded(conds(it),lambda p=p,it=it: core_dsc(p,it,False).start())
    def load(i):
        p,it=seq[i]
        r0,rn,_=parts[p]
        s2,z2,y2=where(it)
        return pltpu.make_async_copy(g_ref.at[s2,(z2*2+y2)*2+c,pl.ds(r0,rn)],buf.at[i%NB,pl.ds(0,rn)],lsem.at[i%NB])
    NB=buf.shape[0]
    for i in range(min(NB-1,len(seq))):
        guarded(conds(seq[i][1]),lambda i=i: load(i).start())
    def contribs(p,it):
        order=parts[p][2][::-1]
        diff={"x":it[0],"y":it[1],"z":it[2]}
        out=[];nxt=None
        for dim in order:
            if dim=="z":
                if it[2]==0: out+=[("z",0,z>0),("z",1,z<zn-1)]
                elif it[2]>0: out.append(("z",0,z>0))
                else: out.append(("z",1,z<zn-1))
                if it[2]!=0: nxt="r" if it[2]>0 else "l"; break
            else:
                if diff[dim]: nxt=dim; break
                out.append((dim,0,None))
        return out,nxt
    semoff=[0]
    for p in range(nP): semoff.append(semoff[-1]+slot_base(parts[p][2][::-1])[1])
    def out_dsc(p,it,nxt):
        r0,rn,_=parts[p]
        dest=where(it)
        s2,z2,y2=dest
        idx=(s2*zn+z2)*2+y2
        dim="z" if nxt in "lr" else nxt
        side=1 if nxt=="l" else 0
        sl=slot(p,dim,side,dest)
        dev={"x":(1-s,d),"y":(s,(z*2+1-y)*2+c),"l":(s,d-4),"r":(s,d+4)}[nxt]
        return pltpu.make_async_remote_copy(land.at[idx,pl.ds(r0,rn)],lks[p].at[sl],ssem.at[p,idx],rsem.at[semoff[p]+sl],device_id=dev,device_id_type=MESH)
    for i,(p,it) in enumerate(seq):
        r0,rn,_=parts[p]
        if i+NB-1<len(seq):
            guarded(conds(seq[i+NB-1][1]),lambda i=i: load(i+NB-1).start())
        def ev(i=i,p=p,it=it,r0=r0,rn=rn):
            dest=where(it)
            s2,z2,y2=dest
            idx=(s2*zn+z2)*2+y2
            con,nxt=contribs(p,it)
            lk=lks[p]
            load(i).wait()
            core_dsc(p,it,True).wait_recv()
            plain=[x for x in con if x[2] is None]
            cond=[x for x in con if x[2] is not None]
            def rdsc(dim,side):
                sl=slot(p,dim,side,dest)
                return pltpu.make_async_remote_copy(lk.at[sl],lk.at[sl],ssem.at[p,idx],rsem.at[semoff[p]+sl],device_id=sib,device_id_type=MESH),sl
            for dim,side,_ in plain: rdsc(dim,side)[0].wait_recv()
            for dim,side,cnd in cond:
                pl.when(cnd)(lambda dim=dim,side=side: rdsc(dim,side)[0].wait_recv())
            if not cond: variants=[(None,plain)]
            elif len(cond)==1:
                variants=[(cond[0][2],plain+cond),(jnp.logical_not(cond[0][2]),plain)]
            else:
                a,b=cond
                variants=[(jnp.logical_and(a[2],b[2]),plain+cond),(jnp.logical_and(a[2],jnp.logical_not(b[2])),plain+[a]),
                          (jnp.logical_and(jnp.logical_not(a[2]),b[2]),plain+[b])]
            def total(lst):
                slots=[slot(p,dim,side,dest) for dim,side,_ in lst]
                CH=16
                def body(k,_):
                    ro=pl.multiple_of(k*CH,CH)
                    acc=buf[i%NB,pl.ds(ro,CH),:].astype(jnp.float32)+land[idx,pl.ds(r0+ro,CH),:].astype(jnp.float32)
                    for sl in slots: acc=acc+lk[sl,pl.ds(ro,CH),:].astype(jnp.float32)
                    if nxt is None: obuf[pl.ds(r0+ro,CH),:]=acc
                    else: land[idx,pl.ds(r0+ro,CH),:]=acc.astype(jnp.bfloat16)
                    return 0
                lax.fori_loop(0,rn//CH,body,0)
            for cnd,lst in variants:
                if cnd is None: total(lst)
                else: pl.when(cnd)(lambda lst=lst: total(lst))
            if nxt is not None: out_dsc(p,it,nxt).start()
            else: pltpu.make_async_copy(obuf.at[pl.ds(r0,rn)],o_ref.at[pl.ds(r0,rn)],osem.at[p]).start()
        guarded(conds(it),ev)
    for p,it in seq:
        def fin(p=p,it=it):
            core_dsc(p,it,False).wait_send()
            nxt=contribs(p,it)[1]
            if nxt is not None: out_dsc(p,it,nxt).wait_send()
        guarded(conds(it),fin)
    for p,(r0,rn,_) in enumerate(parts):
        pltpu.make_async_copy(obuf.at[pl.ds(r0,rn)],o_ref.at[pl.ds(r0,rn)],osem.at[p]).wait()

def slot_count(order,zn):
    sizes={"x":2,"y":2,"z":zn};cur=0
    for k,dim in enumerate(order):
        n=1
        for q in order[k+1:]: n*=sizes[q]
        if dim=="z": n*=2*zn
        cur+=n
    return cur
def rs(g,parts,zn,cid=1,nb=4):
    n=len(parts)
    cnt=[slot_count(p[2][::-1],zn) for p in parts]
    mx=max(p[1] for p in parts)
    return pl.pallas_call(functools.partial(rs_kernel,parts,zn),
        out_shape=jax.ShapeDtypeStruct((480,1280),jnp.float32),
        in_specs=[pl.BlockSpec(memory_space=pl.ANY)],out_specs=pl.BlockSpec(memory_space=pl.ANY),
        scratch_shapes=[pltpu.VMEM((4*zn,480,1280),jnp.bfloat16),pltpu.VMEM((nb,mx,1280),jnp.bfloat16),pltpu.VMEM((480,1280),jnp.float32)]
          +[pltpu.VMEM((cnt[p],parts[p][1],1280),jnp.bfloat16) for p in range(n)]
          +[pltpu.SemaphoreType.DMA((n,4*zn)),pltpu.SemaphoreType.DMA((sum(cnt),)),
          pltpu.SemaphoreType.DMA((n,4*zn)),pltpu.SemaphoreType.DMA((n,4*zn)),pltpu.SemaphoreType.DMA((nb,)),pltpu.SemaphoreType.DMA((n,))],
        compiler_params=pltpu.CompilerParams(collective_id=cid,has_side_effects=True,vmem_limit_bytes=62*2**20))(g)


def normed(value, gain):
    return value * lax.rsqrt(jnp.mean(value * value, axis=-1, keepdims=True) + EPS) * gain


def mul_plain(left, right):
    return jnp.dot(left, right, preferred_element_type=jnp.float32)


def mul_first_t(left, right):
    return lax.dot_general(
        left, right, (((0,), (0,)), ((), ())), preferred_element_type=jnp.float32
    )


def mul_second_t(left, right):
    return lax.dot_general(
        left, right, (((1,), (1,)), ((), ())), preferred_element_type=jnp.float32
    )


def forward_parts(inputs, segment, weights):
    w_query, w_key, w_value, w_mix, w_inner, w_outer, gain_one, gain_two, bias_inner, bias_outer = (
        weights
    )
    row_count, model_width = inputs.shape
    depth = model_width // HEADS
    scale = depth ** (-0.5)
    first = normed(inputs, gain_one).astype(jnp.bfloat16)
    query = mul_plain(first, w_query).astype(jnp.bfloat16)
    keys = mul_plain(first, w_key).astype(jnp.bfloat16)
    values = mul_plain(first, w_value).astype(jnp.bfloat16)
    query_h = query.reshape(row_count, HEADS, depth)
    keys_h = keys.reshape(row_count, HEADS, depth)
    values_h = values.reshape(row_count, HEADS, depth)
    scores = jnp.einsum("qhd,khd->hqk", query_h, keys_h, preferred_element_type=jnp.float32) * scale
    positions = jnp.arange(row_count, dtype=jnp.int32)
    allowed = (segment[:, None] == segment[None, :]) & (positions[None, :] <= positions[:, None])
    scores = jnp.where(allowed[None], scores, NEG)
    top_score = jnp.max(scores, axis=-1, keepdims=True)
    expd = jnp.exp(scores - top_score)
    soft = expd / jnp.sum(expd, axis=-1, keepdims=True)
    probs = soft.astype(jnp.bfloat16)
    attended = jnp.einsum("hqk,khd->qhd", probs, values_h, preferred_element_type=jnp.float32)
    attended = attended.reshape(row_count, model_width).astype(jnp.bfloat16)
    middle = inputs + mul_plain(attended, w_mix)
    second = normed(middle, gain_two).astype(jnp.bfloat16)
    inner = mul_plain(second, w_inner) + bias_inner
    active = jax.nn.gelu(inner, approximate=True).astype(jnp.bfloat16)
    output = middle + (mul_plain(active, w_outer) + bias_outer)
    saved = (first, query_h, keys_h, values_h, soft, probs, attended, middle, second, inner, active)
    return (output, saved)


def layer_backward(inputs, saved, weights, cotangent):
    w_query, w_key, w_value, w_mix, w_inner, w_outer, gain_one, gain_two, bias_inner, bias_outer = (
        weights
    )
    row_count, model_width = inputs.shape
    depth = model_width // HEADS
    scale = depth ** (-0.5)
    first, query_h, keys_h, values_h, soft, probs, attended, middle, second, inner, active = saved
    grad_outer = cotangent.astype(jnp.bfloat16)
    d_bias_outer = jnp.sum(grad_outer.astype(jnp.float32), axis=0)
    d_w_outer = mul_first_t(active, grad_outer)
    d_active = mul_second_t(grad_outer, w_outer)
    gelu_value, gelu_back = jax.vjp(lambda pre_act: jax.nn.gelu(pre_act, approximate=True), inner)
    d_inner = gelu_back(d_active)[0].astype(jnp.bfloat16)
    d_bias_inner = jnp.sum(d_inner.astype(jnp.float32), axis=0)
    d_w_inner = mul_first_t(second, d_inner)
    d_second = mul_second_t(d_inner, w_inner)
    norm_value, norm_back = jax.vjp(normed, middle, gain_two)
    d_middle_norm, d_gain_two = norm_back(d_second)
    d_middle = cotangent + d_middle_norm
    d_branch = d_middle.astype(jnp.bfloat16)
    d_w_mix = mul_first_t(attended, d_branch)
    d_attended = mul_second_t(d_branch, w_mix).astype(jnp.bfloat16).reshape(row_count, HEADS, depth)
    d_probs = jnp.einsum("qhd,khd->hqk", d_attended, values_h, preferred_element_type=jnp.float32)
    d_values = jnp.einsum("hqk,qhd->khd", probs, d_attended, preferred_element_type=jnp.float32)
    d_values = d_values.reshape(row_count, model_width).astype(jnp.bfloat16)
    d_scores = (soft * (d_probs - jnp.sum(d_probs * soft, axis=-1, keepdims=True))).astype(
        jnp.bfloat16
    )
    d_query = (
        jnp.einsum("hqk,khd->qhd", d_scores, keys_h, preferred_element_type=jnp.float32) * scale
    )
    d_query = d_query.reshape(row_count, model_width).astype(jnp.bfloat16)
    d_keys = (
        jnp.einsum("hqk,qhd->khd", d_scores, query_h, preferred_element_type=jnp.float32) * scale
    )
    d_keys = d_keys.reshape(row_count, model_width).astype(jnp.bfloat16)
    d_w_query = mul_first_t(first, d_query)
    d_w_key = mul_first_t(first, d_keys)
    d_w_value = mul_first_t(first, d_values)
    d_first = (
        mul_second_t(d_query, w_query)
        + mul_second_t(d_keys, w_key)
        + mul_second_t(d_values, w_value)
    )
    first_value, first_back = jax.vjp(normed, inputs, gain_one)
    d_inputs_norm, d_gain_one = first_back(d_first)
    d_inputs = d_middle + d_inputs_norm
    d_mats = jnp.stack([w.astype(jnp.bfloat16) for w in (d_w_query, d_w_key, d_w_value, d_w_mix, d_w_inner, d_w_outer)])
    d_gains = jnp.stack([d_gain_one, d_gain_two])
    d_biases = jnp.stack([d_bias_inner, d_bias_outer])
    return (d_inputs, d_mats, d_gains, d_biases)


def one_hot(rank):
    rows = rank.shape[0]
    return (rank[None, :] == jnp.arange(rows, dtype=jnp.int32)[:, None]).astype(jnp.bfloat16)


def rank_of(key):
    return jnp.sum((key[None, :] < key[:, None]).astype(jnp.int32), axis=1)


def gather_weights(own, peers):
    if peers == 16:
        return ag(own, PARTS, peers // 4)
    rows, width = own.shape
    return lax.all_gather(own, BOTH, axis=0, tiled=True).reshape(2, peers, rows, width)


def scatter_grads(terms, peers):
    if peers == 16:
        return rs(terms, PARTS, peers // 4)
    sections, _, rows, width = terms.shape
    terms = terms.reshape(sections * peers * rows, width)
    return lax.psum_scatter(terms, BOTH, scatter_dimension=0, tiled=True).astype(jnp.float32)


def local(entering, deal, seq_lens, mats, gains, biases):
    section = lax.axis_index("section")
    own_dp = lax.axis_index("dp")
    peers = lax.axis_size("dp")
    arrival = entering[0]
    batches, rows, width = arrival.shape
    per_peer = rows // peers
    all_deal = lax.all_gather(deal, "dp", axis=1, tiled=True)
    small = jnp.concatenate([gains[0], biases[0]]).astype(jnp.bfloat16).astype(jnp.float32)
    small = lax.all_gather(small, BOTH, axis=0).reshape(2, peers, 2, -1)
    small = jnp.swapaxes(small, 1, 2).reshape(2, 2, 2, width)
    all_mats = gather_weights(mats[0].astype(jnp.bfloat16), peers)
    all_mats = all_mats.reshape(2, 6, width, width)
    own_rows = own_dp * rows + jnp.arange(rows, dtype=jnp.int32)
    block_ids = jnp.arange(all_deal.shape[1], dtype=jnp.int32) // rows
    sends = []
    returns = []
    for batch in range(batches):
        hit = all_deal[batch][None, :] == own_rows[:, None]
        target = jnp.sum(jnp.where(hit, block_ids[None, :], 0), axis=1)
        key = target * rows + jnp.arange(rows, dtype=jnp.int32)
        pick = one_hot(rank_of(key))
        returns.append(pick)
        sends.append(mul_plain(pick, arrival[batch]).astype(jnp.bfloat16))
    outgoing = jnp.stack(sends).reshape(2 * peers, per_peer, width)
    arrived = lax.all_to_all(outgoing, BOTH, split_axis=0, concat_axis=0, tiled=True)
    arrived = arrived.reshape(2, rows, width)
    own_deal = jnp.where(section == 0, deal[0], deal[1])
    place = one_hot(rank_of(own_deal))
    tokens = mul_first_t(place, arrived[0])
    cotangent = mul_first_t(place, arrived[1])
    lens = jnp.where(section == 0, seq_lens[0, 0], seq_lens[1, 0])
    ends = jnp.cumsum(lens)
    positions = jnp.arange(rows, dtype=jnp.int32)
    segment = jnp.sum((positions[:, None] >= ends[None, :]).astype(jnp.int32), axis=1)
    state = tokens
    kept = []
    weights = []
    for layer in range(2):
        if layer:
            state = state.astype(jnp.bfloat16).astype(jnp.float32)
        mats_l = tuple(all_mats[layer, index] for index in range(6))
        weights.append(mats_l + (small[layer, 0, 0], small[layer, 0, 1], small[layer, 1, 0], small[layer, 1, 1]))
        out, saved = forward_parts(state, segment, weights[layer])
        kept.append((state, saved))
        state = out
    final = state.astype(jnp.bfloat16)
    grads = [None, None]
    down = cotangent
    for layer in (1, 0):
        down, d_mats, d_gains, d_biases = layer_backward(kept[layer][0], kept[layer][1], weights[layer], down)
        down = down.astype(jnp.bfloat16).astype(jnp.float32)
        grads[layer] = (d_mats, d_gains, d_biases)
    terms = jnp.stack([grads[0][0], grads[1][0]]).reshape(2, peers, -1, width)
    shard_mats = scatter_grads(terms, peers)[None]
    small_grads = jnp.stack([jnp.stack([grads[layer][1], grads[layer][2]]) for layer in range(2)])
    small_grads = lax.psum(small_grads.reshape(2, 2, 2 * width), BOTH)
    per = 2 * width // peers
    mine = lax.dynamic_slice(small_grads, (section, 0, own_dp * per), (1, 2, per))
    back = jnp.stack([mul_plain(place, down.astype(jnp.bfloat16)), mul_plain(place, final)]).astype(jnp.bfloat16)
    back = back.reshape(2 * peers, per_peer, width)
    returned = lax.all_to_all(back, BOTH, split_axis=0, concat_axis=0, tiled=True).reshape(2, rows, width)
    results = jnp.stack([mul_first_t(returns[batch], returned[batch]) for batch in range(batches)])
    return (results.astype(jnp.bfloat16)[None], shard_mats, mine[:, 0], mine[:, 1])


def solution(mesh):
    in_specs = (
        P("section", None, "dp", None),
        P(None, "dp"),
        P(None, "dp", None),
        P("section", "dp", None),
        P("section", "dp"),
        P("section", "dp"),
    )
    out_specs = (
        P("section", None, "dp", None),
        P("section", "dp", None),
        P("section", "dp"),
        P("section", "dp"),
    )
    return jax.shard_map(local, mesh=mesh, in_specs=in_specs, out_specs=out_specs, check_vma=False)
```

```python
import functools

import jax
import jax.numpy as jnp
from jax import lax
from jax.experimental import pallas as pl
from jax.experimental.pallas import tpu as pltpu
from jax.sharding import PartitionSpec as P

HEADS = 16
EPS = 1e-06
NEG = -1000000000.0
BOTH = ("section", "dp")
MESH = pl.DeviceIdType.MESH
PARTS = ((0, 112, "zxy"), (112, 112, "zyx"), (224, 128, "xzy"), (352, 128, "yzx"))


def greet(total, me, peers):
    barrier = pltpu.get_barrier_semaphore()

    def one(step, carry):
        other = lax.rem(me + step, total)
        pl.semaphore_signal(
            barrier, inc=1, device_id=(other // peers, lax.rem(other, peers)), device_id_type=MESH
        )
        return carry

    lax.fori_loop(1, total, one, 0)
    pl.semaphore_wait(barrier, total - 1)


def share_kernel(peers, own_ref, all_ref, local_sem, send_sem, recv_sem):
    total = 2 * peers
    me = lax.axis_index("section") * peers + lax.axis_index("dp")
    greet(total, me, peers)
    keep = pltpu.make_async_copy(own_ref, all_ref.at[me], local_sem)
    keep.start()

    def one(step, carry):
        other = lax.rem(me + step, total)
        pltpu.make_async_remote_copy(
            own_ref, all_ref.at[me], send_sem, recv_sem,
            device_id=(other // peers, lax.rem(other, peers)), device_id_type=MESH,
        ).start()
        return carry

    lax.fori_loop(1, total, one, 0)
    rest = all_ref.at[pl.ds(0, total - 1)]
    bulk = pltpu.make_async_remote_copy(
        rest, rest, send_sem, recv_sem, device_id=(0, 0), device_id_type=MESH
    )
    bulk.wait_recv()
    bulk.wait_send()
    keep.wait()


def share(own, peers):
    vm = pl.BlockSpec(memory_space=pltpu.VMEM)
    return pl.pallas_call(
        functools.partial(share_kernel, peers),
        out_shape=jax.ShapeDtypeStruct((2 * peers,) + own.shape, own.dtype),
        in_specs=[vm],
        out_specs=vm,
        scratch_shapes=[pltpu.SemaphoreType.DMA, pltpu.SemaphoreType.DMA, pltpu.SemaphoreType.DMA],
        compiler_params=pltpu.CompilerParams(collective_id=2, has_side_effects=True),
        name="share_small",
    )(own)


def coords():
    s=lax.axis_index("section"); d=lax.axis_index("dp")
    return s,d,d//4,(d//2)%2,d%2

def items():
    out=[]
    for bx in (0,1):
        for by in (0,1):
            for dz in (0,-1,1,-2,2,-3,3):
                out.append((bx,by,dz))
    return out
def hops(it): return it[0]+it[1]+abs(it[2])
def arrival(order,it):
    diff={"x":it[0]!=0,"y":it[1]!=0,"z":it[2]!=0}
    last=None
    for k,dim in enumerate(order):
        if diff[dim]: last=k
    return last

def neighbours(s,d,z,y,c,zn):
    return [(None,(1-s,d)),(None,(s,(z*2+1-y)*2+c)),(None,(s,(z*2+y)*2+1-c)),(z>0,(s,d-4)),(z<zn-1,(s,d+4))]

def ag_kernel(parts,zn,x_ref,w_ref,ssem,rsem,cs,cr,lsem):
    s,d,z,y,c=coords()
    bar=pltpu.get_barrier_semaphore()
    for cond,dev in neighbours(s,d,z,y,c,zn):
        def sig(dev=dev): pl.semaphore_signal(bar,inc=1,device_id=dev,device_id_type=MESH)
        sig() if cond is None else pl.when(cond)(sig)
    inner=jnp.logical_and(z>0,z<zn-1)
    pl.when(inner)(lambda: pl.semaphore_wait(bar,5))
    pl.when(jnp.logical_not(inner))(lambda: pl.semaphore_wait(bar,4))
    lc=pltpu.make_async_copy(x_ref,w_ref.at[s,d],lsem)
    lc.start()
    KIND={"x":0,"y":1,"l":2,"r":3}
    def where(it):
        s2=1-s if it[0] else s
        y2=1-y if it[1] else y
        z2=z+it[2]
        return s2,z2,y2
    def dsc(p,it,kind):
        r0,rn,order=parts[p]
        s2,z2,y2=where(it)
        idx=s2*(2*zn)+z2*2+y2
        own=it==(0,0,0)
        src=x_ref.at[pl.ds(r0,rn)] if own else w_ref.at[s2,(z2*2+y2)*2+c,pl.ds(r0,rn)]
        dst=w_ref.at[s2,(z2*2+y2)*2+c,pl.ds(r0,rn)]
        if kind=="core":
            dev=(s,(z*2+y)*2+1-c)
            return pltpu.make_async_remote_copy(src,dst,cs.at[p,idx],cr.at[p,idx],device_id=dev,device_id_type=MESH)
        dev={"x":(1-s,d),"y":(s,(z*2+1-y)*2+c),"l":(s,d-4),"r":(s,d+4)}[kind]
        return pltpu.make_async_remote_copy(src,dst,ssem.at[KIND[kind],p,idx],rsem.at[p,idx],device_id=dev,device_id_type=MESH)
    def cdsc(p,it):
        r0,rn,order=parts[p]
        s2,z2,y2=where(it)
        idx=s2*(2*zn)+z2*2+y2
        dst=w_ref.at[s2,(z2*2+y2)*2+1-c,pl.ds(r0,rn)]
        return pltpu.make_async_remote_copy(dst,dst,cs.at[p,idx],cr.at[p,idx],device_id=(s,(z*2+y)*2+1-c),device_id_type=MESH)
    def conds(it,kind):
        cs_=[]
        if it[2]<0: cs_.append(z+it[2]>=0)
        if it[2]>0: cs_.append(z+it[2]<=zn-1)
        if kind=="l": cs_.append(z>0)
        if kind=="r": cs_.append(z<zn-1)
        return cs_
    def guarded(cl,fn):
        if not cl: fn(); return
        e=cl[0]
        for q in cl[1:]: e=jnp.logical_and(e,q)
        pl.when(e)(fn)
    def sends(p,it):
        order=parts[p][2]
        a=arrival(order,it)
        ks=[]
        if a is not None and order[a]=="z": ks.append("l" if it[2]>0 else "r")
        for dim in order[(a+1) if a is not None else 0:]:
            ks += ["r","l"] if dim=="z" else [dim]
        ks.append("core")
        return ks
    evs=[]
    for p in range(len(parts)):
        for it in items(): evs.append((hops(it),p,it))
    evs.sort(key=lambda e:e[0])
    todo=[]
    for h,p,it in evs:
        if abs(it[2])>zn-1: continue
        def ev(p=p,it=it):
            if it!=(0,0,0): dsc(p,it,"x").wait_recv()
            for k in sends(p,it):
                guarded([q for q in conds((0,0,0),k)], lambda k=k: dsc(p,it,k).start())
        guarded(conds(it,None),ev)
        todo.append((p,it))
    for p,it in todo:
        def fin(p=p,it=it):
            cdsc(p,it).wait_recv()
            for k in sends(p,it):
                guarded(conds((0,0,0),k), lambda k=k: dsc(p,it,k).wait_send())
        guarded(conds(it,None),fin)
    lc.wait()

def ag(x,parts,zn,cid=0):
    n=len(parts)
    return pl.pallas_call(functools.partial(ag_kernel,parts,zn),
        out_shape=jax.ShapeDtypeStruct((2,4*zn,480,1280),jnp.bfloat16),
        in_specs=[pl.BlockSpec(memory_space=pl.ANY)],out_specs=pl.BlockSpec(memory_space=pl.ANY),
        scratch_shapes=[pltpu.SemaphoreType.DMA((4,n,4*zn)),pltpu.SemaphoreType.DMA((n,4*zn)),
          pltpu.SemaphoreType.DMA((n,4*zn)),pltpu.SemaphoreType.DMA((n,4*zn)),pltpu.SemaphoreType.DMA],
        compiler_params=pltpu.CompilerParams(collective_id=cid,has_side_effects=True))(x)


def rs_kernel(parts,zn,g_ref,v_ref,o_ref,vo_ref,land,buf,obuf,vland,*rest):
    nP=len(parts)
    lks=rest[:nP]
    ssem,rsem,cs,cr,lsem,osem,vsend,vrecv=rest[nP:]
    s,d,z,y,c=coords()
    peers=4*zn
    total_dev=2*peers
    me=s*peers+d
    greet(total_dev,me,peers)
    vland[me]=v_ref[me]
    def small(step,carry):
        other=lax.rem(me+step,total_dev)
        pltpu.make_async_remote_copy(v_ref.at[other],vland.at[me],vsend,vrecv,device_id=(other//peers,lax.rem(other,peers)),device_id_type=MESH).start()
        return carry
    lax.fori_loop(1,total_dev,small,0)
    sib=(s,(z*2+y)*2+1-c)
    def where(it):
        s2=1-s if it[0] else s
        y2=1-y if it[1] else y
        return s2,z+it[2],y2
    def conds(it):
        cl=[]
        if it[2]<0: cl.append(z+it[2]>=0)
        if it[2]>0: cl.append(z+it[2]<=zn-1)
        return cl
    def guarded(cl,fn):
        if not cl: fn(); return
        e=cl[0]
        for q in cl[1:]: e=jnp.logical_and(e,q)
        pl.when(e)(fn)
    def slot_base(order):
        sizes={"x":2,"y":2,"z":zn}
        base={};cur=0
        for k,dim in enumerate(order):
            n=1
            for q in order[k+1:]: n*=sizes[q]
            if dim=="z": n*=2*zn
            base[dim]=cur; cur+=n
        return base,cur
    def slot(p,dim,side,dest):
        order=parts[p][2][::-1]
        base,_=slot_base(order)
        k=order.index(dim)
        v={"x":dest[0],"z":dest[1],"y":dest[2]}
        idx=0
        for q in order[k+1:]:
            idx=idx*(zn if q=="z" else 2)+v[q]
        if dim=="z": idx=(idx*zn+dest[1])*2+side
        return base[dim]+idx
    evs=[]
    for p in range(nP):
        for it in items():
            if abs(it[2])<=zn-1: evs.append((-hops(it),p,it))
    evs.sort(key=lambda e:e[0])
    seq=[(p,it) for _,p,it in evs]
    def core_dsc(p,it,mine):
        r0,rn,_=parts[p]
        s2,z2,y2=where(it)
        idx=(s2*zn+z2)*2+y2
        cc=c if mine else 1-c
        return pltpu.make_async_remote_copy(g_ref.at[s2,(z2*2+y2)*2+cc,pl.ds(r0,rn)],land.at[idx,pl.ds(r0,rn)],cs.at[p,idx],cr.at[p,idx],device_id=sib,device_id_type=MESH)
    for p,it in seq:
        guarded(conds(it),lambda p=p,it=it: core_dsc(p,it,False).start())
    def load(i):
        p,it=seq[i]
        r0,rn,_=parts[p]
        s2,z2,y2=where(it)
        return pltpu.make_async_copy(g_ref.at[s2,(z2*2+y2)*2+c,pl.ds(r0,rn)],buf.at[i%NB,pl.ds(0,rn)],lsem.at[i%NB])
    NB=buf.shape[0]
    for i in range(min(NB-1,len(seq))):
        guarded(conds(seq[i][1]),lambda i=i: load(i).start())
    def contribs(p,it):
        order=parts[p][2][::-1]
        diff={"x":it[0],"y":it[1],"z":it[2]}
        out=[];nxt=None
        for dim in order:
            if dim=="z":
                if it[2]==0: out+=[("z",0,z>0),("z",1,z<zn-1)]
                elif it[2]>0: out.append(("z",0,z>0))
                else: out.append(("z",1,z<zn-1))
                if it[2]!=0: nxt="r" if it[2]>0 else "l"; break
            else:
                if diff[dim]: nxt=dim; break
                out.append((dim,0,None))
        return out,nxt
    semoff=[0]
    for p in range(nP): semoff.append(semoff[-1]+slot_base(parts[p][2][::-1])[1])
    def out_dsc(p,it,nxt):
        r0,rn,_=parts[p]
        dest=where(it)
        s2,z2,y2=dest
        idx=(s2*zn+z2)*2+y2
        dim="z" if nxt in "lr" else nxt
        side=1 if nxt=="l" else 0
        sl=slot(p,dim,side,dest)
        dev={"x":(1-s,d),"y":(s,(z*2+1-y)*2+c),"l":(s,d-4),"r":(s,d+4)}[nxt]
        return pltpu.make_async_remote_copy(land.at[idx,pl.ds(r0,rn)],lks[p].at[sl],ssem.at[p,idx],rsem.at[semoff[p]+sl],device_id=dev,device_id_type=MESH)
    for i,(p,it) in enumerate(seq):
        r0,rn,_=parts[p]
        if i+NB-1<len(seq):
            guarded(conds(seq[i+NB-1][1]),lambda i=i: load(i+NB-1).start())
        def ev(i=i,p=p,it=it,r0=r0,rn=rn):
            dest=where(it)
            s2,z2,y2=dest
            idx=(s2*zn+z2)*2+y2
            con,nxt=contribs(p,it)
            lk=lks[p]
            load(i).wait()
            core_dsc(p,it,True).wait_recv()
            plain=[x for x in con if x[2] is None]
            cond=[x for x in con if x[2] is not None]
            def rdsc(dim,side):
                sl=slot(p,dim,side,dest)
                return pltpu.make_async_remote_copy(lk.at[sl],lk.at[sl],ssem.at[p,idx],rsem.at[semoff[p]+sl],device_id=sib,device_id_type=MESH),sl
            for dim,side,_ in plain: rdsc(dim,side)[0].wait_recv()
            for dim,side,cnd in cond:
                pl.when(cnd)(lambda dim=dim,side=side: rdsc(dim,side)[0].wait_recv())
            if not cond: variants=[(None,plain)]
            elif len(cond)==1:
                variants=[(cond[0][2],plain+cond),(jnp.logical_not(cond[0][2]),plain)]
            else:
                a,b=cond
                variants=[(jnp.logical_and(a[2],b[2]),plain+cond),(jnp.logical_and(a[2],jnp.logical_not(b[2])),plain+[a]),
                          (jnp.logical_and(jnp.logical_not(a[2]),b[2]),plain+[b])]
            def total(lst):
                slots=[slot(p,dim,side,dest) for dim,side,_ in lst]
                CH=16
                def body(k,_):
                    ro=pl.multiple_of(k*CH,CH)
                    acc=buf[i%NB,pl.ds(ro,CH),:].astype(jnp.float32)+land[idx,pl.ds(r0+ro,CH),:].astype(jnp.float32)
                    for sl in slots: acc=acc+lk[sl,pl.ds(ro,CH),:].astype(jnp.float32)
                    if nxt is None: obuf[pl.ds(r0+ro,CH),:]=acc
                    else: land[idx,pl.ds(r0+ro,CH),:]=acc.astype(jnp.bfloat16)
                    return 0
                lax.fori_loop(0,rn//CH,body,0)
            for cnd,lst in variants:
                if cnd is None: total(lst)
                else: pl.when(cnd)(lambda lst=lst: total(lst))
            if nxt is not None: out_dsc(p,it,nxt).start()
            else: pltpu.make_async_copy(obuf.at[pl.ds(r0,rn)],o_ref.at[pl.ds(r0,rn)],osem.at[p]).start()
        guarded(conds(it),ev)
    for p,it in seq:
        def fin(p=p,it=it):
            core_dsc(p,it,False).wait_send()
            nxt=contribs(p,it)[1]
            if nxt is not None: out_dsc(p,it,nxt).wait_send()
        guarded(conds(it),fin)
    for p,(r0,rn,_) in enumerate(parts):
        pltpu.make_async_copy(obuf.at[pl.ds(r0,rn)],o_ref.at[pl.ds(r0,rn)],osem.at[p]).wait()
    rest_of=vland.at[pl.ds(0,total_dev-1)]
    bulk=pltpu.make_async_remote_copy(rest_of,rest_of,vsend,vrecv,device_id=(0,0),device_id_type=MESH)
    bulk.wait_recv()
    bulk.wait_send()
    vo_ref[...]=jnp.sum(vland[...],axis=0)


def slot_count(order,zn):
    sizes={"x":2,"y":2,"z":zn};cur=0
    for k,dim in enumerate(order):
        n=1
        for q in order[k+1:]: n*=sizes[q]
        if dim=="z": n*=2*zn
        cur+=n
    return cur
def rs(g,v,parts,zn,cid=1,nb=4):
    n=len(parts)
    cnt=[slot_count(p[2][::-1],zn) for p in parts]
    mx=max(p[1] for p in parts)
    return pl.pallas_call(functools.partial(rs_kernel,parts,zn),
        out_shape=[jax.ShapeDtypeStruct((480,1280),jnp.float32),jax.ShapeDtypeStruct(v.shape[1:],jnp.float32)],
        in_specs=[pl.BlockSpec(memory_space=pl.ANY),pl.BlockSpec(memory_space=pltpu.VMEM)],
        out_specs=[pl.BlockSpec(memory_space=pl.ANY),pl.BlockSpec(memory_space=pltpu.VMEM)],
        scratch_shapes=[pltpu.VMEM((4*zn,480,1280),jnp.bfloat16),pltpu.VMEM((nb,mx,1280),jnp.bfloat16),pltpu.VMEM((480,1280),jnp.float32),pltpu.VMEM(v.shape,jnp.float32)]
          +[pltpu.VMEM((cnt[p],parts[p][1],1280),jnp.bfloat16) for p in range(n)]
          +[pltpu.SemaphoreType.DMA((n,4*zn)),pltpu.SemaphoreType.DMA((sum(cnt),)),
          pltpu.SemaphoreType.DMA((n,4*zn)),pltpu.SemaphoreType.DMA((n,4*zn)),pltpu.SemaphoreType.DMA((nb,)),pltpu.SemaphoreType.DMA((n,)),pltpu.SemaphoreType.DMA,pltpu.SemaphoreType.DMA],
        compiler_params=pltpu.CompilerParams(collective_id=cid,has_side_effects=True,vmem_limit_bytes=62*2**20))(g,v)


WIN = 256
QB = 128
GC = 0.7978845608028654
GA = 0.044715
VMEM_LIMIT = 62 * 2**20


def nn(left, right):
    return jnp.dot(left, right, preferred_element_type=jnp.float32)


def nt(left, right):
    return lax.dot_general(
        left, right, (((1,), (1,)), ((), ())), preferred_element_type=jnp.float32
    )


def tn(left, right):
    return lax.dot_general(
        left, right, (((0,), (0,)), ((), ())), preferred_element_type=jnp.float32
    )


def head_window(head, depth, width):
    start = jnp.minimum((head * depth) // 128, (width - WIN) // 128) * 128
    start = pl.multiple_of(start, 128)
    lane = lax.broadcasted_iota(jnp.int32, (1, WIN), 1) + (start - head * depth)
    return start, (lane >= 0) & (lane < depth)


def norm_rows(value, gain):
    return value * lax.rsqrt(jnp.mean(value * value, axis=-1, keepdims=True) + EPS) * gain


def norm_back(value, gain, down):
    inv = lax.rsqrt(jnp.mean(value * value, axis=-1, keepdims=True) + EPS)
    unit = value * inv
    scaled = down * gain
    lean = jnp.mean(scaled * unit, axis=-1, keepdims=True)
    return inv * (scaled - unit * lean), jnp.sum(down * unit, axis=0, keepdims=True)


def forward_kernel(
    layer, mats_ref, x_ref, vec_ref, segc_ref, segr_ref,
    y_ref, qkv_out, prob_out, att_out, mid_out, u_out,
    held, qkv, prob, att, mid, u, norm, mask, sems, out_sems,
):
    rows, width = x_ref.shape
    depth = width // HEADS
    scale = depth ** (-0.5)

    def weight(index):
        return pltpu.make_async_copy(
            mats_ref.at[layer, pl.ds(index * width, width)], held.at[index], sems.at[index]
        )

    keeps = [
        pltpu.make_async_copy(src, dst, out_sems.at[index])
        for index, (src, dst) in enumerate(
            ((qkv, qkv_out), (prob, prob_out), (att, att_out), (mid, mid_out), (u, u_out))
        )
    ]
    for index in range(6):
        weight(index).start()
    tiles = [slice(c, c + WIN) for c in range(0, width, WIN)]
    norm[...] = norm_rows(x_ref[...].astype(jnp.float32), vec_ref[0:1, :]).astype(jnp.bfloat16)
    qi = lax.broadcasted_iota(jnp.int32, (rows, rows), 0)
    ki = lax.broadcasted_iota(jnp.int32, (rows, rows), 1)
    mask[...] = jnp.where((segc_ref[...] == segr_ref[...]) & (ki <= qi), 1.0, 0.0)
    for index in range(3):
        weight(index).wait()
        for cols in tiles:
            qkv[index, :, cols] = nn(norm[...], held[index, :, cols]).astype(jnp.bfloat16)
    keeps[0].start()
    att[...] = jnp.zeros_like(att)

    def one_head(head, carry):
        start, lanes = head_window(head, depth, width)
        cols = pl.ds(start, WIN)
        for block in range(rows // QB):
            here = slice(block * QB, (block + 1) * QB)
            upto = slice(0, (block + 1) * QB)
            query = jnp.where(lanes, qkv[0, here, cols], 0)
            score = nt(query, qkv[1, upto, cols]) * scale
            score = jnp.where(mask[here, upto] > 0.5, score, NEG)
            expd = jnp.exp(score - jnp.max(score, axis=-1, keepdims=True))
            soft = (expd * (1.0 / jnp.sum(expd, axis=-1, keepdims=True))).astype(jnp.bfloat16)
            prob[head, here, upto] = soft
            mixed = nn(soft, qkv[2, upto, cols])
            att[here, cols] = jnp.where(lanes, mixed.astype(jnp.bfloat16), att[here, cols])
        return carry

    lax.fori_loop(0, HEADS, one_head, 0)
    keeps[1].start()
    keeps[2].start()
    weight(3).wait()
    for cols in tiles:
        mid[:, cols] = x_ref[:, cols].astype(jnp.float32) + nn(att[...], held[3, :, cols])
    keeps[3].start()
    norm[...] = norm_rows(mid[...], vec_ref[1:2, :]).astype(jnp.bfloat16)
    weight(4).wait()
    for cols in tiles:
        u[:, cols] = nn(norm[...], held[4, :, cols]) + vec_ref[2:3, cols]
    keeps[4].start()
    for cols in tiles:
        pre = u[:, cols]
        act = 0.5 * pre * (1.0 + jnp.tanh(GC * (pre + GA * (pre * pre * pre))))
        norm[:, cols] = act.astype(jnp.bfloat16)
    weight(5).wait()
    for cols in tiles:
        out = mid[:, cols] + (nn(norm[...], held[5, :, cols]) + vec_ref[3:4, cols])
        y_ref[:, cols] = out.astype(jnp.bfloat16)
    for keep in keeps:
        keep.wait()


def forward_layer(layer, mats, x, vec, segc, segr):
    rows, width = x.shape
    f32, b16 = jnp.float32, jnp.bfloat16
    vm = pl.BlockSpec(memory_space=pltpu.VMEM)
    hbm = pl.BlockSpec(memory_space=pl.ANY)
    kept = [
        ((3, rows, width), b16), ((HEADS, rows, rows), b16), ((rows, width), b16),
        ((rows, width), f32), ((rows, width), f32),
    ]
    return pl.pallas_call(
        functools.partial(forward_kernel, layer),
        out_shape=[jax.ShapeDtypeStruct((rows, width), b16)]
        + [jax.ShapeDtypeStruct(shape, dtype) for shape, dtype in kept],
        in_specs=[hbm, vm, vm, vm, vm],
        out_specs=[vm] + [hbm] * 5,
        scratch_shapes=[pltpu.VMEM((6, width, width), b16)]
        + [pltpu.VMEM(shape, dtype) for shape, dtype in kept]
        + [
            pltpu.VMEM((rows, width), b16),
            pltpu.VMEM((rows, rows), f32),
            pltpu.SemaphoreType.DMA((6,)),
            pltpu.SemaphoreType.DMA((5,)),
        ],
        compiler_params=pltpu.CompilerParams(vmem_limit_bytes=VMEM_LIMIT),
        name="layer_forward",
    )(mats, x, vec, segc, segr)


def backward_kernel(layer, aliased, *refs):
    mats_ref, x_ref, vec_ref, dy_ref, qkv_in, prob_in, att_in, mid_in, u_in = refs[:9]
    rest = refs[10:] if aliased else refs[9:]
    (
        grads_ref, dx_ref, dvec_ref,
        held, qkv, prob, att, mid, u, act, low, wide, dmid, dqkv, dscore, turned, stage,
        sems, in_sems, out_sems,
    ) = rest
    rows, width = x_ref.shape
    depth = width // HEADS
    scale = depth ** (-0.5)
    f32, b16 = jnp.float32, jnp.bfloat16
    tiles = [slice(c, c + WIN) for c in range(0, width, WIN)]

    def weight(index):
        return pltpu.make_async_copy(
            mats_ref.at[layer, pl.ds(index * width, width)], held.at[index], sems.at[index]
        )

    loads = [
        pltpu.make_async_copy(src, dst, in_sems.at[index])
        for index, (src, dst) in enumerate(
            ((qkv_in, qkv), (prob_in, prob), (att_in, att), (mid_in, mid), (u_in, u))
        )
    ]
    loads[4].start()
    weight(5).start()
    weight(4).start()
    loads[3].start()
    weight(3).start()
    loads[2].start()
    loads[0].start()
    loads[1].start()
    for index in range(3):
        weight(index).start()

    def put(index, slot):
        return pltpu.make_async_copy(
            stage.at[slot], grads_ref.at[layer, pl.ds(index * width, width)], out_sems.at[index]
        )

    slots = {5: 0, 4: 1, 3: 0, 2: 1, 1: 0, 0: 1}
    before = {3: 5, 2: 4, 1: 3, 0: 2}

    def weight_grad(index, left_t, right):
        slot = slots[index]
        if index in before:
            put(before[index], slot).wait()
        for cols in tiles:
            stage[slot, cols, :] = nn(left_t(cols), right).astype(b16)
        put(index, slot).start()

    dvec_ref[3:4, :] = jnp.sum(dy_ref[...].astype(f32), axis=0, keepdims=True)
    loads[4].wait()
    weight(5).wait()
    for cols in tiles:
        pre = u[:, cols]
        square = pre * pre
        bent = jnp.tanh(GC * (pre + GA * (square * pre)))
        half = 0.5 * (1.0 + bent)
        act[:, cols] = (pre * half).astype(b16)
        slope = half + (0.5 * GC) * pre * (1.0 - bent * bent) * (1.0 + (3.0 * GA) * square)
        down = nt(dy_ref[...], held[5, cols, :]) * slope
        down = down.astype(b16)
        low[:, cols] = down
        dvec_ref[2:3, cols] = jnp.sum(down.astype(f32), axis=0, keepdims=True)
    weight_grad(5, lambda cols: act[:, cols].T, dy_ref[...])
    weight(4).wait()
    for cols in tiles:
        wide[:, cols] = nt(low[...], held[4, cols, :])
    loads[3].wait()
    act[...] = norm_rows(mid[...], vec_ref[1:2, :]).astype(b16)
    weight_grad(4, lambda cols: act[:, cols].T, low[...])
    part, gain_sum = norm_back(mid[...], vec_ref[1:2, :], wide[...])
    dvec_ref[1:2, :] = gain_sum
    total = dy_ref[...].astype(f32) + part
    dmid[...] = total
    low[...] = total.astype(b16)
    loads[2].wait()
    weight_grad(3, lambda cols: att[:, cols].T, low[...])
    weight(3).wait()
    for cols in tiles:
        act[:, cols] = nt(low[...], held[3, cols, :]).astype(b16)
    loads[0].wait()
    loads[1].wait()
    dqkv[...] = jnp.zeros_like(dqkv)

    def one_head(head, carry):
        start, lanes = head_window(head, depth, width)
        cols = pl.ds(start, WIN)
        for block in range(rows // QB):
            here = slice(block * QB, (block + 1) * QB)
            upto = slice(0, (block + 1) * QB)
            down = jnp.where(lanes, act[here, cols], 0)
            dprob = nt(down, qkv[2, upto, cols])
            soft = prob[head, here, upto].astype(f32)
            lean = jnp.sum(dprob * soft, axis=-1, keepdims=True)
            ds = (soft * (dprob - lean)).astype(b16)
            dscore[here, upto] = ds
            dq = (nn(ds, qkv[1, upto, cols]) * scale).astype(b16)
            dqkv[0, here, cols] = jnp.where(lanes, dq, dqkv[0, here, cols])
        for block in range(rows // QB):
            here = slice(block * QB, (block + 1) * QB)
            since = slice(block * QB, rows)
            dk = (tn(dscore[since, here], qkv[0, since, cols]) * scale).astype(b16)
            dqkv[1, here, cols] = jnp.where(lanes, dk, dqkv[1, here, cols])
            dv = tn(prob[head, since, here], act[since, cols]).astype(b16)
            dqkv[2, here, cols] = jnp.where(lanes, dv, dqkv[2, here, cols])
        return carry

    lax.fori_loop(0, HEADS, one_head, 0)
    low[...] = norm_rows(x_ref[...].astype(f32), vec_ref[0:1, :]).astype(b16)
    for cols in tiles:
        turned[cols, :] = low[:, cols].T
    for index in (2, 1, 0):
        weight_grad(index, lambda cols: turned[cols, :], dqkv[index])
    for index in range(3):
        weight(index).wait()
    for cols in tiles:
        wide[:, cols] = (
            nt(dqkv[0], held[0, cols, :]) + nt(dqkv[1], held[1, cols, :]) + nt(dqkv[2], held[2, cols, :])
        )
    part, gain_sum = norm_back(x_ref[...].astype(f32), vec_ref[0:1, :], wide[...])
    dvec_ref[0:1, :] = gain_sum
    dvec_ref[4:8, :] = jnp.zeros_like(dvec_ref[4:8, :])
    dx_ref[...] = (dmid[...] + part).astype(b16)
    put(1, 0).wait()
    put(0, 1).wait()


def backward_layer(layer, mats, x, vec, dy, kept, grads):
    rows, width = x.shape
    f32, b16 = jnp.float32, jnp.bfloat16
    vm = pl.BlockSpec(memory_space=pltpu.VMEM)
    hbm = pl.BlockSpec(memory_space=pl.ANY)
    aliased = grads is not None
    return pl.pallas_call(
        functools.partial(backward_kernel, layer, aliased),
        out_shape=[
            jax.ShapeDtypeStruct(mats.shape, b16),
            jax.ShapeDtypeStruct((rows, width), b16),
            jax.ShapeDtypeStruct((8, width), f32),
        ],
        in_specs=[hbm, vm, vm, vm] + [hbm] * 5 + ([hbm] if aliased else []),
        out_specs=[hbm, vm, vm],
        scratch_shapes=[
            pltpu.VMEM((6, width, width), b16),
            pltpu.VMEM((3, rows, width), b16),
            pltpu.VMEM((HEADS, rows, rows), b16),
            pltpu.VMEM((rows, width), b16),
            pltpu.VMEM((rows, width), f32),
            pltpu.VMEM((rows, width), f32),
            pltpu.VMEM((rows, width), b16),
            pltpu.VMEM((rows, width), b16),
            pltpu.VMEM((rows, width), f32),
            pltpu.VMEM((rows, width), f32),
            pltpu.VMEM((3, rows, width), b16),
            pltpu.VMEM((rows, rows), b16),
            pltpu.VMEM((width, rows), b16),
            pltpu.VMEM((2, width, width), b16),
            pltpu.SemaphoreType.DMA((6,)),
            pltpu.SemaphoreType.DMA((5,)),
            pltpu.SemaphoreType.DMA((6,)),
        ],
        input_output_aliases={9: 0} if aliased else {},
        compiler_params=pltpu.CompilerParams(vmem_limit_bytes=VMEM_LIMIT),
        name="layer_backward",
    )(*((mats, x, vec, dy) + tuple(kept) + ((grads,) if aliased else ())))


def one_hot(rank):
    rows = rank.shape[0]
    return (rank[None, :] == jnp.arange(rows, dtype=jnp.int32)[:, None]).astype(jnp.bfloat16)


def rank_of(key):
    return jnp.sum((key[None, :] < key[:, None]).astype(jnp.int32), axis=1)


def padded(flat):
    lead, size = flat.shape
    full = -(-size // 1024) * 1024
    return jnp.pad(flat, ((0, 0), (0, full - size))).reshape(lead, full // 128, 128)


def share_all(packet, peers):
    if peers == 16:
        return share(packet, peers)
    return lax.all_gather(packet, BOTH, axis=0)


def gather_weights(own, peers):
    if peers == 16:
        return ag(own, PARTS, peers // 4)
    rows, width = own.shape
    return lax.all_gather(own, BOTH, axis=0, tiled=True).reshape(2, peers, rows, width)


def scatter_grads(terms, small, peers):
    if peers == 16:
        return rs(terms, small, PARTS, peers // 4)
    sections, _, rows, width = terms.shape
    terms = terms.reshape(sections * peers * rows, width)
    total = lax.psum_scatter(terms, BOTH, scatter_dimension=0, tiled=True).astype(jnp.float32)
    return total, lax.psum_scatter(small, BOTH, scatter_dimension=0, tiled=True)[0]


def local(entering, deal, seq_lens, mats, gains, biases):
    section = lax.axis_index("section")
    own_dp = lax.axis_index("dp")
    peers = lax.axis_size("dp")
    arrival = entering[0]
    batches, rows, width = arrival.shape
    per_peer = rows // peers
    per = 2 * width // peers
    vecs = jnp.concatenate([gains[0], biases[0]]).astype(jnp.bfloat16).astype(jnp.float32)
    packet = jnp.concatenate([deal.reshape(-1).astype(jnp.float32), vecs])
    shared = share_all(padded(packet[None])[0], peers).reshape(2, peers, -1)
    all_deal = jnp.where(section == 0, shared[0, :, : batches * rows], shared[1, :, : batches * rows])
    all_deal = all_deal.astype(jnp.int32).reshape(peers, batches, rows)
    small = shared[:, :, batches * rows : batches * rows + 2 * per].reshape(2, peers, 2, per)
    small = jnp.swapaxes(small, 1, 2).reshape(2, 4, width)
    small = jnp.pad(small, ((0, 0), (0, 4), (0, 0)))
    all_mats = gather_weights(mats[0].astype(jnp.bfloat16), peers)
    all_mats = all_mats.reshape(2, 6 * width, width)
    own_rows = own_dp * rows + jnp.arange(rows, dtype=jnp.int32)
    block_ids = jnp.arange(peers, dtype=jnp.int32)
    sends = []
    returns = []
    for batch in range(batches):
        hit = all_deal[:, batch][None, :, :] == own_rows[:, None, None]
        target = jnp.sum(jnp.where(hit, block_ids[None, :, None], 0), axis=(1, 2))
        key = target * rows + jnp.arange(rows, dtype=jnp.int32)
        pick = one_hot(rank_of(key))
        returns.append(pick)
        sends.append(nn(pick, arrival[batch]).astype(jnp.bfloat16))
    outgoing = jnp.stack(sends).reshape(2 * peers, per_peer, width)
    arrived = lax.all_to_all(outgoing, BOTH, split_axis=0, concat_axis=0, tiled=True)
    arrived = arrived.reshape(2, rows, width)
    own_deal = jnp.where(section == 0, deal[0], deal[1])
    place = one_hot(rank_of(own_deal))
    tokens = tn(place, arrived[0]).astype(jnp.bfloat16)
    cotangent = tn(place, arrived[1]).astype(jnp.bfloat16)
    lens = jnp.where(section == 0, seq_lens[0, 0], seq_lens[1, 0])
    ends = jnp.cumsum(lens)
    positions = jnp.arange(rows, dtype=jnp.int32)
    segment = jnp.sum((positions[:, None] >= ends[None, :]).astype(jnp.int32), axis=1)
    middle, *kept_low = forward_layer(0, all_mats, tokens, small[0], segment[:, None], segment[None])
    final, *kept_high = forward_layer(1, all_mats, middle, small[1], segment[:, None], segment[None])
    terms, down, vec_high = backward_layer(1, all_mats, middle, small[1], cotangent, kept_high, None)
    terms, down, vec_low = backward_layer(0, all_mats, tokens, small[0], down, kept_low, terms)
    terms = terms.reshape(2, peers, -1, width)
    vec_terms = jnp.stack([vec_low, vec_high])[:, :4].reshape(2, 2, peers, per)
    vec_terms = padded(jnp.swapaxes(vec_terms, 1, 2).reshape(2 * peers, 2 * per))
    shard_mats, vec_total = scatter_grads(terms, vec_terms, peers)
    vec_total = vec_total.reshape(-1)
    back = jnp.stack([nn(place, down), nn(place, final)]).astype(jnp.bfloat16)
    back = back.reshape(2 * peers, per_peer, width)
    returned = lax.all_to_all(back, BOTH, split_axis=0, concat_axis=0, tiled=True).reshape(2, rows, width)
    results = jnp.stack([tn(returns[batch], returned[batch]) for batch in range(batches)])
    return (
        results.astype(jnp.bfloat16)[None],
        shard_mats[None],
        vec_total[None, :per],
        vec_total[None, per : 2 * per],
    )


def solution(mesh):
    in_specs = (
        P("section", None, "dp", None),
        P(None, "dp"),
        P(None, "dp", None),
        P("section", "dp", None),
        P("section", "dp"),
        P("section", "dp"),
    )
    out_specs = (
        P("section", None, "dp", None),
        P("section", "dp", None),
        P("section", "dp"),
        P("section", "dp"),
    )
    return jax.shard_map(local, mesh=mesh, in_specs=in_specs, out_specs=out_specs, check_vma=False)
```

```python
import functools

import jax
import jax.numpy as jnp
from jax import lax
from jax.experimental import pallas as pl
from jax.experimental.pallas import tpu as pltpu
from jax.sharding import PartitionSpec as P

HEADS = 16
EPS = 1e-06
NEG = -1000000000.0
BOTH = ("section", "dp")
MESH = pl.DeviceIdType.MESH
PARTS = ((0, 112, "zxy"), (112, 112, "zyx"), (224, 128, "xzy"), (352, 128, "yzx"))


def greet(total, me, peers):
    barrier = pltpu.get_barrier_semaphore()

    def one(step, carry):
        other = lax.rem(me + step, total)
        pl.semaphore_signal(
            barrier, inc=1, device_id=(other // peers, lax.rem(other, peers)), device_id_type=MESH
        )
        return carry

    lax.fori_loop(1, total, one, 0)
    pl.semaphore_wait(barrier, total - 1)


def coords():
    s=lax.axis_index("section"); d=lax.axis_index("dp")
    return s,d,d//4,(d//2)%2,d%2

def items():
    out=[]
    for bx in (0,1):
        for by in (0,1):
            for dz in (0,-1,1,-2,2,-3,3):
                out.append((bx,by,dz))
    return out
def hops(it): return it[0]+it[1]+abs(it[2])
def arrival(order,it):
    diff={"x":it[0]!=0,"y":it[1]!=0,"z":it[2]!=0}
    last=None
    for k,dim in enumerate(order):
        if diff[dim]: last=k
    return last

def neighbours(s,d,z,y,c,zn):
    return [(None,(1-s,d)),(None,(s,(z*2+1-y)*2+c)),(None,(s,(z*2+y)*2+1-c)),(z>0,(s,d-4)),(z<zn-1,(s,d+4))]


def rs_kernel(parts,zn,g_ref,v_ref,o_ref,vo_ref,land,buf,obuf,vland,*rest):
    nP=len(parts)
    lks=rest[:nP]
    ssem,rsem,cs,cr,lsem,osem,vsend,vrecv=rest[nP:]
    s,d,z,y,c=coords()
    peers=4*zn
    total_dev=2*peers
    me=s*peers+d
    greet(total_dev,me,peers)
    vland[me]=v_ref[me]
    def small(step,carry):
        other=lax.rem(me+step,total_dev)
        pltpu.make_async_remote_copy(v_ref.at[other],vland.at[me],vsend,vrecv,device_id=(other//peers,lax.rem(other,peers)),device_id_type=MESH).start()
        return carry
    lax.fori_loop(1,total_dev,small,0)
    sib=(s,(z*2+y)*2+1-c)
    def where(it):
        s2=1-s if it[0] else s
        y2=1-y if it[1] else y
        return s2,z+it[2],y2
    def conds(it):
        cl=[]
        if it[2]<0: cl.append(z+it[2]>=0)
        if it[2]>0: cl.append(z+it[2]<=zn-1)
        return cl
    def guarded(cl,fn):
        if not cl: fn(); return
        e=cl[0]
        for q in cl[1:]: e=jnp.logical_and(e,q)
        pl.when(e)(fn)
    def slot_base(order):
        sizes={"x":2,"y":2,"z":zn}
        base={};cur=0
        for k,dim in enumerate(order):
            n=1
            for q in order[k+1:]: n*=sizes[q]
            if dim=="z": n*=2*zn
            base[dim]=cur; cur+=n
        return base,cur
    def slot(p,dim,side,dest):
        order=parts[p][2][::-1]
        base,_=slot_base(order)
        k=order.index(dim)
        v={"x":dest[0],"z":dest[1],"y":dest[2]}
        idx=0
        for q in order[k+1:]:
            idx=idx*(zn if q=="z" else 2)+v[q]
        if dim=="z": idx=(idx*zn+dest[1])*2+side
        return base[dim]+idx
    evs=[]
    for p in range(nP):
        for it in items():
            if abs(it[2])<=zn-1: evs.append((-hops(it),p,it))
    evs.sort(key=lambda e:e[0])
    seq=[(p,it) for _,p,it in evs]
    def core_dsc(p,it,mine):
        r0,rn,_=parts[p]
        s2,z2,y2=where(it)
        idx=(s2*zn+z2)*2+y2
        cc=c if mine else 1-c
        return pltpu.make_async_remote_copy(g_ref.at[s2,(z2*2+y2)*2+cc,pl.ds(r0,rn)],land.at[idx,pl.ds(r0,rn)],cs.at[p,idx],cr.at[p,idx],device_id=sib,device_id_type=MESH)
    for p,it in seq:
        guarded(conds(it),lambda p=p,it=it: core_dsc(p,it,False).start())
    def load(i):
        p,it=seq[i]
        r0,rn,_=parts[p]
        s2,z2,y2=where(it)
        return pltpu.make_async_copy(g_ref.at[s2,(z2*2+y2)*2+c,pl.ds(r0,rn)],buf.at[i%NB,pl.ds(0,rn)],lsem.at[i%NB])
    NB=buf.shape[0]
    for i in range(min(NB-1,len(seq))):
        guarded(conds(seq[i][1]),lambda i=i: load(i).start())
    def contribs(p,it):
        order=parts[p][2][::-1]
        diff={"x":it[0],"y":it[1],"z":it[2]}
        out=[];nxt=None
        for dim in order:
            if dim=="z":
                if it[2]==0: out+=[("z",0,z>0),("z",1,z<zn-1)]
                elif it[2]>0: out.append(("z",0,z>0))
                else: out.append(("z",1,z<zn-1))
                if it[2]!=0: nxt="r" if it[2]>0 else "l"; break
            else:
                if diff[dim]: nxt=dim; break
                out.append((dim,0,None))
        return out,nxt
    semoff=[0]
    for p in range(nP): semoff.append(semoff[-1]+slot_base(parts[p][2][::-1])[1])
    def out_dsc(p,it,nxt):
        r0,rn,_=parts[p]
        dest=where(it)
        s2,z2,y2=dest
        idx=(s2*zn+z2)*2+y2
        dim="z" if nxt in "lr" else nxt
        side=1 if nxt=="l" else 0
        sl=slot(p,dim,side,dest)
        dev={"x":(1-s,d),"y":(s,(z*2+1-y)*2+c),"l":(s,d-4),"r":(s,d+4)}[nxt]
        return pltpu.make_async_remote_copy(land.at[idx,pl.ds(r0,rn)],lks[p].at[sl],ssem.at[p,idx],rsem.at[semoff[p]+sl],device_id=dev,device_id_type=MESH)
    for i,(p,it) in enumerate(seq):
        r0,rn,_=parts[p]
        if i+NB-1<len(seq):
            guarded(conds(seq[i+NB-1][1]),lambda i=i: load(i+NB-1).start())
        def ev(i=i,p=p,it=it,r0=r0,rn=rn):
            dest=where(it)
            s2,z2,y2=dest
            idx=(s2*zn+z2)*2+y2
            con,nxt=contribs(p,it)
            lk=lks[p]
            load(i).wait()
            core_dsc(p,it,True).wait_recv()
            plain=[x for x in con if x[2] is None]
            cond=[x for x in con if x[2] is not None]
            def rdsc(dim,side):
                sl=slot(p,dim,side,dest)
                return pltpu.make_async_remote_copy(lk.at[sl],lk.at[sl],ssem.at[p,idx],rsem.at[semoff[p]+sl],device_id=sib,device_id_type=MESH),sl
            for dim,side,_ in plain: rdsc(dim,side)[0].wait_recv()
            for dim,side,cnd in cond:
                pl.when(cnd)(lambda dim=dim,side=side: rdsc(dim,side)[0].wait_recv())
            if not cond: variants=[(None,plain)]
            elif len(cond)==1:
                variants=[(cond[0][2],plain+cond),(jnp.logical_not(cond[0][2]),plain)]
            else:
                a,b=cond
                variants=[(jnp.logical_and(a[2],b[2]),plain+cond),(jnp.logical_and(a[2],jnp.logical_not(b[2])),plain+[a]),
                          (jnp.logical_and(jnp.logical_not(a[2]),b[2]),plain+[b])]
            def total(lst):
                slots=[slot(p,dim,side,dest) for dim,side,_ in lst]
                CH=16
                def body(k,_):
                    ro=pl.multiple_of(k*CH,CH)
                    acc=buf[i%NB,pl.ds(ro,CH),:].astype(jnp.float32)+land[idx,pl.ds(r0+ro,CH),:].astype(jnp.float32)
                    for sl in slots: acc=acc+lk[sl,pl.ds(ro,CH),:].astype(jnp.float32)
                    if nxt is None: obuf[pl.ds(r0+ro,CH),:]=acc
                    else: land[idx,pl.ds(r0+ro,CH),:]=acc.astype(jnp.bfloat16)
                    return 0
                lax.fori_loop(0,rn//CH,body,0)
            for cnd,lst in variants:
                if cnd is None: total(lst)
                else: pl.when(cnd)(lambda lst=lst: total(lst))
            if nxt is not None: out_dsc(p,it,nxt).start()
            else: pltpu.make_async_copy(obuf.at[pl.ds(r0,rn)],o_ref.at[pl.ds(r0,rn)],osem.at[p]).start()
        guarded(conds(it),ev)
    for p,it in seq:
        def fin(p=p,it=it):
            core_dsc(p,it,False).wait_send()
            nxt=contribs(p,it)[1]
            if nxt is not None: out_dsc(p,it,nxt).wait_send()
        guarded(conds(it),fin)
    for p,(r0,rn,_) in enumerate(parts):
        pltpu.make_async_copy(obuf.at[pl.ds(r0,rn)],o_ref.at[pl.ds(r0,rn)],osem.at[p]).wait()
    rest_of=vland.at[pl.ds(0,total_dev-1)]
    bulk=pltpu.make_async_remote_copy(rest_of,rest_of,vsend,vrecv,device_id=(0,0),device_id_type=MESH)
    bulk.wait_recv()
    bulk.wait_send()
    vo_ref[...]=jnp.sum(vland[...],axis=0)


def slot_count(order,zn):
    sizes={"x":2,"y":2,"z":zn};cur=0
    for k,dim in enumerate(order):
        n=1
        for q in order[k+1:]: n*=sizes[q]
        if dim=="z": n*=2*zn
        cur+=n
    return cur
def rs(g,v,parts,zn,cid=1,nb=4):
    n=len(parts)
    cnt=[slot_count(p[2][::-1],zn) for p in parts]
    mx=max(p[1] for p in parts)
    return pl.pallas_call(functools.partial(rs_kernel,parts,zn),
        out_shape=[jax.ShapeDtypeStruct((480,1280),jnp.float32),jax.ShapeDtypeStruct(v.shape[1:],jnp.float32)],
        in_specs=[pl.BlockSpec(memory_space=pl.ANY),pl.BlockSpec(memory_space=pltpu.VMEM)],
        out_specs=[pl.BlockSpec(memory_space=pl.ANY),pl.BlockSpec(memory_space=pltpu.VMEM)],
        scratch_shapes=[pltpu.VMEM((4*zn,480,1280),jnp.bfloat16),pltpu.VMEM((nb,mx,1280),jnp.bfloat16),pltpu.VMEM((480,1280),jnp.float32),pltpu.VMEM(v.shape,jnp.float32)]
          +[pltpu.VMEM((cnt[p],parts[p][1],1280),jnp.bfloat16) for p in range(n)]
          +[pltpu.SemaphoreType.DMA((n,4*zn)),pltpu.SemaphoreType.DMA((sum(cnt),)),
          pltpu.SemaphoreType.DMA((n,4*zn)),pltpu.SemaphoreType.DMA((n,4*zn)),pltpu.SemaphoreType.DMA((nb,)),pltpu.SemaphoreType.DMA((n,)),pltpu.SemaphoreType.DMA,pltpu.SemaphoreType.DMA],
        compiler_params=pltpu.CompilerParams(collective_id=cid,has_side_effects=True,vmem_limit_bytes=62*2**20))(g,v)


WIN = 256
QB = 128
GC = 0.7978845608028654
GA = 0.044715
VMEM_LIMIT = 62 * 2**20


def nn(left, right):
    return jnp.dot(left, right, preferred_element_type=jnp.float32)


def nt(left, right):
    return lax.dot_general(
        left, right, (((1,), (1,)), ((), ())), preferred_element_type=jnp.float32
    )


def tn(left, right):
    return lax.dot_general(
        left, right, (((0,), (0,)), ((), ())), preferred_element_type=jnp.float32
    )


def head_window(head, depth, width):
    start = jnp.minimum((head * depth) // 128, (width - WIN) // 128) * 128
    start = pl.multiple_of(start, 128)
    lane = lax.broadcasted_iota(jnp.int32, (1, WIN), 1) + (start - head * depth)
    return start, (lane >= 0) & (lane < depth)


def norm_rows(value, gain):
    return value * lax.rsqrt(jnp.mean(value * value, axis=-1, keepdims=True) + EPS) * gain


def norm_back(value, gain, down):
    inv = lax.rsqrt(jnp.mean(value * value, axis=-1, keepdims=True) + EPS)
    unit = value * inv
    scaled = down * gain
    lean = jnp.mean(scaled * unit, axis=-1, keepdims=True)
    return inv * (scaled - unit * lean), jnp.sum(down * unit, axis=0, keepdims=True)


def forward_kernel(
    layer, mats_ref, x_ref, vec_ref, segc_ref, segr_ref,
    y_ref, qkv_out, prob_out, att_out, mid_out, u_out,
    held, qkv, prob, att, mid, u, norm, mask, sems, out_sems,
):
    rows, width = x_ref.shape
    depth = width // HEADS
    scale = depth ** (-0.5)

    def weight(index):
        return pltpu.make_async_copy(
            mats_ref.at[layer, pl.ds(index * width, width)], held.at[index], sems.at[index]
        )

    keeps = [
        pltpu.make_async_copy(src, dst, out_sems.at[index])
        for index, (src, dst) in enumerate(
            ((qkv, qkv_out), (prob, prob_out), (att, att_out), (mid, mid_out), (u, u_out))
        )
    ]
    for index in range(6):
        weight(index).start()
    tiles = [slice(c, c + WIN) for c in range(0, width, WIN)]
    norm[...] = norm_rows(x_ref[...].astype(jnp.float32), vec_ref[0:1, :]).astype(jnp.bfloat16)
    qi = lax.broadcasted_iota(jnp.int32, (rows, rows), 0)
    ki = lax.broadcasted_iota(jnp.int32, (rows, rows), 1)
    mask[...] = jnp.where((segc_ref[...] == segr_ref[...]) & (ki <= qi), 1.0, 0.0)
    for index in range(3):
        weight(index).wait()
        for cols in tiles:
            qkv[index, :, cols] = nn(norm[...], held[index, :, cols]).astype(jnp.bfloat16)
    keeps[0].start()
    att[...] = jnp.zeros_like(att)

    def one_head(head, carry):
        start, lanes = head_window(head, depth, width)
        cols = pl.ds(start, WIN)
        for block in range(rows // QB):
            here = slice(block * QB, (block + 1) * QB)
            upto = slice(0, (block + 1) * QB)
            query = jnp.where(lanes, qkv[0, here, cols], 0)
            score = nt(query, qkv[1, upto, cols]) * scale
            score = jnp.where(mask[here, upto] > 0.5, score, NEG)
            expd = jnp.exp(score - jnp.max(score, axis=-1, keepdims=True))
            soft = (expd * (1.0 / jnp.sum(expd, axis=-1, keepdims=True))).astype(jnp.bfloat16)
            prob[head, here, upto] = soft
            mixed = nn(soft, qkv[2, upto, cols])
            att[here, cols] = jnp.where(lanes, mixed.astype(jnp.bfloat16), att[here, cols])
        return carry

    lax.fori_loop(0, HEADS, one_head, 0)
    keeps[1].start()
    keeps[2].start()
    weight(3).wait()
    for cols in tiles:
        mid[:, cols] = x_ref[:, cols].astype(jnp.float32) + nn(att[...], held[3, :, cols])
    keeps[3].start()
    norm[...] = norm_rows(mid[...], vec_ref[1:2, :]).astype(jnp.bfloat16)
    weight(4).wait()
    for cols in tiles:
        u[:, cols] = nn(norm[...], held[4, :, cols]) + vec_ref[2:3, cols]
    keeps[4].start()
    for cols in tiles:
        pre = u[:, cols]
        act = 0.5 * pre * (1.0 + jnp.tanh(GC * (pre + GA * (pre * pre * pre))))
        norm[:, cols] = act.astype(jnp.bfloat16)
    weight(5).wait()
    for cols in tiles:
        out = mid[:, cols] + (nn(norm[...], held[5, :, cols]) + vec_ref[3:4, cols])
        y_ref[:, cols] = out.astype(jnp.bfloat16)
    for keep in keeps:
        keep.wait()


def forward_layer(layer, mats, x, vec, segc, segr):
    rows, width = x.shape
    f32, b16 = jnp.float32, jnp.bfloat16
    vm = pl.BlockSpec(memory_space=pltpu.VMEM)
    hbm = pl.BlockSpec(memory_space=pl.ANY)
    kept = [
        ((3, rows, width), b16), ((HEADS, rows, rows), b16), ((rows, width), b16),
        ((rows, width), f32), ((rows, width), f32),
    ]
    return pl.pallas_call(
        functools.partial(forward_kernel, layer),
        out_shape=[jax.ShapeDtypeStruct((rows, width), b16)]
        + [jax.ShapeDtypeStruct(shape, dtype) for shape, dtype in kept],
        in_specs=[hbm, vm, vm, vm, vm],
        out_specs=[vm] + [hbm] * 5,
        scratch_shapes=[pltpu.VMEM((6, width, width), b16)]
        + [pltpu.VMEM(shape, dtype) for shape, dtype in kept]
        + [
            pltpu.VMEM((rows, width), b16),
            pltpu.VMEM((rows, rows), f32),
            pltpu.SemaphoreType.DMA((6,)),
            pltpu.SemaphoreType.DMA((5,)),
        ],
        compiler_params=pltpu.CompilerParams(vmem_limit_bytes=VMEM_LIMIT),
        name="layer_forward",
    )(mats, x, vec, segc, segr)


def backward_kernel(layer, aliased, *refs):
    mats_ref, x_ref, vec_ref, dy_ref, qkv_in, prob_in, att_in, mid_in, u_in = refs[:9]
    rest = refs[10:] if aliased else refs[9:]
    (
        grads_ref, dx_ref, dvec_ref,
        held, qkv, prob, att, mid, u, act, low, wide, dmid, dqkv, dscore, turned, stage,
        sems, in_sems, out_sems,
    ) = rest
    rows, width = x_ref.shape
    depth = width // HEADS
    scale = depth ** (-0.5)
    f32, b16 = jnp.float32, jnp.bfloat16
    tiles = [slice(c, c + WIN) for c in range(0, width, WIN)]

    def weight(index):
        return pltpu.make_async_copy(
            mats_ref.at[layer, pl.ds(index * width, width)], held.at[index], sems.at[index]
        )

    loads = [
        pltpu.make_async_copy(src, dst, in_sems.at[index])
        for index, (src, dst) in enumerate(
            ((qkv_in, qkv), (prob_in, prob), (att_in, att), (mid_in, mid), (u_in, u))
        )
    ]
    loads[4].start()
    weight(5).start()
    weight(4).start()
    loads[3].start()
    weight(3).start()
    loads[2].start()
    loads[0].start()
    loads[1].start()
    for index in range(3):
        weight(index).start()

    def put(index, slot):
        return pltpu.make_async_copy(
            stage.at[slot], grads_ref.at[layer, pl.ds(index * width, width)], out_sems.at[index]
        )

    slots = {5: 0, 4: 1, 3: 0, 2: 1, 1: 0, 0: 1}
    before = {3: 5, 2: 4, 1: 3, 0: 2}

    def weight_grad(index, left_t, right):
        slot = slots[index]
        if index in before:
            put(before[index], slot).wait()
        for cols in tiles:
            stage[slot, cols, :] = nn(left_t(cols), right).astype(b16)
        put(index, slot).start()

    dvec_ref[3:4, :] = jnp.sum(dy_ref[...].astype(f32), axis=0, keepdims=True)
    loads[4].wait()
    weight(5).wait()
    for cols in tiles:
        pre = u[:, cols]
        square = pre * pre
        bent = jnp.tanh(GC * (pre + GA * (square * pre)))
        half = 0.5 * (1.0 + bent)
        act[:, cols] = (pre * half).astype(b16)
        slope = half + (0.5 * GC) * pre * (1.0 - bent * bent) * (1.0 + (3.0 * GA) * square)
        down = nt(dy_ref[...], held[5, cols, :]) * slope
        down = down.astype(b16)
        low[:, cols] = down
        dvec_ref[2:3, cols] = jnp.sum(down.astype(f32), axis=0, keepdims=True)
    weight_grad(5, lambda cols: act[:, cols].T, dy_ref[...])
    weight(4).wait()
    for cols in tiles:
        wide[:, cols] = nt(low[...], held[4, cols, :])
    loads[3].wait()
    act[...] = norm_rows(mid[...], vec_ref[1:2, :]).astype(b16)
    weight_grad(4, lambda cols: act[:, cols].T, low[...])
    part, gain_sum = norm_back(mid[...], vec_ref[1:2, :], wide[...])
    dvec_ref[1:2, :] = gain_sum
    total = dy_ref[...].astype(f32) + part
    dmid[...] = total
    low[...] = total.astype(b16)
    loads[2].wait()
    weight_grad(3, lambda cols: att[:, cols].T, low[...])
    weight(3).wait()
    for cols in tiles:
        act[:, cols] = nt(low[...], held[3, cols, :]).astype(b16)
    loads[0].wait()
    loads[1].wait()
    dqkv[...] = jnp.zeros_like(dqkv)

    def one_head(head, carry):
        start, lanes = head_window(head, depth, width)
        cols = pl.ds(start, WIN)
        for block in range(rows // QB):
            here = slice(block * QB, (block + 1) * QB)
            upto = slice(0, (block + 1) * QB)
            down = jnp.where(lanes, act[here, cols], 0)
            dprob = nt(down, qkv[2, upto, cols])
            soft = prob[head, here, upto].astype(f32)
            lean = jnp.sum(dprob * soft, axis=-1, keepdims=True)
            ds = (soft * (dprob - lean)).astype(b16)
            dscore[here, upto] = ds
            dq = (nn(ds, qkv[1, upto, cols]) * scale).astype(b16)
            dqkv[0, here, cols] = jnp.where(lanes, dq, dqkv[0, here, cols])
        for block in range(rows // QB):
            here = slice(block * QB, (block + 1) * QB)
            since = slice(block * QB, rows)
            dk = (tn(dscore[since, here], qkv[0, since, cols]) * scale).astype(b16)
            dqkv[1, here, cols] = jnp.where(lanes, dk, dqkv[1, here, cols])
            dv = tn(prob[head, since, here], act[since, cols]).astype(b16)
            dqkv[2, here, cols] = jnp.where(lanes, dv, dqkv[2, here, cols])
        return carry

    lax.fori_loop(0, HEADS, one_head, 0)
    low[...] = norm_rows(x_ref[...].astype(f32), vec_ref[0:1, :]).astype(b16)
    for cols in tiles:
        turned[cols, :] = low[:, cols].T
    for index in (2, 1, 0):
        weight_grad(index, lambda cols: turned[cols, :], dqkv[index])
    for index in range(3):
        weight(index).wait()
    for cols in tiles:
        wide[:, cols] = (
            nt(dqkv[0], held[0, cols, :]) + nt(dqkv[1], held[1, cols, :]) + nt(dqkv[2], held[2, cols, :])
        )
    part, gain_sum = norm_back(x_ref[...].astype(f32), vec_ref[0:1, :], wide[...])
    dvec_ref[0:1, :] = gain_sum
    dvec_ref[4:8, :] = jnp.zeros_like(dvec_ref[4:8, :])
    dx_ref[...] = (dmid[...] + part).astype(b16)
    put(1, 0).wait()
    put(0, 1).wait()


def backward_layer(layer, mats, x, vec, dy, kept, grads):
    rows, width = x.shape
    f32, b16 = jnp.float32, jnp.bfloat16
    vm = pl.BlockSpec(memory_space=pltpu.VMEM)
    hbm = pl.BlockSpec(memory_space=pl.ANY)
    aliased = grads is not None
    return pl.pallas_call(
        functools.partial(backward_kernel, layer, aliased),
        out_shape=[
            jax.ShapeDtypeStruct(mats.shape, b16),
            jax.ShapeDtypeStruct((rows, width), b16),
            jax.ShapeDtypeStruct((8, width), f32),
        ],
        in_specs=[hbm, vm, vm, vm] + [hbm] * 5 + ([hbm] if aliased else []),
        out_specs=[hbm, vm, vm],
        scratch_shapes=[
            pltpu.VMEM((6, width, width), b16),
            pltpu.VMEM((3, rows, width), b16),
            pltpu.VMEM((HEADS, rows, rows), b16),
            pltpu.VMEM((rows, width), b16),
            pltpu.VMEM((rows, width), f32),
            pltpu.VMEM((rows, width), f32),
            pltpu.VMEM((rows, width), b16),
            pltpu.VMEM((rows, width), b16),
            pltpu.VMEM((rows, width), f32),
            pltpu.VMEM((rows, width), f32),
            pltpu.VMEM((3, rows, width), b16),
            pltpu.VMEM((rows, rows), b16),
            pltpu.VMEM((width, rows), b16),
            pltpu.VMEM((2, width, width), b16),
            pltpu.SemaphoreType.DMA((6,)),
            pltpu.SemaphoreType.DMA((5,)),
            pltpu.SemaphoreType.DMA((6,)),
        ],
        input_output_aliases={9: 0} if aliased else {},
        compiler_params=pltpu.CompilerParams(vmem_limit_bytes=VMEM_LIMIT),
        name="layer_backward",
    )(*((mats, x, vec, dy) + tuple(kept) + ((grads,) if aliased else ())))


def as_row(column):
    rows = column.shape[0]
    return jnp.broadcast_to(column, (rows, 128)).T[0:1, :]


def as_column(row):
    size = row.shape[1]
    return jnp.broadcast_to(row, (128, size)).T[:, 0:1]


def ones_where(flag):
    return jnp.where(flag, 1.0, 0.0)


def gather_events(parts,zn,place,own,w_ref,ssem,rsem,cs,cr):
    s,d,z,y,c=place
    KIND={"x":0,"y":1,"l":2,"r":3}
    def where(it):
        s2=1-s if it[0] else s
        y2=1-y if it[1] else y
        z2=z+it[2]
        return s2,z2,y2
    def dsc(p,it,kind):
        r0,rn,order=parts[p]
        s2,z2,y2=where(it)
        idx=s2*(2*zn)+z2*2+y2
        is_own=it==(0,0,0)
        src=own.at[pl.ds(r0,rn)] if is_own else w_ref.at[s2,(z2*2+y2)*2+c,pl.ds(r0,rn)]
        dst=w_ref.at[s2,(z2*2+y2)*2+c,pl.ds(r0,rn)]
        if kind=="core":
            dev=(s,(z*2+y)*2+1-c)
            return pltpu.make_async_remote_copy(src,dst,cs.at[p,idx],cr.at[p,idx],device_id=dev,device_id_type=MESH)
        dev={"x":(1-s,d),"y":(s,(z*2+1-y)*2+c),"l":(s,d-4),"r":(s,d+4)}[kind]
        return pltpu.make_async_remote_copy(src,dst,ssem.at[KIND[kind],p,idx],rsem.at[p,idx],device_id=dev,device_id_type=MESH)
    def cdsc(p,it):
        r0,rn,order=parts[p]
        s2,z2,y2=where(it)
        idx=s2*(2*zn)+z2*2+y2
        dst=w_ref.at[s2,(z2*2+y2)*2+1-c,pl.ds(r0,rn)]
        return pltpu.make_async_remote_copy(dst,dst,cs.at[p,idx],cr.at[p,idx],device_id=(s,(z*2+y)*2+1-c),device_id_type=MESH)
    def conds(it,kind):
        cs_=[]
        if it[2]<0: cs_.append(z+it[2]>=0)
        if it[2]>0: cs_.append(z+it[2]<=zn-1)
        if kind=="l": cs_.append(z>0)
        if kind=="r": cs_.append(z<zn-1)
        return cs_
    def guarded(cl,fn):
        if not cl: fn(); return
        e=cl[0]
        for q in cl[1:]: e=jnp.logical_and(e,q)
        pl.when(e)(fn)
    def sends(p,it):
        order=parts[p][2]
        a=arrival(order,it)
        ks=[]
        if a is not None and order[a]=="z": ks.append("l" if it[2]>0 else "r")
        for dim in order[(a+1) if a is not None else 0:]:
            ks += ["r","l"] if dim=="z" else [dim]
        ks.append("core")
        return ks
    evs=[]
    for p in range(len(parts)):
        for it in items():
            if abs(it[2])<zn: evs.append((hops(it),p,it))
    evs.sort(key=lambda e:e[0])
    first=[]
    later=[]
    for h,p,it in evs:
        def ev(p=p,it=it):
            if it!=(0,0,0): dsc(p,it,"x").wait_recv()
            for k in sends(p,it):
                guarded(conds((0,0,0),k), lambda k=k: dsc(p,it,k).start())
        (later if h else first).append(lambda it=it,ev=ev: guarded(conds(it,None),ev))
    def finish():
        for _,p,it in evs:
            def fin(p=p,it=it):
                cdsc(p,it).wait_recv()
                for k in sends(p,it):
                    guarded(conds((0,0,0),k), lambda k=k: dsc(p,it,k).wait_send())
            guarded(conds(it,None),fin)
    return first,later,finish


def enter_kernel(
    parts, zn, mats_ref, packet_ref, deal_ref, tokens_ref,
    w_ref, shared_ref, x_ref, cot_ref, picks_ref, place_ref,
    own, wide_rows, strips32, sendbuf, landed, order,
    own_sem, lsem, ssem, rsem, cs, cr, psend, precv, tsend, trecv,
):
    s, d, z, y, c = coords()
    peers = 4 * zn
    total = 2 * peers
    me = s * peers + d
    batches, rows, width = tokens_ref.shape
    per_peer = rows // peers
    strips = width // 128
    f32, b16 = jnp.float32, jnp.bfloat16
    cast_in = pltpu.make_async_copy(mats_ref, wide_rows, own_sem)
    cast_in.start()
    greet(total, me, peers)
    shared_ref[me] = packet_ref[...]

    def tell(step, carry):
        other = lax.rem(me + step, total)
        pltpu.make_async_remote_copy(
            packet_ref, shared_ref.at[me], psend, precv,
            device_id=(other // peers, lax.rem(other, peers)), device_id_type=MESH,
        ).start()
        return carry

    lax.fori_loop(1, total, tell, 0)
    cast_in.wait()
    own[...] = wide_rows[...].astype(b16)
    lc = pltpu.make_async_copy(own, w_ref.at[s, d], lsem)
    lc.start()
    start_events, rest_events, finish = gather_events(
        parts, zn, (s, d, z, y, c), own, w_ref, ssem, rsem, cs, cr
    )
    for event in start_events:
        event()
    sub = lax.broadcasted_iota(jnp.int32, (rows, rows), 0).astype(f32)
    lane = lax.broadcasted_iota(jnp.int32, (rows, rows), 1).astype(f32)
    mine_row = jnp.where(s == 0, deal_ref[0:1, :], deal_ref[1:2, :])
    mine_col = as_column(mine_row)
    rank_col = jnp.sum(ones_where(mine_row < mine_col), axis=1, keepdims=True)
    order[...] = ones_where(lane == rank_col).astype(b16)
    rank_row = jnp.sum(ones_where(mine_col < mine_row), axis=0, keepdims=True)
    place_ref[...] = ones_where(sub == rank_row).astype(b16)
    rest = shared_ref.at[pl.ds(0, total - 1)]
    bulk = pltpu.make_async_remote_copy(
        rest, rest, psend, precv, device_id=(0, 0), device_id_type=MESH
    )
    bulk.wait_recv()
    index_col = lax.broadcasted_iota(jnp.int32, (rows, 1), 0).astype(f32)
    ids_col = index_col + (d * rows).astype(f32)
    for batch in range(batches):

        def look(block, found):
            known = shared_ref[s * peers + block]
            for line in range(rows // 128):
                at = batch * (rows // 128) + line
                found = jnp.where(ids_col == known[at : at + 1, :], block.astype(f32), found)
            return found

        found = lax.fori_loop(0, peers, look, jnp.zeros((rows, 128), f32))
        key_col = jnp.sum(found, axis=1, keepdims=True) * rows + index_col
        key_row = as_row(key_col)
        rank_row = jnp.sum(ones_where(key_col < key_row), axis=0, keepdims=True)
        rank_col = jnp.sum(ones_where(key_row < key_col), axis=1, keepdims=True)
        picks_ref[batch] = ones_where(lane == rank_col).astype(b16)
        pick = ones_where(sub == rank_row).astype(b16)
        for strip in range(strips):
            part = nn(pick, tokens_ref[batch, :, strip * 128 : (strip + 1) * 128])
            strips32[:, strip * per_peer : (strip + 1) * per_peer, :] = part.reshape(peers, per_peer, 128)
        sendbuf[batch] = strips32[...].astype(b16)

    landed[me] = sendbuf[s, d]

    def give(step, carry):
        other = lax.rem(me + step, total)
        sec, dp = other // peers, lax.rem(other, peers)
        pltpu.make_async_remote_copy(
            sendbuf.at[sec, dp], landed.at[me], tsend, trecv.at[s],
            device_id=(sec, dp), device_id_type=MESH,
        ).start()
        return carry

    lax.fori_loop(1, total, give, 0)
    for event in rest_events:
        event()

    def take(kind, out_ref):
        def wait(count):
            some = landed.at[pl.ds(0, count)]
            pltpu.make_async_remote_copy(
                some, some, tsend, trecv.at[kind], device_id=(0, 0), device_id_type=MESH
            ).wait_recv()

        pl.when(s == kind)(lambda: wait(peers - 1))
        pl.when(s != kind)(lambda: wait(peers))
        strips32[...] = landed[pl.ds(kind * peers, peers)].astype(f32)
        for strip in range(strips):
            part = strips32[:, strip * per_peer : (strip + 1) * per_peer, :].reshape(rows, 128)
            out_ref[:, strip * 128 : (strip + 1) * 128] = nn(order[...], part.astype(b16)).astype(b16)

    take(0, x_ref)
    take(1, cot_ref)
    finish()
    lc.wait()
    bulk.wait_send()
    most = landed.at[pl.ds(0, total - 1)]
    pltpu.make_async_remote_copy(
        most, most, tsend, trecv.at[0], device_id=(0, 0), device_id_type=MESH
    ).wait_send()


def enter(mats, packet, deal, tokens, parts, zn):
    n = len(parts)
    peers = 4 * zn
    batches, rows, width = tokens.shape
    strip_rows = rows // peers * (width // 128)
    f32, b16 = jnp.float32, jnp.bfloat16
    vm = pl.BlockSpec(memory_space=pltpu.VMEM)
    hbm = pl.BlockSpec(memory_space=pl.ANY)
    dma = pltpu.SemaphoreType.DMA
    return pl.pallas_call(
        functools.partial(enter_kernel, parts, zn),
        out_shape=[
            jax.ShapeDtypeStruct((2, peers) + mats.shape, b16),
            jax.ShapeDtypeStruct((2 * peers,) + packet.shape, f32),
            jax.ShapeDtypeStruct((rows, width), b16),
            jax.ShapeDtypeStruct((rows, width), b16),
            jax.ShapeDtypeStruct((batches, rows, rows), b16),
            jax.ShapeDtypeStruct((rows, rows), b16),
        ],
        in_specs=[hbm, vm, vm, vm],
        out_specs=[hbm, vm, vm, vm, vm, vm],
        scratch_shapes=[
            pltpu.VMEM(mats.shape, b16),
            pltpu.VMEM(mats.shape, f32),
            pltpu.VMEM((peers, strip_rows, 128), f32),
            pltpu.VMEM((batches, peers, strip_rows, 128), b16),
            pltpu.VMEM((2 * peers, strip_rows, 128), b16),
            pltpu.VMEM((rows, rows), b16),
            dma, dma, dma((4, n, peers)), dma((n, peers)), dma((n, peers)), dma((n, peers)),
            dma, dma, dma, dma((2,)),
        ],
        compiler_params=pltpu.CompilerParams(
            collective_id=0, has_side_effects=True, vmem_limit_bytes=VMEM_LIMIT
        ),
        name="enter",
    )(mats, packet, deal, tokens)


def one_hot(rank):
    rows = rank.shape[0]
    return (rank[None, :] == jnp.arange(rows, dtype=jnp.int32)[:, None]).astype(jnp.bfloat16)


def rank_of(key):
    return jnp.sum((key[None, :] < key[:, None]).astype(jnp.int32), axis=1)


def padded(flat):
    lead, size = flat.shape
    full = -(-size // 1024) * 1024
    return jnp.pad(flat, ((0, 0), (0, full - size))).reshape(lead, full // 128, 128)


def enter_plain(own, packet, deal, tokens, peers):
    section = lax.axis_index("section")
    batches, rows, width = tokens.shape
    per_peer = rows // peers
    shared = lax.all_gather(packet, BOTH, axis=0)
    low = own.astype(jnp.bfloat16)
    mats = lax.all_gather(low, BOTH, axis=0, tiled=True).reshape((2, peers) + own.shape)
    flat = shared.reshape(2, peers, -1)[:, :, : batches * rows]
    dealt = jnp.where(section == 0, flat[0], flat[1]).astype(jnp.int32).reshape(peers, batches, rows)
    own_rows = lax.axis_index("dp") * rows + jnp.arange(rows, dtype=jnp.int32)
    blocks = jnp.arange(peers, dtype=jnp.int32)
    picks = []
    sends = []
    for batch in range(batches):
        hit = dealt[:, batch][None, :, :] == own_rows[:, None, None]
        target = jnp.sum(jnp.where(hit, blocks[None, :, None], 0), axis=(1, 2))
        pick = one_hot(rank_of(target * rows + jnp.arange(rows, dtype=jnp.int32)))
        picks.append(pick.T)
        sends.append(nn(pick, tokens[batch]).astype(jnp.bfloat16))
    outgoing = jnp.stack(sends).reshape(2 * peers, per_peer, width)
    arrived = lax.all_to_all(outgoing, BOTH, split_axis=0, concat_axis=0, tiled=True)
    arrived = arrived.reshape(2, rows, width)
    place = one_hot(rank_of(jnp.where(section == 0, deal[0], deal[1])))
    x, cot = (tn(place, arrived[kind]).astype(jnp.bfloat16) for kind in range(2))
    return mats, shared, x, cot, jnp.stack(picks), place


def scatter_grads(terms, small, peers):
    if peers == 16:
        return rs(terms, small, PARTS, peers // 4)
    sections, _, rows, width = terms.shape
    terms = terms.reshape(sections * peers * rows, width)
    total = lax.psum_scatter(terms, BOTH, scatter_dimension=0, tiled=True).astype(jnp.float32)
    return total, lax.psum_scatter(small, BOTH, scatter_dimension=0, tiled=True)[0]


def local(entering, deal, seq_lens, mats, gains, biases):
    section = lax.axis_index("section")
    peers = lax.axis_size("dp")
    arrival = entering[0]
    batches, rows, width = arrival.shape
    per_peer = rows // peers
    per = 2 * width // peers
    vecs = jnp.concatenate([gains[0], biases[0]]).astype(jnp.bfloat16).astype(jnp.float32)
    packet = jnp.concatenate([deal.reshape(-1).astype(jnp.float32), vecs])
    packet = padded(packet[None])[0]
    packet = jnp.pad(packet, ((0, -packet.shape[0] % 8), (0, 0)))
    args = (mats[0], packet, deal.astype(jnp.float32), arrival)
    entered = enter(*args, PARTS, peers // 4) if peers == 16 else enter_plain(*args, peers)
    all_mats, shared, tokens, cotangent, returns, place = entered
    shared = shared.reshape(2, peers, -1)
    small = shared[:, :, batches * rows : batches * rows + 2 * per].reshape(2, peers, 2, per)
    small = jnp.swapaxes(small, 1, 2).reshape(2, 4, width)
    small = jnp.pad(small, ((0, 0), (0, 4), (0, 0)))
    all_mats = all_mats.reshape(2, 6 * width, width)
    lens = jnp.where(section == 0, seq_lens[0, 0], seq_lens[1, 0])
    ends = jnp.cumsum(lens)
    positions = jnp.arange(rows, dtype=jnp.int32)
    segment = jnp.sum((positions[:, None] >= ends[None, :]).astype(jnp.int32), axis=1)
    middle, *kept_low = forward_layer(0, all_mats, tokens, small[0], segment[:, None], segment[None])
    final, *kept_high = forward_layer(1, all_mats, middle, small[1], segment[:, None], segment[None])
    terms, down, vec_high = backward_layer(1, all_mats, middle, small[1], cotangent, kept_high, None)
    terms, down, vec_low = backward_layer(0, all_mats, tokens, small[0], down, kept_low, terms)
    terms = terms.reshape(2, peers, -1, width)
    vec_terms = jnp.stack([vec_low, vec_high])[:, :4].reshape(2, 2, peers, per)
    vec_terms = padded(jnp.swapaxes(vec_terms, 1, 2).reshape(2 * peers, 2 * per))
    shard_mats, vec_total = scatter_grads(terms, vec_terms, peers)
    vec_total = vec_total.reshape(-1)
    back = jnp.stack([nn(place, down), nn(place, final)]).astype(jnp.bfloat16)
    back = back.reshape(2 * peers, per_peer, width)
    returned = lax.all_to_all(back, BOTH, split_axis=0, concat_axis=0, tiled=True).reshape(2, rows, width)
    results = jnp.stack([nn(returns[batch], returned[batch]) for batch in range(batches)])
    return (
        results.astype(jnp.bfloat16)[None],
        shard_mats[None],
        vec_total[None, :per],
        vec_total[None, per : 2 * per],
    )


def solution(mesh):
    in_specs = (
        P("section", None, "dp", None),
        P(None, "dp"),
        P(None, "dp", None),
        P("section", "dp", None),
        P("section", "dp"),
        P("section", "dp"),
    )
    out_specs = (
        P("section", None, "dp", None),
        P("section", "dp", None),
        P("section", "dp"),
        P("section", "dp"),
    )
    return jax.shard_map(local, mesh=mesh, in_specs=in_specs, out_specs=out_specs, check_vma=False)
```

```python
import functools

import jax
import jax.numpy as jnp
from jax import lax
from jax.experimental import pallas as pl
from jax.experimental.pallas import tpu as pltpu
from jax.sharding import PartitionSpec as P

HEADS = 16
EPS = 1e-06
NEG = -1000000000.0
BOTH = ("section", "dp")
MESH = pl.DeviceIdType.MESH
PARTS = ((0, 112, "zxy"), (112, 112, "zyx"), (224, 128, "xzy"), (352, 128, "yzx"))


def greet(total, me, peers):
    barrier = pltpu.get_barrier_semaphore()

    def one(step, carry):
        other = lax.rem(me + step, total)
        pl.semaphore_signal(
            barrier, inc=1, device_id=(other // peers, lax.rem(other, peers)), device_id_type=MESH
        )
        return carry

    lax.fori_loop(1, total, one, 0)
    pl.semaphore_wait(barrier, total - 1)


def coords():
    s=lax.axis_index("section"); d=lax.axis_index("dp")
    return s,d,d//4,(d//2)%2,d%2

def items():
    out=[]
    for bx in (0,1):
        for by in (0,1):
            for dz in (0,-1,1,-2,2,-3,3):
                out.append((bx,by,dz))
    return out
def hops(it): return it[0]+it[1]+abs(it[2])
def arrival(order,it):
    diff={"x":it[0]!=0,"y":it[1]!=0,"z":it[2]!=0}
    last=None
    for k,dim in enumerate(order):
        if diff[dim]: last=k
    return last

def neighbours(s,d,z,y,c,zn):
    return [(None,(1-s,d)),(None,(s,(z*2+1-y)*2+c)),(None,(s,(z*2+y)*2+1-c)),(z>0,(s,d-4)),(z<zn-1,(s,d+4))]


def rs_kernel(parts,zn,g_ref,v_ref,o_ref,vo_ref,land,buf,obuf,vland,*rest):
    nP=len(parts)
    lks=rest[:nP]
    ssem,rsem,cs,cr,lsem,osem,vsend,vrecv=rest[nP:]
    s,d,z,y,c=coords()
    peers=4*zn
    total_dev=2*peers
    me=s*peers+d
    greet(total_dev,me,peers)
    vland[me]=v_ref[me]
    def small(step,carry):
        other=lax.rem(me+step,total_dev)
        pltpu.make_async_remote_copy(v_ref.at[other],vland.at[me],vsend,vrecv,device_id=(other//peers,lax.rem(other,peers)),device_id_type=MESH).start()
        return carry
    lax.fori_loop(1,total_dev,small,0)
    sib=(s,(z*2+y)*2+1-c)
    def where(it):
        s2=1-s if it[0] else s
        y2=1-y if it[1] else y
        return s2,z+it[2],y2
    def conds(it):
        cl=[]
        if it[2]<0: cl.append(z+it[2]>=0)
        if it[2]>0: cl.append(z+it[2]<=zn-1)
        return cl
    def guarded(cl,fn):
        if not cl: fn(); return
        e=cl[0]
        for q in cl[1:]: e=jnp.logical_and(e,q)
        pl.when(e)(fn)
    def slot_base(order):
        sizes={"x":2,"y":2,"z":zn}
        base={};cur=0
        for k,dim in enumerate(order):
            n=1
            for q in order[k+1:]: n*=sizes[q]
            if dim=="z": n*=2*zn
            base[dim]=cur; cur+=n
        return base,cur
    def slot(p,dim,side,dest):
        order=parts[p][2][::-1]
        base,_=slot_base(order)
        k=order.index(dim)
        v={"x":dest[0],"z":dest[1],"y":dest[2]}
        idx=0
        for q in order[k+1:]:
            idx=idx*(zn if q=="z" else 2)+v[q]
        if dim=="z": idx=(idx*zn+dest[1])*2+side
        return base[dim]+idx
    evs=[]
    for p in range(nP):
        for it in items():
            if abs(it[2])<=zn-1: evs.append((-hops(it),p,it))
    evs.sort(key=lambda e:e[0])
    seq=[(p,it) for _,p,it in evs]
    def core_dsc(p,it,mine):
        r0,rn,_=parts[p]
        s2,z2,y2=where(it)
        idx=(s2*zn+z2)*2+y2
        cc=c if mine else 1-c
        return pltpu.make_async_remote_copy(g_ref.at[s2,(z2*2+y2)*2+cc,pl.ds(r0,rn)],land.at[idx,pl.ds(r0,rn)],cs.at[p,idx],cr.at[p,idx],device_id=sib,device_id_type=MESH)
    for p,it in seq:
        guarded(conds(it),lambda p=p,it=it: core_dsc(p,it,False).start())
    def load(i):
        p,it=seq[i]
        r0,rn,_=parts[p]
        s2,z2,y2=where(it)
        return pltpu.make_async_copy(g_ref.at[s2,(z2*2+y2)*2+c,pl.ds(r0,rn)],buf.at[i%NB,pl.ds(0,rn)],lsem.at[i%NB])
    NB=buf.shape[0]
    for i in range(min(NB-1,len(seq))):
        guarded(conds(seq[i][1]),lambda i=i: load(i).start())
    def contribs(p,it):
        order=parts[p][2][::-1]
        diff={"x":it[0],"y":it[1],"z":it[2]}
        out=[];nxt=None
        for dim in order:
            if dim=="z":
                if it[2]==0: out+=[("z",0,z>0),("z",1,z<zn-1)]
                elif it[2]>0: out.append(("z",0,z>0))
                else: out.append(("z",1,z<zn-1))
                if it[2]!=0: nxt="r" if it[2]>0 else "l"; break
            else:
                if diff[dim]: nxt=dim; break
                out.append((dim,0,None))
        return out,nxt
    semoff=[0]
    for p in range(nP): semoff.append(semoff[-1]+slot_base(parts[p][2][::-1])[1])
    def out_dsc(p,it,nxt):
        r0,rn,_=parts[p]
        dest=where(it)
        s2,z2,y2=dest
        idx=(s2*zn+z2)*2+y2
        dim="z" if nxt in "lr" else nxt
        side=1 if nxt=="l" else 0
        sl=slot(p,dim,side,dest)
        dev={"x":(1-s,d),"y":(s,(z*2+1-y)*2+c),"l":(s,d-4),"r":(s,d+4)}[nxt]
        return pltpu.make_async_remote_copy(land.at[idx,pl.ds(r0,rn)],lks[p].at[sl],ssem.at[p,idx],rsem.at[semoff[p]+sl],device_id=dev,device_id_type=MESH)
    for i,(p,it) in enumerate(seq):
        r0,rn,_=parts[p]
        if i+NB-1<len(seq):
            guarded(conds(seq[i+NB-1][1]),lambda i=i: load(i+NB-1).start())
        def ev(i=i,p=p,it=it,r0=r0,rn=rn):
            dest=where(it)
            s2,z2,y2=dest
            idx=(s2*zn+z2)*2+y2
            con,nxt=contribs(p,it)
            lk=lks[p]
            load(i).wait()
            core_dsc(p,it,True).wait_recv()
            plain=[x for x in con if x[2] is None]
            cond=[x for x in con if x[2] is not None]
            def rdsc(dim,side):
                sl=slot(p,dim,side,dest)
                return pltpu.make_async_remote_copy(lk.at[sl],lk.at[sl],ssem.at[p,idx],rsem.at[semoff[p]+sl],device_id=sib,device_id_type=MESH),sl
            for dim,side,_ in plain: rdsc(dim,side)[0].wait_recv()
            for dim,side,cnd in cond:
                pl.when(cnd)(lambda dim=dim,side=side: rdsc(dim,side)[0].wait_recv())
            if not cond: variants=[(None,plain)]
            elif len(cond)==1:
                variants=[(cond[0][2],plain+cond),(jnp.logical_not(cond[0][2]),plain)]
            else:
                a,b=cond
                variants=[(jnp.logical_and(a[2],b[2]),plain+cond),(jnp.logical_and(a[2],jnp.logical_not(b[2])),plain+[a]),
                          (jnp.logical_and(jnp.logical_not(a[2]),b[2]),plain+[b])]
            def total(lst):
                slots=[slot(p,dim,side,dest) for dim,side,_ in lst]
                CH=16
                def body(k,_):
                    ro=pl.multiple_of(k*CH,CH)
                    acc=buf[i%NB,pl.ds(ro,CH),:].astype(jnp.float32)+land[idx,pl.ds(r0+ro,CH),:].astype(jnp.float32)
                    for sl in slots: acc=acc+lk[sl,pl.ds(ro,CH),:].astype(jnp.float32)
                    if nxt is None: obuf[pl.ds(r0+ro,CH),:]=acc
                    else: land[idx,pl.ds(r0+ro,CH),:]=acc.astype(jnp.bfloat16)
                    return 0
                lax.fori_loop(0,rn//CH,body,0)
            for cnd,lst in variants:
                if cnd is None: total(lst)
                else: pl.when(cnd)(lambda lst=lst: total(lst))
            if nxt is not None: out_dsc(p,it,nxt).start()
            else: pltpu.make_async_copy(obuf.at[pl.ds(r0,rn)],o_ref.at[pl.ds(r0,rn)],osem.at[p]).start()
        guarded(conds(it),ev)
    for p,it in seq:
        def fin(p=p,it=it):
            core_dsc(p,it,False).wait_send()
            nxt=contribs(p,it)[1]
            if nxt is not None: out_dsc(p,it,nxt).wait_send()
        guarded(conds(it),fin)
    for p,(r0,rn,_) in enumerate(parts):
        pltpu.make_async_copy(obuf.at[pl.ds(r0,rn)],o_ref.at[pl.ds(r0,rn)],osem.at[p]).wait()
    rest_of=vland.at[pl.ds(0,total_dev-1)]
    bulk=pltpu.make_async_remote_copy(rest_of,rest_of,vsend,vrecv,device_id=(0,0),device_id_type=MESH)
    bulk.wait_recv()
    bulk.wait_send()
    vo_ref[...]=jnp.sum(vland[...],axis=0)


def slot_count(order,zn):
    sizes={"x":2,"y":2,"z":zn};cur=0
    for k,dim in enumerate(order):
        n=1
        for q in order[k+1:]: n*=sizes[q]
        if dim=="z": n*=2*zn
        cur+=n
    return cur
def rs(g,v,parts,zn,cid=1,nb=4):
    n=len(parts)
    cnt=[slot_count(p[2][::-1],zn) for p in parts]
    mx=max(p[1] for p in parts)
    return pl.pallas_call(functools.partial(rs_kernel,parts,zn),
        out_shape=[jax.ShapeDtypeStruct((480,1280),jnp.float32),jax.ShapeDtypeStruct(v.shape[1:],jnp.float32)],
        in_specs=[pl.BlockSpec(memory_space=pl.ANY),pl.BlockSpec(memory_space=pltpu.VMEM)],
        out_specs=[pl.BlockSpec(memory_space=pl.ANY),pl.BlockSpec(memory_space=pltpu.VMEM)],
        scratch_shapes=[pltpu.VMEM((4*zn,480,1280),jnp.bfloat16),pltpu.VMEM((nb,mx,1280),jnp.bfloat16),pltpu.VMEM((480,1280),jnp.float32),pltpu.VMEM(v.shape,jnp.float32)]
          +[pltpu.VMEM((cnt[p],parts[p][1],1280),jnp.bfloat16) for p in range(n)]
          +[pltpu.SemaphoreType.DMA((n,4*zn)),pltpu.SemaphoreType.DMA((sum(cnt),)),
          pltpu.SemaphoreType.DMA((n,4*zn)),pltpu.SemaphoreType.DMA((n,4*zn)),pltpu.SemaphoreType.DMA((nb,)),pltpu.SemaphoreType.DMA((n,)),pltpu.SemaphoreType.DMA,pltpu.SemaphoreType.DMA],
        compiler_params=pltpu.CompilerParams(collective_id=cid,has_side_effects=True,vmem_limit_bytes=62*2**20))(g,v)


WIN = 256
QB = 128
GROUP = 4
LOG2E = 1.4426950408889634
LN2 = 0.6931471805599453
GC = 0.7978845608028654
GA = 0.044715
VMEM_LIMIT = 62 * 2**20


def nn(left, right):
    return jnp.dot(left, right, preferred_element_type=jnp.float32)


def nt(left, right):
    return lax.dot_general(
        left, right, (((1,), (1,)), ((), ())), preferred_element_type=jnp.float32
    )


def tn(left, right):
    return lax.dot_general(
        left, right, (((0,), (0,)), ((), ())), preferred_element_type=jnp.float32
    )


def head_window(head, depth, width):
    start = jnp.minimum((head * depth) // 128, (width - WIN) // 128) * 128
    start = pl.multiple_of(start, 128)
    lane = lax.broadcasted_iota(jnp.int32, (1, WIN), 1) + (start - head * depth)
    return start, (lane >= 0) & (lane < depth)


def norm_rows(value, gain):
    return value * lax.rsqrt(jnp.mean(value * value, axis=-1, keepdims=True) + EPS) * gain


def norm_back(value, gain, down):
    inv = lax.rsqrt(jnp.mean(value * value, axis=-1, keepdims=True) + EPS)
    unit = value * inv
    scaled = down * gain
    lean = jnp.mean(scaled * unit, axis=-1, keepdims=True)
    return inv * (scaled - unit * lean), jnp.sum(down * unit, axis=0, keepdims=True)


def forward_kernel(
    layer, mats_ref, x_ref, vec_ref, segc_ref, segr_ref,
    y_ref, qkv_out, prob_out, att_out, mid_out, u_out,
    held, qkv, prob, att, mid, u, norm, mask, sems, out_sems,
):
    rows, width = x_ref.shape
    depth = width // HEADS
    scale = depth ** (-0.5)

    def weight(index):
        return pltpu.make_async_copy(
            mats_ref.at[layer, pl.ds(index * width, width)], held.at[index], sems.at[index]
        )

    keeps = [
        pltpu.make_async_copy(src, dst, out_sems.at[index])
        for index, (src, dst) in enumerate(
            ((qkv, qkv_out), (prob, prob_out), (att, att_out), (mid, mid_out), (u, u_out))
        )
    ]
    for index in range(6):
        weight(index).start()
    tiles = [slice(c, c + WIN) for c in range(0, width, WIN)]
    norm[...] = norm_rows(x_ref[...].astype(jnp.float32), vec_ref[0:1, :]).astype(jnp.bfloat16)
    qi = lax.broadcasted_iota(jnp.int32, (rows, rows), 0)
    ki = lax.broadcasted_iota(jnp.int32, (rows, rows), 1)
    mask[...] = jnp.where((segc_ref[...] == segr_ref[...]) & (ki <= qi), 3e38, NEG)
    for index in range(3):
        weight(index).wait()
        for cols in tiles:
            part = nn(norm[...], held[index, :, cols])
            if index == 0:
                part = part * (scale * LOG2E)
            qkv[index, :, cols] = part.astype(jnp.bfloat16)
    keeps[0].start()
    att[...] = jnp.zeros_like(att)

    def head_group(group, carry):
        blocks = range(rows // QB)
        heres = [slice(block * QB, (block + 1) * QB) for block in blocks]
        uptos = [slice(0, (block + 1) * QB) for block in blocks]
        work = []
        for k in range(GROUP):
            head = group * GROUP + k
            start, lanes = head_window(head, depth, width)
            work += [(head, pl.ds(start, WIN), lanes, heres[b], uptos[b]) for b in blocks]
        scores = [nt(jnp.where(lanes, qkv[0, here, cols], 0), qkv[1, upto, cols]) for head, cols, lanes, here, upto in work]
        scores = [jnp.minimum(score, mask[w[3], w[4]]) for score, w in zip(scores, work)]
        tops = [jnp.max(score, axis=-1, keepdims=True) for score in scores]
        expds = [jnp.exp2(score - top) for score, top in zip(scores, tops)]
        sums = [1.0 / jnp.sum(e, axis=-1, keepdims=True) for e in expds]
        softs = [(e * r).astype(jnp.bfloat16) for e, r in zip(expds, sums)]
        for soft, (head, cols, lanes, here, upto) in zip(softs, work):
            prob[head, here, upto] = soft
        mixes = [nn(soft, qkv[2, w[4], w[1]]).astype(jnp.bfloat16) for soft, w in zip(softs, work)]
        for mixed, (head, cols, lanes, here, upto) in zip(mixes, work):
            att[here, cols] = jnp.where(lanes, mixed, att[here, cols])
        return carry

    lax.fori_loop(0, HEADS // GROUP, head_group, 0)
    keeps[1].start()
    keeps[2].start()
    weight(3).wait()
    for cols in tiles:
        mid[:, cols] = x_ref[:, cols].astype(jnp.float32) + nn(att[...], held[3, :, cols])
    keeps[3].start()
    norm[...] = norm_rows(mid[...], vec_ref[1:2, :]).astype(jnp.bfloat16)
    weight(4).wait()
    for cols in tiles:
        u[:, cols] = nn(norm[...], held[4, :, cols]) + vec_ref[2:3, cols]
    keeps[4].start()
    for cols in tiles:
        pre = u[:, cols]
        act = 0.5 * pre * (1.0 + jnp.tanh(GC * (pre + GA * (pre * pre * pre))))
        norm[:, cols] = act.astype(jnp.bfloat16)
    weight(5).wait()
    for cols in tiles:
        out = mid[:, cols] + (nn(norm[...], held[5, :, cols]) + vec_ref[3:4, cols])
        y_ref[:, cols] = out.astype(jnp.bfloat16)
    for keep in keeps:
        keep.wait()


def forward_layer(layer, mats, x, vec, segc, segr):
    rows, width = x.shape
    f32, b16 = jnp.float32, jnp.bfloat16
    vm = pl.BlockSpec(memory_space=pltpu.VMEM)
    hbm = pl.BlockSpec(memory_space=pl.ANY)
    kept = [
        ((3, rows, width), b16), ((HEADS, rows, rows), b16), ((rows, width), b16),
        ((rows, width), f32), ((rows, width), f32),
    ]
    return pl.pallas_call(
        functools.partial(forward_kernel, layer),
        out_shape=[jax.ShapeDtypeStruct((rows, width), b16)]
        + [jax.ShapeDtypeStruct(shape, dtype) for shape, dtype in kept],
        in_specs=[hbm, vm, vm, vm, vm],
        out_specs=[vm] + [hbm] * 5,
        scratch_shapes=[pltpu.VMEM((6, width, width), b16)]
        + [pltpu.VMEM(shape, dtype) for shape, dtype in kept]
        + [
            pltpu.VMEM((rows, width), b16),
            pltpu.VMEM((rows, rows), f32),
            pltpu.SemaphoreType.DMA((6,)),
            pltpu.SemaphoreType.DMA((5,)),
        ],
        compiler_params=pltpu.CompilerParams(vmem_limit_bytes=VMEM_LIMIT),
        name="layer_forward",
    )(mats, x, vec, segc, segr)


def backward_kernel(layer, aliased, *refs):
    mats_ref, x_ref, vec_ref, dy_ref, qkv_in, prob_in, att_in, mid_in, u_in = refs[:9]
    rest = refs[10:] if aliased else refs[9:]
    (
        grads_ref, dx_ref, dvec_ref,
        held, qkv, prob, att, mid, u, act, low, wide, dmid, dqkv, dscore, turned, stage,
        sems, in_sems, out_sems,
    ) = rest
    rows, width = x_ref.shape
    depth = width // HEADS
    scale = depth ** (-0.5)
    f32, b16 = jnp.float32, jnp.bfloat16
    tiles = [slice(c, c + WIN) for c in range(0, width, WIN)]

    def weight(index):
        return pltpu.make_async_copy(
            mats_ref.at[layer, pl.ds(index * width, width)], held.at[index], sems.at[index]
        )

    loads = [
        pltpu.make_async_copy(src, dst, in_sems.at[index])
        for index, (src, dst) in enumerate(
            ((qkv_in, qkv), (prob_in, prob), (att_in, att), (mid_in, mid), (u_in, u))
        )
    ]
    loads[4].start()
    weight(5).start()
    weight(4).start()
    loads[3].start()
    weight(3).start()
    loads[2].start()
    loads[0].start()
    loads[1].start()
    for index in range(3):
        weight(index).start()

    def put(index, slot):
        return pltpu.make_async_copy(
            stage.at[slot], grads_ref.at[layer, pl.ds(index * width, width)], out_sems.at[index]
        )

    slots = {5: 0, 4: 1, 3: 0, 2: 1, 1: 0, 0: 1}
    before = {3: 5, 2: 4, 1: 3, 0: 2}

    def weight_grad(index, left_t, right):
        slot = slots[index]
        if index in before:
            put(before[index], slot).wait()
        for cols in tiles:
            stage[slot, cols, :] = nn(left_t(cols), right).astype(b16)
        put(index, slot).start()

    dvec_ref[3:4, :] = jnp.sum(dy_ref[...].astype(f32), axis=0, keepdims=True)
    loads[4].wait()
    weight(5).wait()
    for cols in tiles:
        pre = u[:, cols]
        square = pre * pre
        bent = jnp.tanh(GC * (pre + GA * (square * pre)))
        half = 0.5 * (1.0 + bent)
        act[:, cols] = (pre * half).astype(b16)
        slope = half + (0.5 * GC) * pre * (1.0 - bent * bent) * (1.0 + (3.0 * GA) * square)
        down = nt(dy_ref[...], held[5, cols, :]) * slope
        down = down.astype(b16)
        low[:, cols] = down
        dvec_ref[2:3, cols] = jnp.sum(down.astype(f32), axis=0, keepdims=True)
    weight_grad(5, lambda cols: act[:, cols].T, dy_ref[...])
    weight(4).wait()
    for cols in tiles:
        wide[:, cols] = nt(low[...], held[4, cols, :])
    loads[3].wait()
    act[...] = norm_rows(mid[...], vec_ref[1:2, :]).astype(b16)
    weight_grad(4, lambda cols: act[:, cols].T, low[...])
    part, gain_sum = norm_back(mid[...], vec_ref[1:2, :], wide[...])
    dvec_ref[1:2, :] = gain_sum
    total = dy_ref[...].astype(f32) + part
    dmid[...] = total
    low[...] = total.astype(b16)
    loads[2].wait()
    weight_grad(3, lambda cols: att[:, cols].T, low[...])
    weight(3).wait()
    for cols in tiles:
        act[:, cols] = nt(low[...], held[3, cols, :]).astype(b16)
    loads[0].wait()
    loads[1].wait()
    dqkv[...] = jnp.zeros_like(dqkv)

    def head_group(group, carry):
        blocks = range(rows // QB)
        heres = [slice(block * QB, (block + 1) * QB) for block in blocks]
        uptos = [slice(0, (block + 1) * QB) for block in blocks]
        sinces = [slice(block * QB, rows) for block in blocks]
        work = []
        for k in range(GROUP):
            head = group * GROUP + k
            start, lanes = head_window(head, depth, width)
            work += [(head, pl.ds(start, WIN), lanes, heres[b], uptos[b], sinces[b], k) for b in blocks]
        dprobs = [nt(jnp.where(w[2], act[w[3], w[1]], 0), qkv[2, w[4], w[1]]) for w in work]
        softs = [prob[w[0], w[3], w[4]].astype(f32) for w in work]
        leans = [jnp.sum(dp * soft, axis=-1, keepdims=True) for dp, soft in zip(dprobs, softs)]
        dss = [(soft * (dp - lean)).astype(b16) for dp, soft, lean in zip(dprobs, softs, leans)]
        for ds, w in zip(dss, work):
            dscore[w[6], w[3], w[4]] = ds
        dvs = [tn(prob[w[0], w[5], w[3]], act[w[5], w[1]]).astype(b16) for w in work]
        dqs = [(nn(ds, qkv[1, w[4], w[1]]) * scale).astype(b16) for ds, w in zip(dss, work)]
        dks = [(tn(dscore[w[6], w[5], w[3]], qkv[0, w[5], w[1]]) * LN2).astype(b16) for w in work]
        for dq, dk, dv, w in zip(dqs, dks, dvs, work):
            for index, value in enumerate((dq, dk, dv)):
                dqkv[index, w[3], w[1]] = jnp.where(w[2], value, dqkv[index, w[3], w[1]])
        return carry

    lax.fori_loop(0, HEADS // GROUP, head_group, 0)
    low[...] = norm_rows(x_ref[...].astype(f32), vec_ref[0:1, :]).astype(b16)
    for cols in tiles:
        turned[cols, :] = low[:, cols].T
    for index in (2, 1, 0):
        weight_grad(index, lambda cols: turned[cols, :], dqkv[index])
    for index in range(3):
        weight(index).wait()
    for cols in tiles:
        wide[:, cols] = (
            nt(dqkv[0], held[0, cols, :]) + nt(dqkv[1], held[1, cols, :]) + nt(dqkv[2], held[2, cols, :])
        )
    part, gain_sum = norm_back(x_ref[...].astype(f32), vec_ref[0:1, :], wide[...])
    dvec_ref[0:1, :] = gain_sum
    dvec_ref[4:8, :] = jnp.zeros_like(dvec_ref[4:8, :])
    dx_ref[...] = (dmid[...] + part).astype(b16)
    put(1, 0).wait()
    put(0, 1).wait()


def backward_layer(layer, mats, x, vec, dy, kept, grads):
    rows, width = x.shape
    f32, b16 = jnp.float32, jnp.bfloat16
    vm = pl.BlockSpec(memory_space=pltpu.VMEM)
    hbm = pl.BlockSpec(memory_space=pl.ANY)
    aliased = grads is not None
    return pl.pallas_call(
        functools.partial(backward_kernel, layer, aliased),
        out_shape=[
            jax.ShapeDtypeStruct(mats.shape, b16),
            jax.ShapeDtypeStruct((rows, width), b16),
            jax.ShapeDtypeStruct((8, width), f32),
        ],
        in_specs=[hbm, vm, vm, vm] + [hbm] * 5 + ([hbm] if aliased else []),
        out_specs=[hbm, vm, vm],
        scratch_shapes=[
            pltpu.VMEM((6, width, width), b16),
            pltpu.VMEM((3, rows, width), b16),
            pltpu.VMEM((HEADS, rows, rows), b16),
            pltpu.VMEM((rows, width), b16),
            pltpu.VMEM((rows, width), f32),
            pltpu.VMEM((rows, width), f32),
            pltpu.VMEM((rows, width), b16),
            pltpu.VMEM((rows, width), b16),
            pltpu.VMEM((rows, width), f32),
            pltpu.VMEM((rows, width), f32),
            pltpu.VMEM((3, rows, width), b16),
            pltpu.VMEM((GROUP, rows, rows), b16),
            pltpu.VMEM((width, rows), b16),
            pltpu.VMEM((2, width, width), b16),
            pltpu.SemaphoreType.DMA((6,)),
            pltpu.SemaphoreType.DMA((5,)),
            pltpu.SemaphoreType.DMA((6,)),
        ],
        input_output_aliases={9: 0} if aliased else {},
        compiler_params=pltpu.CompilerParams(vmem_limit_bytes=VMEM_LIMIT),
        name="layer_backward",
    )(*((mats, x, vec, dy) + tuple(kept) + ((grads,) if aliased else ())))


def as_row(column):
    rows = column.shape[0]
    return jnp.broadcast_to(column, (rows, 128)).T[0:1, :]


def as_column(row):
    size = row.shape[1]
    return jnp.broadcast_to(row, (128, size)).T[:, 0:1]


def ones_where(flag):
    return jnp.where(flag, 1.0, 0.0)


def gather_events(parts,zn,place,own,w_ref,ssem,rsem,cs,cr):
    s,d,z,y,c=place
    KIND={"x":0,"y":1,"l":2,"r":3}
    def where(it):
        s2=1-s if it[0] else s
        y2=1-y if it[1] else y
        z2=z+it[2]
        return s2,z2,y2
    def dsc(p,it,kind):
        r0,rn,order=parts[p]
        s2,z2,y2=where(it)
        idx=s2*(2*zn)+z2*2+y2
        is_own=it==(0,0,0)
        src=own.at[pl.ds(r0,rn)] if is_own else w_ref.at[s2,(z2*2+y2)*2+c,pl.ds(r0,rn)]
        dst=w_ref.at[s2,(z2*2+y2)*2+c,pl.ds(r0,rn)]
        if kind=="core":
            dev=(s,(z*2+y)*2+1-c)
            return pltpu.make_async_remote_copy(src,dst,cs.at[p,idx],cr.at[p,idx],device_id=dev,device_id_type=MESH)
        dev={"x":(1-s,d),"y":(s,(z*2+1-y)*2+c),"l":(s,d-4),"r":(s,d+4)}[kind]
        return pltpu.make_async_remote_copy(src,dst,ssem.at[KIND[kind],p,idx],rsem.at[p,idx],device_id=dev,device_id_type=MESH)
    def cdsc(p,it):
        r0,rn,order=parts[p]
        s2,z2,y2=where(it)
        idx=s2*(2*zn)+z2*2+y2
        dst=w_ref.at[s2,(z2*2+y2)*2+1-c,pl.ds(r0,rn)]
        return pltpu.make_async_remote_copy(dst,dst,cs.at[p,idx],cr.at[p,idx],device_id=(s,(z*2+y)*2+1-c),device_id_type=MESH)
    def conds(it,kind):
        cs_=[]
        if it[2]<0: cs_.append(z+it[2]>=0)
        if it[2]>0: cs_.append(z+it[2]<=zn-1)
        if kind=="l": cs_.append(z>0)
        if kind=="r": cs_.append(z<zn-1)
        return cs_
    def guarded(cl,fn):
        if not cl: fn(); return
        e=cl[0]
        for q in cl[1:]: e=jnp.logical_and(e,q)
        pl.when(e)(fn)
    def sends(p,it):
        order=parts[p][2]
        a=arrival(order,it)
        ks=[]
        if a is not None and order[a]=="z": ks.append("l" if it[2]>0 else "r")
        for dim in order[(a+1) if a is not None else 0:]:
            ks += ["r","l"] if dim=="z" else [dim]
        ks.append("core")
        return ks
    evs=[]
    for p in range(len(parts)):
        for it in items():
            if abs(it[2])<zn: evs.append((hops(it),p,it))
    evs.sort(key=lambda e:e[0])
    first=[]
    later=[]
    for h,p,it in evs:
        def ev(p=p,it=it):
            if it!=(0,0,0): dsc(p,it,"x").wait_recv()
            for k in sends(p,it):
                guarded(conds((0,0,0),k), lambda k=k: dsc(p,it,k).start())
        (later if h else first).append(lambda it=it,ev=ev: guarded(conds(it,None),ev))
    def finish():
        for _,p,it in evs:
            def fin(p=p,it=it):
                cdsc(p,it).wait_recv()
                for k in sends(p,it):
                    guarded(conds((0,0,0),k), lambda k=k: dsc(p,it,k).wait_send())
            guarded(conds(it,None),fin)
    return first,later,finish


def enter_kernel(
    parts, zn, mats_ref, packet_ref, deal_ref, tokens_ref,
    w_ref, shared_ref, x_ref, cot_ref, picks_ref, place_ref,
    own, wide_rows, strips32, sendbuf, landed, order,
    own_sem, lsem, ssem, rsem, cs, cr, psend, precv, tsend, trecv,
):
    s, d, z, y, c = coords()
    peers = 4 * zn
    total = 2 * peers
    me = s * peers + d
    batches, rows, width = tokens_ref.shape
    per_peer = rows // peers
    strips = width // 128
    f32, b16 = jnp.float32, jnp.bfloat16
    cast_in = pltpu.make_async_copy(mats_ref, wide_rows, own_sem)
    cast_in.start()
    greet(total, me, peers)
    shared_ref[me] = packet_ref[...]

    def tell(step, carry):
        other = lax.rem(me + step, total)
        pltpu.make_async_remote_copy(
            packet_ref, shared_ref.at[me], psend, precv,
            device_id=(other // peers, lax.rem(other, peers)), device_id_type=MESH,
        ).start()
        return carry

    lax.fori_loop(1, total, tell, 0)
    cast_in.wait()
    own[...] = wide_rows[...].astype(b16)
    lc = pltpu.make_async_copy(own, w_ref.at[s, d], lsem)
    lc.start()
    start_events, rest_events, finish = gather_events(
        parts, zn, (s, d, z, y, c), own, w_ref, ssem, rsem, cs, cr
    )
    for event in start_events:
        event()
    sub = lax.broadcasted_iota(jnp.int32, (rows, rows), 0).astype(f32)
    lane = lax.broadcasted_iota(jnp.int32, (rows, rows), 1).astype(f32)
    mine_row = jnp.where(s == 0, deal_ref[0:1, :], deal_ref[1:2, :])
    mine_col = as_column(mine_row)
    rank_col = jnp.sum(ones_where(mine_row < mine_col), axis=1, keepdims=True)
    order[...] = ones_where(lane == rank_col).astype(b16)
    rank_row = jnp.sum(ones_where(mine_col < mine_row), axis=0, keepdims=True)
    place_ref[...] = ones_where(sub == rank_row).astype(b16)
    rest = shared_ref.at[pl.ds(0, total - 1)]
    bulk = pltpu.make_async_remote_copy(
        rest, rest, psend, precv, device_id=(0, 0), device_id_type=MESH
    )
    bulk.wait_recv()
    index_col = lax.broadcasted_iota(jnp.int32, (rows, 1), 0).astype(f32)
    ids_col = index_col + (d * rows).astype(f32)
    for batch in range(batches):

        def look(block, found):
            known = shared_ref[s * peers + block]
            for line in range(rows // 128):
                at = batch * (rows // 128) + line
                found = jnp.where(ids_col == known[at : at + 1, :], block.astype(f32), found)
            return found

        found = lax.fori_loop(0, peers, look, jnp.zeros((rows, 128), f32))
        key_col = jnp.sum(found, axis=1, keepdims=True) * rows + index_col
        key_row = as_row(key_col)
        rank_row = jnp.sum(ones_where(key_col < key_row), axis=0, keepdims=True)
        rank_col = jnp.sum(ones_where(key_row < key_col), axis=1, keepdims=True)
        picks_ref[batch] = ones_where(lane == rank_col).astype(b16)
        pick = ones_where(sub == rank_row).astype(b16)
        for strip in range(strips):
            part = nn(pick, tokens_ref[batch, :, strip * 128 : (strip + 1) * 128])
            strips32[:, strip * per_peer : (strip + 1) * per_peer, :] = part.reshape(peers, per_peer, 128)
        sendbuf[batch] = strips32[...].astype(b16)

    landed[me] = sendbuf[s, d]

    def give(step, carry):
        other = lax.rem(me + step, total)
        sec, dp = other // peers, lax.rem(other, peers)
        pltpu.make_async_remote_copy(
            sendbuf.at[sec, dp], landed.at[me], tsend, trecv.at[s],
            device_id=(sec, dp), device_id_type=MESH,
        ).start()
        return carry

    lax.fori_loop(1, total, give, 0)
    for event in rest_events:
        event()

    def take(kind, out_ref):
        def wait(count):
            some = landed.at[pl.ds(0, count)]
            pltpu.make_async_remote_copy(
                some, some, tsend, trecv.at[kind], device_id=(0, 0), device_id_type=MESH
            ).wait_recv()

        pl.when(s == kind)(lambda: wait(peers - 1))
        pl.when(s != kind)(lambda: wait(peers))
        strips32[...] = landed[pl.ds(kind * peers, peers)].astype(f32)
        for strip in range(strips):
            part = strips32[:, strip * per_peer : (strip + 1) * per_peer, :].reshape(rows, 128)
            out_ref[:, strip * 128 : (strip + 1) * 128] = nn(order[...], part.astype(b16)).astype(b16)

    take(0, x_ref)
    take(1, cot_ref)
    finish()
    lc.wait()
    bulk.wait_send()
    most = landed.at[pl.ds(0, total - 1)]
    pltpu.make_async_remote_copy(
        most, most, tsend, trecv.at[0], device_id=(0, 0), device_id_type=MESH
    ).wait_send()


def enter(mats, packet, deal, tokens, parts, zn):
    n = len(parts)
    peers = 4 * zn
    batches, rows, width = tokens.shape
    strip_rows = rows // peers * (width // 128)
    f32, b16 = jnp.float32, jnp.bfloat16
    vm = pl.BlockSpec(memory_space=pltpu.VMEM)
    hbm = pl.BlockSpec(memory_space=pl.ANY)
    dma = pltpu.SemaphoreType.DMA
    return pl.pallas_call(
        functools.partial(enter_kernel, parts, zn),
        out_shape=[
            jax.ShapeDtypeStruct((2, peers) + mats.shape, b16),
            jax.ShapeDtypeStruct((2 * peers,) + packet.shape, f32),
            jax.ShapeDtypeStruct((rows, width), b16),
            jax.ShapeDtypeStruct((rows, width), b16),
            jax.ShapeDtypeStruct((batches, rows, rows), b16),
            jax.ShapeDtypeStruct((rows, rows), b16),
        ],
        in_specs=[hbm, vm, vm, vm],
        out_specs=[hbm, vm, vm, vm, vm, vm],
        scratch_shapes=[
            pltpu.VMEM(mats.shape, b16),
            pltpu.VMEM(mats.shape, f32),
            pltpu.VMEM((peers, strip_rows, 128), f32),
            pltpu.VMEM((batches, peers, strip_rows, 128), b16),
            pltpu.VMEM((2 * peers, strip_rows, 128), b16),
            pltpu.VMEM((rows, rows), b16),
            dma, dma, dma((4, n, peers)), dma((n, peers)), dma((n, peers)), dma((n, peers)),
            dma, dma, dma, dma((2,)),
        ],
        compiler_params=pltpu.CompilerParams(
            collective_id=0, has_side_effects=True, vmem_limit_bytes=VMEM_LIMIT
        ),
        name="enter",
    )(mats, packet, deal, tokens)


def one_hot(rank):
    rows = rank.shape[0]
    return (rank[None, :] == jnp.arange(rows, dtype=jnp.int32)[:, None]).astype(jnp.bfloat16)


def rank_of(key):
    return jnp.sum((key[None, :] < key[:, None]).astype(jnp.int32), axis=1)


def padded(flat):
    lead, size = flat.shape
    full = -(-size // 1024) * 1024
    return jnp.pad(flat, ((0, 0), (0, full - size))).reshape(lead, full // 128, 128)


def enter_plain(own, packet, deal, tokens, peers):
    section = lax.axis_index("section")
    batches, rows, width = tokens.shape
    per_peer = rows // peers
    shared = lax.all_gather(packet, BOTH, axis=0)
    low = own.astype(jnp.bfloat16)
    mats = lax.all_gather(low, BOTH, axis=0, tiled=True).reshape((2, peers) + own.shape)
    flat = shared.reshape(2, peers, -1)[:, :, : batches * rows]
    dealt = jnp.where(section == 0, flat[0], flat[1]).astype(jnp.int32).reshape(peers, batches, rows)
    own_rows = lax.axis_index("dp") * rows + jnp.arange(rows, dtype=jnp.int32)
    blocks = jnp.arange(peers, dtype=jnp.int32)
    picks = []
    sends = []
    for batch in range(batches):
        hit = dealt[:, batch][None, :, :] == own_rows[:, None, None]
        target = jnp.sum(jnp.where(hit, blocks[None, :, None], 0), axis=(1, 2))
        pick = one_hot(rank_of(target * rows + jnp.arange(rows, dtype=jnp.int32)))
        picks.append(pick.T)
        sends.append(nn(pick, tokens[batch]).astype(jnp.bfloat16))
    outgoing = jnp.stack(sends).reshape(2 * peers, per_peer, width)
    arrived = lax.all_to_all(outgoing, BOTH, split_axis=0, concat_axis=0, tiled=True)
    arrived = arrived.reshape(2, rows, width)
    place = one_hot(rank_of(jnp.where(section == 0, deal[0], deal[1])))
    x, cot = (tn(place, arrived[kind]).astype(jnp.bfloat16) for kind in range(2))
    return mats, shared, x, cot, jnp.stack(picks), place


def scatter_grads(terms, small, peers):
    if peers == 16:
        return rs(terms, small, PARTS, peers // 4)
    sections, _, rows, width = terms.shape
    terms = terms.reshape(sections * peers * rows, width)
    total = lax.psum_scatter(terms, BOTH, scatter_dimension=0, tiled=True).astype(jnp.float32)
    return total, lax.psum_scatter(small, BOTH, scatter_dimension=0, tiled=True)[0]


def local(entering, deal, seq_lens, mats, gains, biases):
    section = lax.axis_index("section")
    peers = lax.axis_size("dp")
    arrival = entering[0]
    batches, rows, width = arrival.shape
    per_peer = rows // peers
    per = 2 * width // peers
    vecs = jnp.concatenate([gains[0], biases[0]]).astype(jnp.bfloat16).astype(jnp.float32)
    packet = jnp.concatenate([deal.reshape(-1).astype(jnp.float32), vecs])
    packet = padded(packet[None])[0]
    packet = jnp.pad(packet, ((0, -packet.shape[0] % 8), (0, 0)))
    args = (mats[0], packet, deal.astype(jnp.float32), arrival)
    entered = enter(*args, PARTS, peers // 4) if peers == 16 else enter_plain(*args, peers)
    all_mats, shared, tokens, cotangent, returns, place = entered
    shared = shared.reshape(2, peers, -1)
    small = shared[:, :, batches * rows : batches * rows + 2 * per].reshape(2, peers, 2, per)
    small = jnp.swapaxes(small, 1, 2).reshape(2, 4, width)
    small = jnp.pad(small, ((0, 0), (0, 4), (0, 0)))
    all_mats = all_mats.reshape(2, 6 * width, width)
    lens = jnp.where(section == 0, seq_lens[0, 0], seq_lens[1, 0])
    ends = jnp.cumsum(lens)
    positions = jnp.arange(rows, dtype=jnp.int32)
    segment = jnp.sum((positions[:, None] >= ends[None, :]).astype(jnp.int32), axis=1)
    middle, *kept_low = forward_layer(0, all_mats, tokens, small[0], segment[:, None], segment[None])
    final, *kept_high = forward_layer(1, all_mats, middle, small[1], segment[:, None], segment[None])
    terms, down, vec_high = backward_layer(1, all_mats, middle, small[1], cotangent, kept_high, None)
    terms, down, vec_low = backward_layer(0, all_mats, tokens, small[0], down, kept_low, terms)
    terms = terms.reshape(2, peers, -1, width)
    vec_terms = jnp.stack([vec_low, vec_high])[:, :4].reshape(2, 2, peers, per)
    vec_terms = padded(jnp.swapaxes(vec_terms, 1, 2).reshape(2 * peers, 2 * per))
    shard_mats, vec_total = scatter_grads(terms, vec_terms, peers)
    vec_total = vec_total.reshape(-1)
    back = jnp.stack([nn(place, down), nn(place, final)]).astype(jnp.bfloat16)
    back = back.reshape(2 * peers, per_peer, width)
    returned = lax.all_to_all(back, BOTH, split_axis=0, concat_axis=0, tiled=True).reshape(2, rows, width)
    results = jnp.stack([nn(returns[batch], returned[batch]) for batch in range(batches)])
    return (
        results.astype(jnp.bfloat16)[None],
        shard_mats[None],
        vec_total[None, :per],
        vec_total[None, per : 2 * per],
    )


def solution(mesh):
    in_specs = (
        P("section", None, "dp", None),
        P(None, "dp"),
        P(None, "dp", None),
        P("section", "dp", None),
        P("section", "dp"),
        P("section", "dp"),
    )
    out_specs = (
        P("section", None, "dp", None),
        P("section", "dp", None),
        P("section", "dp"),
        P("section", "dp"),
    )
    return jax.shard_map(local, mesh=mesh, in_specs=in_specs, out_specs=out_specs, check_vma=False)
```

```python
import functools

import jax
import jax.numpy as jnp
from jax import lax
from jax.experimental import pallas as pl
from jax.experimental.pallas import tpu as pltpu
from jax.sharding import PartitionSpec as P

HEADS = 16
EPS = 1e-06
NEG = -1000000000.0
BOTH = ("section", "dp")
MESH = pl.DeviceIdType.MESH
PARTS = ((0, 112, "zxy"), (112, 112, "zyx"), (224, 128, "xzy"), (352, 128, "yzx"))


WIN = 256
QB = 128
GROUP = 4
LOG2E = 1.4426950408889634
LN2 = 0.6931471805599453
GC = 0.7978845608028654
GA = 0.044715
VMEM_LIMIT = 62 * 2**20


def nn(left, right):
    return jnp.dot(left, right, preferred_element_type=jnp.float32)


def nt(left, right):
    return lax.dot_general(
        left, right, (((1,), (1,)), ((), ())), preferred_element_type=jnp.float32
    )


def tn(left, right):
    return lax.dot_general(
        left, right, (((0,), (0,)), ((), ())), preferred_element_type=jnp.float32
    )


def head_window(head, depth, width):
    start = jnp.minimum((head * depth) // 128, (width - WIN) // 128) * 128
    start = pl.multiple_of(start, 128)
    lane = lax.broadcasted_iota(jnp.int32, (1, WIN), 1) + (start - head * depth)
    return start, (lane >= 0) & (lane < depth)


def norm_rows(value, gain):
    return value * lax.rsqrt(jnp.mean(value * value, axis=-1, keepdims=True) + EPS) * gain


def norm_back(value, gain, down):
    inv = lax.rsqrt(jnp.mean(value * value, axis=-1, keepdims=True) + EPS)
    unit = value * inv
    scaled = down * gain
    lean = jnp.mean(scaled * unit, axis=-1, keepdims=True)
    return inv * (scaled - unit * lean), jnp.sum(down * unit, axis=0, keepdims=True)


def signal_all(total, me, peers):
    barrier = pltpu.get_barrier_semaphore()

    def one(step, carry):
        other = lax.rem(me + step, total)
        pl.semaphore_signal(
            barrier, inc=1, device_id=(other // peers, lax.rem(other, peers)), device_id_type=MESH
        )
        return carry

    lax.fori_loop(1, total, one, 0)


def wait_all(total):
    pl.semaphore_wait(pltpu.get_barrier_semaphore(), total - 1)


def greet(total, me, peers):
    signal_all(total, me, peers)
    wait_all(total)


def cut_strips(pick, source, strips32):
    peers = strips32.shape[0]
    strips = source.shape[-1] // 128
    each = strips32.shape[1] // strips
    for strip in range(strips):
        part = nn(pick, source[:, strip * 128 : (strip + 1) * 128])
        strips32[:, strip * each : (strip + 1) * each, :] = part.reshape(peers, each, 128)


def join_strips(order, strips32, out_ref):
    peers = strips32.shape[0]
    strips = out_ref.shape[-1] // 128
    each = strips32.shape[1] // strips
    for strip in range(strips):
        part = strips32[:, strip * each : (strip + 1) * each, :].reshape(peers * each, 128)
        part = nn(order, part.astype(jnp.bfloat16)).astype(jnp.bfloat16)
        out_ref[:, strip * 128 : (strip + 1) * 128] = part


def bulk_copy(ref, count, send_sem, recv_sem):
    some = ref.at[pl.ds(0, count)]
    return pltpu.make_async_remote_copy(
        some, some, send_sem, recv_sem, device_id=(0, 0), device_id_type=MESH
    )


def coords():
    s=lax.axis_index("section"); d=lax.axis_index("dp")
    return s,d,d//4,(d//2)%2,d%2

def items():
    out=[]
    for bx in (0,1):
        for by in (0,1):
            for dz in (0,-1,1,-2,2,-3,3):
                out.append((bx,by,dz))
    return out
def hops(it): return it[0]+it[1]+abs(it[2])
def arrival(order,it):
    diff={"x":it[0]!=0,"y":it[1]!=0,"z":it[2]!=0}
    last=None
    for k,dim in enumerate(order):
        if diff[dim]: last=k
    return last

def neighbours(s,d,z,y,c,zn):
    return [(None,(1-s,d)),(None,(s,(z*2+1-y)*2+c)),(None,(s,(z*2+y)*2+1-c)),(z>0,(s,d-4)),(z<zn-1,(s,d+4))]


def forward_kernel(layer, peers, *refs):
    mats_ref, x_ref, vec_ref, segc_ref, segr_ref = refs[:5]
    if peers:
        give_ref, order_ref = refs[5:7]
        cot_ref = refs[13]
        landed, strips32, send_sem, recv_sem = refs[-4:]
        refs = refs[:5] + refs[7:13] + refs[14:-4]
        s, d = lax.axis_index("section"), lax.axis_index("dp")
        total, me = 2 * peers, s * peers + d
        signal_all(total, me, peers)
    y_ref, qkv_out, prob_out, att_out, mid_out, u_out = refs[5:11]
    held, qkv, prob, att, mid, u, norm, mask, sems, out_sems = refs[11:]
    rows, width = x_ref.shape
    depth = width // HEADS
    scale = depth ** (-0.5)

    def weight(index):
        return pltpu.make_async_copy(
            mats_ref.at[layer, pl.ds(index * width, width)], held.at[index], sems.at[index]
        )

    keeps = [
        pltpu.make_async_copy(src, dst, out_sems.at[index])
        for index, (src, dst) in enumerate(
            ((qkv, qkv_out), (prob, prob_out), (att, att_out), (mid, mid_out), (u, u_out))
        )
    ]
    for index in range(6):
        weight(index).start()
    tiles = [slice(c, c + WIN) for c in range(0, width, WIN)]
    norm[...] = norm_rows(x_ref[...].astype(jnp.float32), vec_ref[0:1, :]).astype(jnp.bfloat16)
    qi = lax.broadcasted_iota(jnp.int32, (rows, rows), 0)
    ki = lax.broadcasted_iota(jnp.int32, (rows, rows), 1)
    mask[...] = jnp.where((segc_ref[...] == segr_ref[...]) & (ki <= qi), 3e38, NEG)
    for index in range(3):
        weight(index).wait()
        for cols in tiles:
            part = nn(norm[...], held[index, :, cols])
            if index == 0:
                part = part * (scale * LOG2E)
            qkv[index, :, cols] = part.astype(jnp.bfloat16)
    keeps[0].start()
    if peers:
        wait_all(total)

        @pl.when(s == 1)
        def _():
            landed[d] = give_ref[1, d]

            def give(step, carry):
                other = lax.rem(me + step, total)
                sec, dp = other // peers, lax.rem(other, peers)
                pltpu.make_async_remote_copy(
                    give_ref.at[sec, dp], landed.at[d], send_sem, recv_sem,
                    device_id=(sec, dp), device_id_type=MESH,
                ).start()
                return carry

            lax.fori_loop(1, total, give, 0)

    att[...] = jnp.zeros_like(att)

    def head_group(group, carry):
        blocks = range(rows // QB)
        heres = [slice(block * QB, (block + 1) * QB) for block in blocks]
        uptos = [slice(0, (block + 1) * QB) for block in blocks]
        work = []
        for k in range(GROUP):
            head = group * GROUP + k
            start, lanes = head_window(head, depth, width)
            work += [(head, pl.ds(start, WIN), lanes, heres[b], uptos[b]) for b in blocks]
        scores = [nt(jnp.where(lanes, qkv[0, here, cols], 0), qkv[1, upto, cols]) for head, cols, lanes, here, upto in work]
        scores = [jnp.minimum(score, mask[w[3], w[4]]) for score, w in zip(scores, work)]
        tops = [jnp.max(score, axis=-1, keepdims=True) for score in scores]
        expds = [jnp.exp2(score - top) for score, top in zip(scores, tops)]
        sums = [1.0 / jnp.sum(e, axis=-1, keepdims=True) for e in expds]
        softs = [(e * r).astype(jnp.bfloat16) for e, r in zip(expds, sums)]
        for soft, (head, cols, lanes, here, upto) in zip(softs, work):
            prob[head, here, upto] = soft
        mixes = [nn(soft, qkv[2, w[4], w[1]]).astype(jnp.bfloat16) for soft, w in zip(softs, work)]
        for mixed, (head, cols, lanes, here, upto) in zip(mixes, work):
            att[here, cols] = jnp.where(lanes, mixed, att[here, cols])
        return carry

    lax.fori_loop(0, HEADS // GROUP, head_group, 0)
    keeps[1].start()
    keeps[2].start()
    weight(3).wait()
    for cols in tiles:
        mid[:, cols] = x_ref[:, cols].astype(jnp.float32) + nn(att[...], held[3, :, cols])
    keeps[3].start()
    norm[...] = norm_rows(mid[...], vec_ref[1:2, :]).astype(jnp.bfloat16)
    weight(4).wait()
    for cols in tiles:
        u[:, cols] = nn(norm[...], held[4, :, cols]) + vec_ref[2:3, cols]
    keeps[4].start()
    for cols in tiles:
        pre = u[:, cols]
        act = 0.5 * pre * (1.0 + jnp.tanh(GC * (pre + GA * (pre * pre * pre))))
        norm[:, cols] = act.astype(jnp.bfloat16)
    weight(5).wait()
    for cols in tiles:
        out = mid[:, cols] + (nn(norm[...], held[5, :, cols]) + vec_ref[3:4, cols])
        y_ref[:, cols] = out.astype(jnp.bfloat16)
    if peers:
        pl.when(s == 1)(lambda: bulk_copy(landed, peers - 1, send_sem, recv_sem).wait_recv())
        pl.when(s != 1)(lambda: bulk_copy(landed, peers, send_sem, recv_sem).wait_recv())
        strips32[...] = landed[...].astype(jnp.float32)
        join_strips(order_ref[...], strips32, cot_ref)

        @pl.when(s == 1)
        def _():
            bulk_copy(give_ref.at[0], peers, send_sem, recv_sem).wait_send()
            bulk_copy(give_ref.at[0], peers - 1, send_sem, recv_sem).wait_send()

    for keep in keeps:
        keep.wait()


def forward_layer(layer, mats, x, vec, segc, segr, trade=None):
    rows, width = x.shape
    f32, b16 = jnp.float32, jnp.bfloat16
    vm = pl.BlockSpec(memory_space=pltpu.VMEM)
    hbm = pl.BlockSpec(memory_space=pl.ANY)
    kept = [
        ((3, rows, width), b16), ((HEADS, rows, rows), b16), ((rows, width), b16),
        ((rows, width), f32), ((rows, width), f32),
    ]
    peers = trade[0].shape[1] if trade else 0
    block = trade[0].shape[1:] if trade else None
    dma = pltpu.SemaphoreType.DMA
    return pl.pallas_call(
        functools.partial(forward_kernel, layer, peers),
        out_shape=[jax.ShapeDtypeStruct((rows, width), b16)]
        + [jax.ShapeDtypeStruct(shape, dtype) for shape, dtype in kept]
        + [jax.ShapeDtypeStruct((rows, width), b16)] * bool(trade),
        in_specs=[hbm, vm, vm, vm, vm] + [vm, vm] * bool(trade),
        out_specs=[vm] + [hbm] * 5 + [vm] * bool(trade),
        scratch_shapes=[pltpu.VMEM((6, width, width), b16)]
        + [pltpu.VMEM(shape, dtype) for shape, dtype in kept]
        + [
            pltpu.VMEM((rows, width), b16),
            pltpu.VMEM((rows, rows), f32),
            dma((6,)),
            dma((5,)),
        ]
        + ([pltpu.VMEM(block, b16), pltpu.VMEM(block, f32), dma, dma] if trade else []),
        compiler_params=pltpu.CompilerParams(
            vmem_limit_bytes=VMEM_LIMIT,
            **(dict(collective_id=3, has_side_effects=True) if trade else {}),
        ),
        name="layer_forward",
    )(mats, x, vec, segc, segr, *(trade or ()))


def give_back(to, s, d, me, peers, sendbuf, returned, local_sem, send_sem, recv_sem):
    keep = pltpu.make_async_copy(sendbuf.at[d], returned.at[me], local_sem)
    pl.when(s == to)(lambda: keep.start())

    def give(step, carry):
        dp = lax.rem(d + step, peers)
        pltpu.make_async_remote_copy(
            sendbuf.at[dp], returned.at[me], send_sem, recv_sem,
            device_id=(to, dp), device_id_type=MESH,
        ).start()
        return carry

    @pl.when(s != to)
    def _():
        give(0, 0)

    lax.fori_loop(1, peers, give, 0)

    def finish():
        @pl.when(s == to)
        def _():
            keep.wait()
            bulk_copy(returned, 2 * peers - 1, send_sem, recv_sem).wait_recv()
            bulk_copy(sendbuf, peers - 1, send_sem, recv_sem).wait_send()

        pl.when(s != to)(lambda: bulk_copy(sendbuf, peers, send_sem, recv_sem).wait_send())

    return finish


def backward_kernel(layer, aliased, peers, *refs):
    if peers:
        final_ref, place_ref = refs[9:11]
        returned = refs[14]
        strips32, sendbuf, local_sem, send_sem, recv_sem = refs[-5:]
        refs = refs[:9] + refs[11:14] + refs[15:-5]
        s, d = lax.axis_index("section"), lax.axis_index("dp")
        total, me = 2 * peers, s * peers + d
        signal_all(total, me, peers)
    mats_ref, x_ref, vec_ref, dy_ref, qkv_in, prob_in, att_in, mid_in, u_in = refs[:9]
    rest = refs[10:] if aliased else refs[9:]
    (
        grads_ref, dx_ref, dvec_ref,
        held, qkv, prob, att, mid, u, act, low, wide, dmid, dqkv, dscore, turned, stage,
        sems, in_sems, out_sems,
    ) = rest
    rows, width = x_ref.shape
    depth = width // HEADS
    scale = depth ** (-0.5)
    f32, b16 = jnp.float32, jnp.bfloat16
    tiles = [slice(c, c + WIN) for c in range(0, width, WIN)]

    def weight(index):
        return pltpu.make_async_copy(
            mats_ref.at[layer, pl.ds(index * width, width)], held.at[index], sems.at[index]
        )

    loads = [
        pltpu.make_async_copy(src, dst, in_sems.at[index])
        for index, (src, dst) in enumerate(
            ((qkv_in, qkv), (prob_in, prob), (att_in, att), (mid_in, mid), (u_in, u))
        )
    ]
    loads[4].start()
    weight(5).start()
    weight(4).start()
    loads[3].start()
    weight(3).start()
    loads[2].start()
    loads[0].start()
    loads[1].start()
    for index in range(3):
        weight(index).start()

    if peers:
        cut_strips(place_ref[...], final_ref, strips32)
        sendbuf[...] = strips32[...].astype(b16)
        wait_all(total)
        back = give_back(1, s, d, me, peers, sendbuf, returned, local_sem, send_sem, recv_sem)

    def put(index, slot):
        return pltpu.make_async_copy(
            stage.at[slot], grads_ref.at[layer, pl.ds(index * width, width)], out_sems.at[index]
        )

    slots = {5: 0, 4: 1, 3: 0, 2: 1, 1: 0, 0: 1}
    before = {3: 5, 2: 4, 1: 3, 0: 2}

    def weight_grad(index, left_t, right):
        slot = slots[index]
        if index in before:
            put(before[index], slot).wait()
        for cols in tiles:
            stage[slot, cols, :] = nn(left_t(cols), right).astype(b16)
        put(index, slot).start()

    dvec_ref[3:4, :] = jnp.sum(dy_ref[...].astype(f32), axis=0, keepdims=True)
    loads[4].wait()
    weight(5).wait()
    for cols in tiles:
        pre = u[:, cols]
        square = pre * pre
        bent = jnp.tanh(GC * (pre + GA * (square * pre)))
        half = 0.5 * (1.0 + bent)
        act[:, cols] = (pre * half).astype(b16)
        slope = half + (0.5 * GC) * pre * (1.0 - bent * bent) * (1.0 + (3.0 * GA) * square)
        down = nt(dy_ref[...], held[5, cols, :]) * slope
        down = down.astype(b16)
        low[:, cols] = down
        dvec_ref[2:3, cols] = jnp.sum(down.astype(f32), axis=0, keepdims=True)
    weight_grad(5, lambda cols: act[:, cols].T, dy_ref[...])
    weight(4).wait()
    for cols in tiles:
        wide[:, cols] = nt(low[...], held[4, cols, :])
    loads[3].wait()
    act[...] = norm_rows(mid[...], vec_ref[1:2, :]).astype(b16)
    weight_grad(4, lambda cols: act[:, cols].T, low[...])
    part, gain_sum = norm_back(mid[...], vec_ref[1:2, :], wide[...])
    dvec_ref[1:2, :] = gain_sum
    total = dy_ref[...].astype(f32) + part
    dmid[...] = total
    low[...] = total.astype(b16)
    loads[2].wait()
    weight_grad(3, lambda cols: att[:, cols].T, low[...])
    weight(3).wait()
    for cols in tiles:
        act[:, cols] = nt(low[...], held[3, cols, :]).astype(b16)
    loads[0].wait()
    loads[1].wait()
    dqkv[...] = jnp.zeros_like(dqkv)

    def head_group(group, carry):
        blocks = range(rows // QB)
        heres = [slice(block * QB, (block + 1) * QB) for block in blocks]
        uptos = [slice(0, (block + 1) * QB) for block in blocks]
        sinces = [slice(block * QB, rows) for block in blocks]
        work = []
        for k in range(GROUP):
            head = group * GROUP + k
            start, lanes = head_window(head, depth, width)
            work += [(head, pl.ds(start, WIN), lanes, heres[b], uptos[b], sinces[b], k) for b in blocks]
        dprobs = [nt(jnp.where(w[2], act[w[3], w[1]], 0), qkv[2, w[4], w[1]]) for w in work]
        softs = [prob[w[0], w[3], w[4]].astype(f32) for w in work]
        leans = [jnp.sum(dp * soft, axis=-1, keepdims=True) for dp, soft in zip(dprobs, softs)]
        dss = [(soft * (dp - lean)).astype(b16) for dp, soft, lean in zip(dprobs, softs, leans)]
        for ds, w in zip(dss, work):
            dscore[w[6], w[3], w[4]] = ds
        dvs = [tn(prob[w[0], w[5], w[3]], act[w[5], w[1]]).astype(b16) for w in work]
        dqs = [(nn(ds, qkv[1, w[4], w[1]]) * scale).astype(b16) for ds, w in zip(dss, work)]
        dks = [(tn(dscore[w[6], w[5], w[3]], qkv[0, w[5], w[1]]) * LN2).astype(b16) for w in work]
        for dq, dk, dv, w in zip(dqs, dks, dvs, work):
            for index, value in enumerate((dq, dk, dv)):
                dqkv[index, w[3], w[1]] = jnp.where(w[2], value, dqkv[index, w[3], w[1]])
        return carry

    lax.fori_loop(0, HEADS // GROUP, head_group, 0)
    low[...] = norm_rows(x_ref[...].astype(f32), vec_ref[0:1, :]).astype(b16)
    for cols in tiles:
        turned[cols, :] = low[:, cols].T
    for index in (2, 1, 0):
        weight_grad(index, lambda cols: turned[cols, :], dqkv[index])
    for index in range(3):
        weight(index).wait()
    for cols in tiles:
        wide[:, cols] = (
            nt(dqkv[0], held[0, cols, :]) + nt(dqkv[1], held[1, cols, :]) + nt(dqkv[2], held[2, cols, :])
        )
    part, gain_sum = norm_back(x_ref[...].astype(f32), vec_ref[0:1, :], wide[...])
    dvec_ref[0:1, :] = gain_sum
    dvec_ref[4:8, :] = jnp.zeros_like(dvec_ref[4:8, :])
    dx_ref[...] = (dmid[...] + part).astype(b16)
    put(1, 0).wait()
    put(0, 1).wait()
    if peers:
        back()


def backward_layer(layer, mats, x, vec, dy, kept, grads, trade=None):
    rows, width = x.shape
    f32, b16 = jnp.float32, jnp.bfloat16
    vm = pl.BlockSpec(memory_space=pltpu.VMEM)
    hbm = pl.BlockSpec(memory_space=pl.ANY)
    aliased = grads is not None
    peers, block = (trade[2], trade[3]) if trade else (0, None)
    dma = pltpu.SemaphoreType.DMA
    return pl.pallas_call(
        functools.partial(backward_kernel, layer, aliased, peers),
        out_shape=[
            jax.ShapeDtypeStruct(mats.shape, b16),
            jax.ShapeDtypeStruct((rows, width), b16),
            jax.ShapeDtypeStruct((8, width), f32),
        ]
        + ([jax.ShapeDtypeStruct((2 * peers,) + block, b16)] if trade else []),
        in_specs=[hbm, vm, vm, vm] + [hbm] * 5 + ([hbm] if aliased else []) + [vm, vm] * bool(trade),
        out_specs=[hbm, vm, vm] + [hbm] * bool(trade),
        scratch_shapes=[
            pltpu.VMEM((6, width, width), b16),
            pltpu.VMEM((3, rows, width), b16),
            pltpu.VMEM((HEADS, rows, rows), b16),
            pltpu.VMEM((rows, width), b16),
            pltpu.VMEM((rows, width), f32),
            pltpu.VMEM((rows, width), f32),
            pltpu.VMEM((rows, width), b16),
            pltpu.VMEM((rows, width), b16),
            pltpu.VMEM((rows, width), f32),
            pltpu.VMEM((rows, width), f32),
            pltpu.VMEM((3, rows, width), b16),
            pltpu.VMEM((GROUP, rows, rows), b16),
            pltpu.VMEM((width, rows), b16),
            pltpu.VMEM((2, width, width), b16),
            dma((6,)),
            dma((5,)),
            dma((6,)),
        ]
        + (
            [pltpu.VMEM((peers,) + block, f32), pltpu.VMEM((peers,) + block, b16), dma, dma, dma]
            if trade
            else []
        ),
        input_output_aliases={9: 0} if aliased else {},
        compiler_params=pltpu.CompilerParams(
            vmem_limit_bytes=VMEM_LIMIT,
            **(dict(collective_id=4, has_side_effects=True) if trade else {}),
        ),
        name="layer_backward",
    )(*((mats, x, vec, dy) + tuple(kept) + ((grads,) if aliased else ()) + (tuple(trade[:2]) if trade else ())))


def rs_kernel(parts,zn,g_ref,v_ref,dx_ref,place_ref,picks_ref,early_ref,o_ref,vo_ref,res_ref,land,buf,obuf,vland,strips32,sendbuf,returned,*rest):
    nP=len(parts)
    lks=rest[:nP]
    ssem,rsem,cs,cr,lsem,osem,vsend,vrecv,tlocal,tsend,trecv,tearly=rest[nP:]
    s,d,z,y,c=coords()
    peers=4*zn
    total_dev=2*peers
    me=s*peers+d
    signal_all(total_dev,me,peers)
    early=pltpu.make_async_copy(early_ref,returned,tearly)
    pl.when(s==1)(lambda: early.start())
    cut_strips(place_ref[...],dx_ref,strips32)
    sendbuf[...]=strips32[...].astype(jnp.bfloat16)
    wait_all(total_dev)
    vland[me]=v_ref[me]
    def small(step,carry):
        other=lax.rem(me+step,total_dev)
        pltpu.make_async_remote_copy(v_ref.at[other],vland.at[me],vsend,vrecv,device_id=(other//peers,lax.rem(other,peers)),device_id_type=MESH).start()
        return carry
    lax.fori_loop(1,total_dev,small,0)
    sib=(s,(z*2+y)*2+1-c)
    def where(it):
        s2=1-s if it[0] else s
        y2=1-y if it[1] else y
        return s2,z+it[2],y2
    def conds(it):
        cl=[]
        if it[2]<0: cl.append(z+it[2]>=0)
        if it[2]>0: cl.append(z+it[2]<=zn-1)
        return cl
    def guarded(cl,fn):
        if not cl: fn(); return
        e=cl[0]
        for q in cl[1:]: e=jnp.logical_and(e,q)
        pl.when(e)(fn)
    def slot_base(order):
        sizes={"x":2,"y":2,"z":zn}
        base={};cur=0
        for k,dim in enumerate(order):
            n=1
            for q in order[k+1:]: n*=sizes[q]
            if dim=="z": n*=2*zn
            base[dim]=cur; cur+=n
        return base,cur
    def slot(p,dim,side,dest):
        order=parts[p][2][::-1]
        base,_=slot_base(order)
        k=order.index(dim)
        v={"x":dest[0],"z":dest[1],"y":dest[2]}
        idx=0
        for q in order[k+1:]:
            idx=idx*(zn if q=="z" else 2)+v[q]
        if dim=="z": idx=(idx*zn+dest[1])*2+side
        return base[dim]+idx
    evs=[]
    for p in range(nP):
        for it in items():
            if abs(it[2])<=zn-1: evs.append((-hops(it),p,it))
    evs.sort(key=lambda e:e[0])
    seq=[(p,it) for _,p,it in evs]
    def core_dsc(p,it,mine):
        r0,rn,_=parts[p]
        s2,z2,y2=where(it)
        idx=(s2*zn+z2)*2+y2
        cc=c if mine else 1-c
        return pltpu.make_async_remote_copy(g_ref.at[s2,(z2*2+y2)*2+cc,pl.ds(r0,rn)],land.at[idx,pl.ds(r0,rn)],cs.at[p,idx],cr.at[p,idx],device_id=sib,device_id_type=MESH)
    for p,it in seq:
        guarded(conds(it),lambda p=p,it=it: core_dsc(p,it,False).start())
    back=give_back(0,s,d,me,peers,sendbuf,returned,tlocal,tsend,trecv)
    def load(i):
        p,it=seq[i]
        r0,rn,_=parts[p]
        s2,z2,y2=where(it)
        return pltpu.make_async_copy(g_ref.at[s2,(z2*2+y2)*2+c,pl.ds(r0,rn)],buf.at[i%NB,pl.ds(0,rn)],lsem.at[i%NB])
    NB=buf.shape[0]
    for i in range(min(NB-1,len(seq))):
        guarded(conds(seq[i][1]),lambda i=i: load(i).start())
    def contribs(p,it):
        order=parts[p][2][::-1]
        diff={"x":it[0],"y":it[1],"z":it[2]}
        out=[];nxt=None
        for dim in order:
            if dim=="z":
                if it[2]==0: out+=[("z",0,z>0),("z",1,z<zn-1)]
                elif it[2]>0: out.append(("z",0,z>0))
                else: out.append(("z",1,z<zn-1))
                if it[2]!=0: nxt="r" if it[2]>0 else "l"; break
            else:
                if diff[dim]: nxt=dim; break
                out.append((dim,0,None))
        return out,nxt
    semoff=[0]
    for p in range(nP): semoff.append(semoff[-1]+slot_base(parts[p][2][::-1])[1])
    def out_dsc(p,it,nxt):
        r0,rn,_=parts[p]
        dest=where(it)
        s2,z2,y2=dest
        idx=(s2*zn+z2)*2+y2
        dim="z" if nxt in "lr" else nxt
        side=1 if nxt=="l" else 0
        sl=slot(p,dim,side,dest)
        dev={"x":(1-s,d),"y":(s,(z*2+1-y)*2+c),"l":(s,d-4),"r":(s,d+4)}[nxt]
        return pltpu.make_async_remote_copy(land.at[idx,pl.ds(r0,rn)],lks[p].at[sl],ssem.at[p,idx],rsem.at[semoff[p]+sl],device_id=dev,device_id_type=MESH)
    for i,(p,it) in enumerate(seq):
        r0,rn,_=parts[p]
        if i+NB-1<len(seq):
            guarded(conds(seq[i+NB-1][1]),lambda i=i: load(i+NB-1).start())
        def ev(i=i,p=p,it=it,r0=r0,rn=rn):
            dest=where(it)
            s2,z2,y2=dest
            idx=(s2*zn+z2)*2+y2
            con,nxt=contribs(p,it)
            lk=lks[p]
            load(i).wait()
            core_dsc(p,it,True).wait_recv()
            plain=[x for x in con if x[2] is None]
            cond=[x for x in con if x[2] is not None]
            def rdsc(dim,side):
                sl=slot(p,dim,side,dest)
                return pltpu.make_async_remote_copy(lk.at[sl],lk.at[sl],ssem.at[p,idx],rsem.at[semoff[p]+sl],device_id=sib,device_id_type=MESH),sl
            for dim,side,_ in plain: rdsc(dim,side)[0].wait_recv()
            for dim,side,cnd in cond:
                pl.when(cnd)(lambda dim=dim,side=side: rdsc(dim,side)[0].wait_recv())
            if not cond: variants=[(None,plain)]
            elif len(cond)==1:
                variants=[(cond[0][2],plain+cond),(jnp.logical_not(cond[0][2]),plain)]
            else:
                a,b=cond
                variants=[(jnp.logical_and(a[2],b[2]),plain+cond),(jnp.logical_and(a[2],jnp.logical_not(b[2])),plain+[a]),
                          (jnp.logical_and(jnp.logical_not(a[2]),b[2]),plain+[b])]
            def total(lst):
                slots=[slot(p,dim,side,dest) for dim,side,_ in lst]
                CH=16
                def body(k,_):
                    ro=pl.multiple_of(k*CH,CH)
                    acc=buf[i%NB,pl.ds(ro,CH),:].astype(jnp.float32)+land[idx,pl.ds(r0+ro,CH),:].astype(jnp.float32)
                    for sl in slots: acc=acc+lk[sl,pl.ds(ro,CH),:].astype(jnp.float32)
                    if nxt is None: obuf[pl.ds(r0+ro,CH),:]=acc
                    else: land[idx,pl.ds(r0+ro,CH),:]=acc.astype(jnp.bfloat16)
                    return 0
                lax.fori_loop(0,rn//CH,body,0)
            for cnd,lst in variants:
                if cnd is None: total(lst)
                else: pl.when(cnd)(lambda lst=lst: total(lst))
            if nxt is not None: out_dsc(p,it,nxt).start()
            else: pltpu.make_async_copy(obuf.at[pl.ds(r0,rn)],o_ref.at[pl.ds(r0,rn)],osem.at[p]).start()
        guarded(conds(it),ev)
    for p,it in seq:
        def fin(p=p,it=it):
            core_dsc(p,it,False).wait_send()
            nxt=contribs(p,it)[1]
            if nxt is not None: out_dsc(p,it,nxt).wait_send()
        guarded(conds(it),fin)
    for p,(r0,rn,_) in enumerate(parts):
        pltpu.make_async_copy(obuf.at[pl.ds(r0,rn)],o_ref.at[pl.ds(r0,rn)],osem.at[p]).wait()
    rest_of=vland.at[pl.ds(0,total_dev-1)]
    bulk=pltpu.make_async_remote_copy(rest_of,rest_of,vsend,vrecv,device_id=(0,0),device_id_type=MESH)
    bulk.wait_recv()
    bulk.wait_send()
    vo_ref[...]=jnp.sum(vland[...],axis=0)
    back()
    pl.when(s==1)(lambda: early.wait())
    for batch in range(2):
        strips32[...]=returned[batch*peers:(batch+1)*peers].astype(jnp.float32)
        join_strips(picks_ref[batch],strips32,res_ref.at[batch])


def slot_count(order,zn):
    sizes={"x":2,"y":2,"z":zn};cur=0
    for k,dim in enumerate(order):
        n=1
        for q in order[k+1:]: n*=sizes[q]
        if dim=="z": n*=2*zn
        cur+=n
    return cur
def rs(g,v,dx,place,picks,early,parts,zn,cid=1,nb=4):
    n=len(parts)
    cnt=[slot_count(p[2][::-1],zn) for p in parts]
    mx=max(p[1] for p in parts)
    return pl.pallas_call(functools.partial(rs_kernel,parts,zn),
        out_shape=[jax.ShapeDtypeStruct((480,1280),jnp.float32),jax.ShapeDtypeStruct(v.shape[1:],jnp.float32),
            jax.ShapeDtypeStruct((2,)+dx.shape,jnp.bfloat16)],
        in_specs=[pl.BlockSpec(memory_space=pl.ANY)]+[pl.BlockSpec(memory_space=pltpu.VMEM)]*4+[pl.BlockSpec(memory_space=pl.ANY)],
        out_specs=[pl.BlockSpec(memory_space=pl.ANY)]+[pl.BlockSpec(memory_space=pltpu.VMEM)]*2,
        scratch_shapes=[pltpu.VMEM((4*zn,480,1280),jnp.bfloat16),pltpu.VMEM((nb,mx,1280),jnp.bfloat16),pltpu.VMEM((480,1280),jnp.float32),pltpu.VMEM(v.shape,jnp.float32),
            pltpu.VMEM((4*zn,)+early.shape[1:],jnp.float32),pltpu.VMEM((4*zn,)+early.shape[1:],jnp.bfloat16),pltpu.VMEM(early.shape,jnp.bfloat16)]
          +[pltpu.VMEM((cnt[p],parts[p][1],1280),jnp.bfloat16) for p in range(n)]
          +[pltpu.SemaphoreType.DMA((n,4*zn)),pltpu.SemaphoreType.DMA((sum(cnt),)),
          pltpu.SemaphoreType.DMA((n,4*zn)),pltpu.SemaphoreType.DMA((n,4*zn)),pltpu.SemaphoreType.DMA((nb,)),pltpu.SemaphoreType.DMA((n,))]+[pltpu.SemaphoreType.DMA]*6,
        compiler_params=pltpu.CompilerParams(collective_id=cid,has_side_effects=True,vmem_limit_bytes=62*2**20))(g,v,dx,place,picks,early)


def as_row(column):
    rows = column.shape[0]
    return jnp.broadcast_to(column, (rows, 128)).T[0:1, :]


def as_column(row):
    size = row.shape[1]
    return jnp.broadcast_to(row, (128, size)).T[:, 0:1]


def ones_where(flag):
    return jnp.where(flag, 1.0, 0.0)


def gather_events(parts,zn,place,own,w_ref,ssem,rsem,cs,cr):
    s,d,z,y,c=place
    KIND={"x":0,"y":1,"l":2,"r":3}
    def where(it):
        s2=1-s if it[0] else s
        y2=1-y if it[1] else y
        z2=z+it[2]
        return s2,z2,y2
    def dsc(p,it,kind):
        r0,rn,order=parts[p]
        s2,z2,y2=where(it)
        idx=s2*(2*zn)+z2*2+y2
        is_own=it==(0,0,0)
        src=own.at[pl.ds(r0,rn)] if is_own else w_ref.at[s2,(z2*2+y2)*2+c,pl.ds(r0,rn)]
        dst=w_ref.at[s2,(z2*2+y2)*2+c,pl.ds(r0,rn)]
        if kind=="core":
            dev=(s,(z*2+y)*2+1-c)
            return pltpu.make_async_remote_copy(src,dst,cs.at[p,idx],cr.at[p,idx],device_id=dev,device_id_type=MESH)
        dev={"x":(1-s,d),"y":(s,(z*2+1-y)*2+c),"l":(s,d-4),"r":(s,d+4)}[kind]
        return pltpu.make_async_remote_copy(src,dst,ssem.at[KIND[kind],p,idx],rsem.at[p,idx],device_id=dev,device_id_type=MESH)
    def cdsc(p,it):
        r0,rn,order=parts[p]
        s2,z2,y2=where(it)
        idx=s2*(2*zn)+z2*2+y2
        dst=w_ref.at[s2,(z2*2+y2)*2+1-c,pl.ds(r0,rn)]
        return pltpu.make_async_remote_copy(dst,dst,cs.at[p,idx],cr.at[p,idx],device_id=(s,(z*2+y)*2+1-c),device_id_type=MESH)
    def conds(it,kind):
        cs_=[]
        if it[2]<0: cs_.append(z+it[2]>=0)
        if it[2]>0: cs_.append(z+it[2]<=zn-1)
        if kind=="l": cs_.append(z>0)
        if kind=="r": cs_.append(z<zn-1)
        return cs_
    def guarded(cl,fn):
        if not cl: fn(); return
        e=cl[0]
        for q in cl[1:]: e=jnp.logical_and(e,q)
        pl.when(e)(fn)
    def sends(p,it):
        order=parts[p][2]
        a=arrival(order,it)
        ks=[]
        if a is not None and order[a]=="z": ks.append("l" if it[2]>0 else "r")
        for dim in order[(a+1) if a is not None else 0:]:
            ks += ["r","l"] if dim=="z" else [dim]
        ks.append("core")
        return ks
    evs=[]
    for p in range(len(parts)):
        for it in items():
            if abs(it[2])<zn: evs.append((hops(it),p,it))
    evs.sort(key=lambda e:e[0])
    first=[]
    later=[]
    for h,p,it in evs:
        def ev(p=p,it=it):
            if it!=(0,0,0): dsc(p,it,"x").wait_recv()
            for k in sends(p,it):
                guarded(conds((0,0,0),k), lambda k=k: dsc(p,it,k).start())
        (later if h else first).append(lambda it=it,ev=ev: guarded(conds(it,None),ev))
    def finish():
        for _,p,it in evs:
            def fin(p=p,it=it):
                cdsc(p,it).wait_recv()
                for k in sends(p,it):
                    guarded(conds((0,0,0),k), lambda k=k: dsc(p,it,k).wait_send())
            guarded(conds(it,None),fin)
    return first,later,finish


def enter_kernel(
    parts, zn, mats_ref, packet_ref, deal_ref, tokens_ref,
    w_ref, shared_ref, x_ref, order, picks_ref, place_ref, sendbuf,
    own, wide_rows, strips32, landed,
    own_sem, lsem, ssem, rsem, cs, cr, psend, precv, tsend, trecv,
):
    s, d, z, y, c = coords()
    peers = 4 * zn
    total = 2 * peers
    me = s * peers + d
    batches, rows, width = tokens_ref.shape
    f32, b16 = jnp.float32, jnp.bfloat16
    cast_in = pltpu.make_async_copy(mats_ref, wide_rows, own_sem)
    cast_in.start()
    greet(total, me, peers)
    shared_ref[me] = packet_ref[...]

    def tell(step, carry):
        other = lax.rem(me + step, total)
        pltpu.make_async_remote_copy(
            packet_ref, shared_ref.at[me], psend, precv,
            device_id=(other // peers, lax.rem(other, peers)), device_id_type=MESH,
        ).start()
        return carry

    lax.fori_loop(1, total, tell, 0)
    cast_in.wait()
    own[...] = wide_rows[...].astype(b16)
    lc = pltpu.make_async_copy(own, w_ref.at[s, d], lsem)
    lc.start()
    start_events, rest_events, finish = gather_events(
        parts, zn, (s, d, z, y, c), own, w_ref, ssem, rsem, cs, cr
    )
    for event in start_events:
        event()
    sub = lax.broadcasted_iota(jnp.int32, (rows, rows), 0).astype(f32)
    lane = lax.broadcasted_iota(jnp.int32, (rows, rows), 1).astype(f32)
    mine_row = jnp.where(s == 0, deal_ref[0:1, :], deal_ref[1:2, :])
    mine_col = as_column(mine_row)
    rank_col = jnp.sum(ones_where(mine_row < mine_col), axis=1, keepdims=True)
    order[...] = ones_where(lane == rank_col).astype(b16)
    rank_row = jnp.sum(ones_where(mine_col < mine_row), axis=0, keepdims=True)
    place_ref[...] = ones_where(sub == rank_row).astype(b16)
    rest = shared_ref.at[pl.ds(0, total - 1)]
    bulk = pltpu.make_async_remote_copy(
        rest, rest, psend, precv, device_id=(0, 0), device_id_type=MESH
    )
    bulk.wait_recv()
    index_col = lax.broadcasted_iota(jnp.int32, (rows, 1), 0).astype(f32)
    ids_col = index_col + (d * rows).astype(f32)
    for batch in range(batches):

        def look(block, found):
            known = shared_ref[s * peers + block]
            for line in range(rows // 128):
                at = batch * (rows // 128) + line
                found = jnp.where(ids_col == known[at : at + 1, :], block.astype(f32), found)
            return found

        found = lax.fori_loop(0, peers, look, jnp.zeros((rows, 128), f32))
        key_col = jnp.sum(found, axis=1, keepdims=True) * rows + index_col
        key_row = as_row(key_col)
        rank_row = jnp.sum(ones_where(key_col < key_row), axis=0, keepdims=True)
        rank_col = jnp.sum(ones_where(key_row < key_col), axis=1, keepdims=True)
        picks_ref[batch] = ones_where(lane == rank_col).astype(b16)
        pick = ones_where(sub == rank_row).astype(b16)
        cut_strips(pick, tokens_ref.at[batch], strips32)
        sendbuf[batch] = strips32[...].astype(b16)

    @pl.when(s == 0)
    def _():
        landed[d] = sendbuf[0, d]

        def give(step, carry):
            other = lax.rem(me + step, total)
            sec, dp = other // peers, lax.rem(other, peers)
            pltpu.make_async_remote_copy(
                sendbuf.at[sec, dp], landed.at[d], tsend, trecv,
                device_id=(sec, dp), device_id_type=MESH,
            ).start()
            return carry

        lax.fori_loop(1, total, give, 0)

    for event in rest_events:
        event()

    pl.when(s == 0)(lambda: bulk_copy(landed, peers - 1, tsend, trecv).wait_recv())
    pl.when(s != 0)(lambda: bulk_copy(landed, peers, tsend, trecv).wait_recv())
    strips32[...] = landed[...].astype(f32)
    join_strips(order[...], strips32, x_ref)
    finish()
    lc.wait()
    bulk.wait_send()

    @pl.when(s == 0)
    def _():
        bulk_copy(sendbuf.at[0], peers, tsend, trecv).wait_send()
        bulk_copy(sendbuf.at[0], peers - 1, tsend, trecv).wait_send()


def enter(mats, packet, deal, tokens, parts, zn):
    n = len(parts)
    peers = 4 * zn
    batches, rows, width = tokens.shape
    strip_rows = rows // peers * (width // 128)
    f32, b16 = jnp.float32, jnp.bfloat16
    vm = pl.BlockSpec(memory_space=pltpu.VMEM)
    hbm = pl.BlockSpec(memory_space=pl.ANY)
    dma = pltpu.SemaphoreType.DMA
    return pl.pallas_call(
        functools.partial(enter_kernel, parts, zn),
        out_shape=[
            jax.ShapeDtypeStruct((2, peers) + mats.shape, b16),
            jax.ShapeDtypeStruct((2 * peers,) + packet.shape, f32),
            jax.ShapeDtypeStruct((rows, width), b16),
            jax.ShapeDtypeStruct((rows, rows), b16),
            jax.ShapeDtypeStruct((batches, rows, rows), b16),
            jax.ShapeDtypeStruct((rows, rows), b16),
            jax.ShapeDtypeStruct((batches, peers, strip_rows, 128), b16),
        ],
        in_specs=[hbm, vm, vm, vm],
        out_specs=[hbm, vm, vm, vm, vm, vm, vm],
        scratch_shapes=[
            pltpu.VMEM(mats.shape, b16),
            pltpu.VMEM(mats.shape, f32),
            pltpu.VMEM((peers, strip_rows, 128), f32),
            pltpu.VMEM((peers, strip_rows, 128), b16),
            dma, dma, dma((4, n, peers)), dma((n, peers)), dma((n, peers)), dma((n, peers)),
            dma, dma, dma, dma,
        ],
        compiler_params=pltpu.CompilerParams(
            collective_id=0, has_side_effects=True, vmem_limit_bytes=VMEM_LIMIT
        ),
        name="enter",
    )(mats, packet, deal, tokens)


def one_hot(rank):
    rows = rank.shape[0]
    return (rank[None, :] == jnp.arange(rows, dtype=jnp.int32)[:, None]).astype(jnp.bfloat16)


def rank_of(key):
    return jnp.sum((key[None, :] < key[:, None]).astype(jnp.int32), axis=1)


def padded(flat):
    lead, size = flat.shape
    full = -(-size // 1024) * 1024
    return jnp.pad(flat, ((0, 0), (0, full - size))).reshape(lead, full // 128, 128)


def enter_plain(own, packet, deal, tokens, peers):
    section = lax.axis_index("section")
    batches, rows, width = tokens.shape
    per_peer = rows // peers
    shared = lax.all_gather(packet, BOTH, axis=0)
    low = own.astype(jnp.bfloat16)
    mats = lax.all_gather(low, BOTH, axis=0, tiled=True).reshape((2, peers) + own.shape)
    flat = shared.reshape(2, peers, -1)[:, :, : batches * rows]
    dealt = jnp.where(section == 0, flat[0], flat[1]).astype(jnp.int32).reshape(peers, batches, rows)
    own_rows = lax.axis_index("dp") * rows + jnp.arange(rows, dtype=jnp.int32)
    blocks = jnp.arange(peers, dtype=jnp.int32)
    picks = []
    sends = []
    for batch in range(batches):
        hit = dealt[:, batch][None, :, :] == own_rows[:, None, None]
        target = jnp.sum(jnp.where(hit, blocks[None, :, None], 0), axis=(1, 2))
        pick = one_hot(rank_of(target * rows + jnp.arange(rows, dtype=jnp.int32)))
        picks.append(pick.T)
        sends.append(nn(pick, tokens[batch]).astype(jnp.bfloat16))
    outgoing = jnp.stack(sends).reshape(2 * peers, per_peer, width)
    arrived = lax.all_to_all(outgoing, BOTH, split_axis=0, concat_axis=0, tiled=True)
    arrived = arrived.reshape(2, rows, width)
    place = one_hot(rank_of(jnp.where(section == 0, deal[0], deal[1])))
    x, cot = (tn(place, arrived[kind]).astype(jnp.bfloat16) for kind in range(2))
    return mats, shared, x, cot, jnp.stack(picks), place


def leave_plain(terms, small, down, final, place, picks, peers):
    sections, _, rows, width = terms.shape
    terms = terms.reshape(sections * peers * rows, width)
    total = lax.psum_scatter(terms, BOTH, scatter_dimension=0, tiled=True).astype(jnp.float32)
    small = lax.psum_scatter(small, BOTH, scatter_dimension=0, tiled=True)[0]
    back = jnp.stack([nn(place, down), nn(place, final)]).astype(jnp.bfloat16)
    count = down.shape[0]
    back = back.reshape(2 * peers, count // peers, width)
    back = lax.all_to_all(back, BOTH, split_axis=0, concat_axis=0, tiled=True)
    back = back.reshape(-1, count, width)
    results = jnp.stack([nn(picks[batch], back[batch]) for batch in range(back.shape[0])])
    return total, small, results.astype(jnp.bfloat16)


def local(entering, deal, seq_lens, mats, gains, biases):
    section = lax.axis_index("section")
    peers = lax.axis_size("dp")
    arrival = entering[0]
    batches, rows, width = arrival.shape
    per = 2 * width // peers
    vecs = jnp.concatenate([gains[0], biases[0]]).astype(jnp.bfloat16).astype(jnp.float32)
    packet = jnp.concatenate([deal.reshape(-1).astype(jnp.float32), vecs])
    packet = padded(packet[None])[0]
    packet = jnp.pad(packet, ((0, -packet.shape[0] % 8), (0, 0)))
    args = (mats[0], packet, deal.astype(jnp.float32), arrival)
    direct = peers == 16
    if direct:
        all_mats, shared, tokens, order, picks, place, gives = enter(*args, PARTS, peers // 4)
    else:
        all_mats, shared, tokens, cotangent, picks, place = enter_plain(*args, peers)
    shared = shared.reshape(2, peers, -1)
    small = shared[:, :, batches * rows : batches * rows + 2 * per].reshape(2, peers, 2, per)
    small = jnp.swapaxes(small, 1, 2).reshape(2, 4, width)
    small = jnp.pad(small, ((0, 0), (0, 4), (0, 0)))
    all_mats = all_mats.reshape(2, 6 * width, width)
    lens = jnp.where(section == 0, seq_lens[0, 0], seq_lens[1, 0])
    ends = jnp.cumsum(lens)
    positions = jnp.arange(rows, dtype=jnp.int32)
    segment = jnp.sum((positions[:, None] >= ends[None, :]).astype(jnp.int32), axis=1)
    segc, segr = segment[:, None], segment[None]
    if direct:
        middle, *kept_low, cotangent = forward_layer(
            0, all_mats, tokens, small[0], segc, segr, (gives, order)
        )
    else:
        middle, *kept_low = forward_layer(0, all_mats, tokens, small[0], segc, segr)
    final, *kept_high = forward_layer(1, all_mats, middle, small[1], segc, segr)
    trade = (final, place, peers, gives.shape[2:]) if direct else None
    terms, down, vec_high, *early = backward_layer(
        1, all_mats, middle, small[1], cotangent, kept_high, None, trade
    )
    terms, down, vec_low = backward_layer(0, all_mats, tokens, small[0], down, kept_low, terms)
    terms = terms.reshape(2, peers, -1, width)
    vec_terms = jnp.stack([vec_low, vec_high])[:, :4].reshape(2, 2, peers, per)
    vec_terms = padded(jnp.swapaxes(vec_terms, 1, 2).reshape(2 * peers, 2 * per))
    if direct:
        shard_mats, vec_total, results = rs(
            terms, vec_terms, down, place, picks, early[0], PARTS, peers // 4
        )
    else:
        shard_mats, vec_total, results = leave_plain(
            terms, vec_terms, down, final, place, picks, peers
        )
    vec_total = vec_total.reshape(-1)
    return (
        results[None],
        shard_mats[None],
        vec_total[None, :per],
        vec_total[None, per : 2 * per],
    )


def solution(mesh):
    in_specs = (
        P("section", None, "dp", None),
        P(None, "dp"),
        P(None, "dp", None),
        P("section", "dp", None),
        P("section", "dp"),
        P("section", "dp"),
    )
    out_specs = (
        P("section", None, "dp", None),
        P("section", "dp", None),
        P("section", "dp"),
        P("section", "dp"),
    )
    return jax.shard_map(local, mesh=mesh, in_specs=in_specs, out_specs=out_specs, check_vma=False)
```

```python
import functools

import jax
import jax.numpy as jnp
from jax import lax
from jax.experimental import pallas as pl
from jax.experimental.pallas import tpu as pltpu
from jax.sharding import PartitionSpec as P

HEADS = 16
EPS = 1e-06
NEG = -1000000000.0
BOTH = ("section", "dp")
MESH = pl.DeviceIdType.MESH
GATHER_PARTS = ((0, 112, "zxy"), (112, 112, "zyx"), (224, 128, "xzy"), (352, 128, "yzx"))
SCATTER_PARTS = ((0, 112, "zxy"), (112, 112, "zyx"), (224, 128, "xzy"), (352, 128, "yzx"))
TAKE_NUM, TAKE_DEN = 3, 4
SETTLE_NUM, SETTLE_DEN = 7, 8
GIVE_NUM, GIVE_DEN = 0, 1
HAND_NUM, HAND_DEN = 0, 1


WIN = 256
QB = 128
GROUP = 4
LOG2E = 1.4426950408889634
LN2 = 0.6931471805599453
GC = 0.7978845608028654
GA = 0.044715
VMEM_LIMIT = 62 * 2**20


def nn(left, right):
    return jnp.dot(left, right, preferred_element_type=jnp.float32)


def nt(left, right):
    return lax.dot_general(
        left, right, (((1,), (1,)), ((), ())), preferred_element_type=jnp.float32
    )


def tn(left, right):
    return lax.dot_general(
        left, right, (((0,), (0,)), ((), ())), preferred_element_type=jnp.float32
    )


def head_window(head, depth, width):
    start = jnp.minimum((head * depth) // 128, (width - WIN) // 128) * 128
    start = pl.multiple_of(start, 128)
    lane = lax.broadcasted_iota(jnp.int32, (1, WIN), 1) + (start - head * depth)
    return start, (lane >= 0) & (lane < depth)


def norm_rows(value, gain):
    return value * lax.rsqrt(jnp.mean(value * value, axis=-1, keepdims=True) + EPS) * gain


def norm_back(value, gain, down):
    inv = lax.rsqrt(jnp.mean(value * value, axis=-1, keepdims=True) + EPS)
    unit = value * inv
    scaled = down * gain
    lean = jnp.mean(scaled * unit, axis=-1, keepdims=True)
    return inv * (scaled - unit * lean), jnp.sum(down * unit, axis=0, keepdims=True)


def signal_all(total, me, peers):
    barrier = pltpu.get_barrier_semaphore()

    def one(step, carry):
        other = lax.rem(me + step, total)
        pl.semaphore_signal(
            barrier, inc=1, device_id=(other // peers, lax.rem(other, peers)), device_id_type=MESH
        )
        return carry

    lax.fori_loop(1, total, one, 0)


def wait_all(total):
    pl.semaphore_wait(pltpu.get_barrier_semaphore(), total - 1)


def greet(total, me, peers):
    signal_all(total, me, peers)
    wait_all(total)


def cut_strips(pick, source, strips32):
    peers = strips32.shape[0]
    strips = source.shape[-1] // 128
    each = strips32.shape[1] // strips
    for strip in range(strips):
        part = nn(pick, source[:, strip * 128 : (strip + 1) * 128])
        strips32[:, strip * each : (strip + 1) * each, :] = part.reshape(peers, each, 128)


def join_strips(order, strips32, out_ref):
    peers = strips32.shape[0]
    strips = out_ref.shape[-1] // 128
    each = strips32.shape[1] // strips
    for strip in range(strips):
        part = strips32[:, strip * each : (strip + 1) * each, :].reshape(peers * each, 128)
        part = nn(order, part.astype(jnp.bfloat16)).astype(jnp.bfloat16)
        out_ref[:, strip * 128 : (strip + 1) * 128] = part


def bulk_copy(ref, count, send_sem, recv_sem):
    some = ref.at[pl.ds(0, count)]
    return pltpu.make_async_remote_copy(
        some, some, send_sem, recv_sem, device_id=(0, 0), device_id_type=MESH
    )


def coords():
    s=lax.axis_index("section"); d=lax.axis_index("dp")
    return s,d,d//4,(d//2)%2,d%2

def items():
    out=[]
    for bx in (0,1):
        for by in (0,1):
            for dz in (0,-1,1,-2,2,-3,3):
                out.append((bx,by,dz))
    return out
def hops(it): return it[0]+it[1]+abs(it[2])
def arrival(order,it):
    diff={"x":it[0]!=0,"y":it[1]!=0,"z":it[2]!=0}
    last=None
    for k,dim in enumerate(order):
        if diff[dim]: last=k
    return last

def neighbours(s,d,z,y,c,zn):
    return [(None,(1-s,d)),(None,(s,(z*2+1-y)*2+c)),(None,(s,(z*2+y)*2+1-c)),(z>0,(s,d-4)),(z<zn-1,(s,d+4))]


SLOTS = 4
USES = (
    [(0, index) for index in range(6)] + [(1, index) for index in range(6)]
    + [(1, index) for index in (5, 4, 3, 2, 1, 0)] + [(0, index) for index in (5, 4, 3, 2, 1, 0)]
)


def plan_loads():
    def next_use(what, since):
        return next((t for t in range(since, len(USES)) if USES[t] == what), len(USES))

    held = [None] * SLOTS
    loads = []
    for done in range(-1, len(USES)):
        for t in range(done + 1, len(USES)):
            if USES[t] in held:
                continue
            away = [next_use(what, done + 1) if what else len(USES) + 1 for what in held]
            slot = max(range(SLOTS), key=lambda k: away[k])
            if away[slot] <= t:
                break
            held[slot] = USES[t]
            loads.append((done, t, slot))
    return loads


def both_layers_kernel(*refs):
    mats_ref, x_ref, vec_ref, segc_ref, segr_ref, cot_ref = refs[:6]
    y_ref, grads_ref, dx_ref, dvec_ref = refs[6:10]
    (
        held, qkvs, probs, atts, mids, us, between, act, low, mask, dqkv, dscore, turned,
    stage, sems, out_sems,
    ) = refs[10:]
    rows, width = x_ref.shape
    depth = width // HEADS
    scale = depth ** (-0.5)
    f32, b16 = jnp.float32, jnp.bfloat16
    tiles = [slice(c, c + WIN) for c in range(0, width, WIN)]
    loads = plan_loads()
    pending = {}

    def load(number):
        done, use, slot = loads[number]
        layer, index = USES[use]
        return pltpu.make_async_copy(
            mats_ref.at[layer, pl.ds(index * width, width)], held.at[slot], sems.at[number]
        )

    def after(done):
        for number, (when, use, slot) in enumerate(loads):
            if when == done:
                load(number).start()
                pending[slot] = number

    def acquire(use):
        number = max(
            k for k, (when, first, slot) in enumerate(loads) if USES[first] == USES[use] and first <= use
        )
        slot = loads[number][2]
        if pending.get(slot) == number:
            load(number).wait()
            pending.pop(slot)
        return held.at[slot]

    after(-1)
    qi = lax.broadcasted_iota(jnp.int32, (rows, rows), 0)
    ki = lax.broadcasted_iota(jnp.int32, (rows, rows), 1)
    mask[...] = jnp.where((segc_ref[...] == segr_ref[...]) & (ki <= qi), 3e38, NEG)

    def forward(layer, source, out_ref):
        qkv, prob, att, mid, u = (ref.at[layer] for ref in (qkvs, probs, atts, mids, us))
        gain_one, gain_two = vec_ref[layer, 0:1, :], vec_ref[layer, 1:2, :]
        bias_one, bias_two = vec_ref[layer, 2:3, :], vec_ref[layer, 3:4, :]
        use = 6 * layer
        low[...] = norm_rows(source[...].astype(f32), gain_one).astype(b16)
        for index in range(3):
            weight = acquire(use + index)
            for cols in tiles:
                part = nn(low[...], weight[:, cols])
                if index == 0:
                    part = part * (scale * LOG2E)
                qkv[index, :, cols] = part.astype(b16)
            after(use + index)
        att[...] = jnp.zeros_like(att)

        def head_group(group, carry):
            blocks = range(rows // QB)
            heres = [slice(block * QB, (block + 1) * QB) for block in blocks]
            uptos = [slice(0, (block + 1) * QB) for block in blocks]
            work = []
            for k in range(GROUP):
                head = group * GROUP + k
                start, lanes = head_window(head, depth, width)
                work += [(head, pl.ds(start, WIN), lanes, heres[b], uptos[b]) for b in blocks]
            scores = [nt(jnp.where(lanes, qkv[0, here, cols], 0), qkv[1, upto, cols]) for head, cols, lanes, here, upto in work]
            scores = [jnp.minimum(score, mask[w[3], w[4]]) for score, w in zip(scores, work)]
            tops = [jnp.max(score, axis=-1, keepdims=True) for score in scores]
            expds = [jnp.exp2(score - top) for score, top in zip(scores, tops)]
            sums = [1.0 / jnp.sum(e, axis=-1, keepdims=True) for e in expds]
            softs = [(e * r).astype(jnp.bfloat16) for e, r in zip(expds, sums)]
            for soft, (head, cols, lanes, here, upto) in zip(softs, work):
                prob[head, here, upto] = soft
            mixes = [nn(soft, qkv[2, w[4], w[1]]).astype(jnp.bfloat16) for soft, w in zip(softs, work)]
            for mixed, (head, cols, lanes, here, upto) in zip(mixes, work):
                att[here, cols] = jnp.where(lanes, mixed, att[here, cols])
            return carry
        lax.fori_loop(0, HEADS // GROUP, head_group, 0)
        weight = acquire(use + 3)
        for cols in tiles:
            mid[:, cols] = source[:, cols].astype(f32) + nn(att[...], weight[:, cols])
        after(use + 3)
        low[...] = norm_rows(mid[...], gain_two).astype(b16)
        weight = acquire(use + 4)
        for cols in tiles:
            pre = nn(low[...], weight[:, cols]) + bias_one[:, cols]
            u[:, cols] = pre
            bent = 0.5 * pre * (1.0 + jnp.tanh(GC * (pre + GA * (pre * pre * pre))))
            act[:, cols] = bent.astype(b16)
        after(use + 4)
        weight = acquire(use + 5)
        for cols in tiles:
            out = mid[:, cols] + (nn(act[...], weight[:, cols]) + bias_two[:, cols])
            out_ref[:, cols] = out.astype(b16)
        after(use + 5)

    pieces = (tiles[:3], tiles[3:])
    in_slot = [None, None]

    def put(layer, index, slot):
        first = pieces[slot][0].start
        count = pieces[slot][-1].stop - first
        return pltpu.make_async_copy(
            stage.at[slot, pl.ds(0, count)],
            grads_ref.at[layer, pl.ds(index * width + first, count)],
            out_sems.at[layer, index, slot],
        )

    def weight_grad(layer, index, left_t, right):
        for slot, piece in enumerate(pieces):
            if in_slot[slot] is not None:
                put(*in_slot[slot], slot).wait()
            for cols in piece:
                at = slice(cols.start - piece[0].start, cols.stop - piece[0].start)
                stage[slot, at, :] = nn(left_t(cols), right).astype(b16)
            put(layer, index, slot).start()
            in_slot[slot] = (layer, index)

    def backward(layer, source, dy_ref, out_ref, use):
        qkv, prob, att, mid, u = (ref.at[layer] for ref in (qkvs, probs, atts, mids, us))
        wide, dmid = u, mid
        gain_one, gain_two = vec_ref[layer, 0:1, :], vec_ref[layer, 1:2, :]
        dvec_ref[layer, 3:4, :] = jnp.sum(dy_ref[...].astype(f32), axis=0, keepdims=True)
        weight = acquire(use)
        for cols in tiles:
            pre = u[:, cols]
            square = pre * pre
            bent = jnp.tanh(GC * (pre + GA * (square * pre)))
            half = 0.5 * (1.0 + bent)
            act[:, cols] = (pre * half).astype(b16)
            slope = half + (0.5 * GC) * pre * (1.0 - bent * bent) * (1.0 + (3.0 * GA) * square)
            down = (nt(dy_ref[...], weight[cols, :]) * slope).astype(b16)
            low[:, cols] = down
            dvec_ref[layer, 2:3, cols] = jnp.sum(down.astype(f32), axis=0, keepdims=True)
        after(use)
        weight_grad(layer, 5, lambda cols: act[:, cols].T, dy_ref[...])
        weight = acquire(use + 1)
        for cols in tiles:
            wide[:, cols] = nt(low[...], weight[cols, :])
        after(use + 1)
        act[...] = norm_rows(mid[...], gain_two).astype(b16)
        weight_grad(layer, 4, lambda cols: act[:, cols].T, low[...])
        part, gain_sum = norm_back(mid[...], gain_two, wide[...])
        dvec_ref[layer, 1:2, :] = gain_sum
        total = dy_ref[...].astype(f32) + part
        dmid[...] = total
        low[...] = total.astype(b16)
        weight_grad(layer, 3, lambda cols: att[:, cols].T, low[...])
        weight = acquire(use + 2)
        for cols in tiles:
            act[:, cols] = nt(low[...], weight[cols, :]).astype(b16)
        after(use + 2)
        dqkv[...] = jnp.zeros_like(dqkv)

        def head_group(group, carry):
            blocks = range(rows // QB)
            heres = [slice(block * QB, (block + 1) * QB) for block in blocks]
            uptos = [slice(0, (block + 1) * QB) for block in blocks]
            sinces = [slice(block * QB, rows) for block in blocks]
            work = []
            for k in range(GROUP):
                head = group * GROUP + k
                start, lanes = head_window(head, depth, width)
                work += [(head, pl.ds(start, WIN), lanes, heres[b], uptos[b], sinces[b], k) for b in blocks]
            dprobs = [nt(jnp.where(w[2], act[w[3], w[1]], 0), qkv[2, w[4], w[1]]) for w in work]
            softs = [prob[w[0], w[3], w[4]].astype(f32) for w in work]
            leans = [jnp.sum(dp * soft, axis=-1, keepdims=True) for dp, soft in zip(dprobs, softs)]
            dss = [(soft * (dp - lean)).astype(b16) for dp, soft, lean in zip(dprobs, softs, leans)]
            for ds, w in zip(dss, work):
                dscore[w[6], w[3], w[4]] = ds
            dvs = [tn(prob[w[0], w[5], w[3]], act[w[5], w[1]]).astype(b16) for w in work]
            dqs = [(nn(ds, qkv[1, w[4], w[1]]) * scale).astype(b16) for ds, w in zip(dss, work)]
            dks = [(tn(dscore[w[6], w[5], w[3]], qkv[0, w[5], w[1]]) * LN2).astype(b16) for w in work]
            for dq, dk, dv, w in zip(dqs, dks, dvs, work):
                for index, value in enumerate((dq, dk, dv)):
                    dqkv[index, w[3], w[1]] = jnp.where(w[2], value, dqkv[index, w[3], w[1]])
            return carry
        lax.fori_loop(0, HEADS // GROUP, head_group, 0)
        low[...] = norm_rows(source[...].astype(f32), gain_one).astype(b16)
        for cols in tiles:
            turned[cols, :] = low[:, cols].T
        for index in (2, 1, 0):
            weight_grad(layer, index, lambda cols: turned[cols, :], dqkv[index])
        w_value, w_key, w_query = acquire(use + 3), acquire(use + 4), acquire(use + 5)
        for cols in tiles:
            wide[:, cols] = (
                nt(dqkv[0], w_query[cols, :]) + nt(dqkv[1], w_key[cols, :]) + nt(dqkv[2], w_value[cols, :])
            )
        for k in (3, 4, 5):
            after(use + k)
        part, gain_sum = norm_back(source[...].astype(f32), gain_one, wide[...])
        dvec_ref[layer, 0:1, :] = gain_sum
        dvec_ref[layer, 4:8, :] = jnp.zeros_like(dvec_ref[layer, 4:8, :])
        out_ref[...] = (dmid[...] + part).astype(b16)

    forward(0, x_ref, between)
    forward(1, between, y_ref)
    backward(1, between, cot_ref, dx_ref, 12)
    backward(0, x_ref, dx_ref, dx_ref, 18)
    for slot in range(2):
        put(*in_slot[slot], slot).wait()


def both_layers(mats, x, vec, segc, segr, cot):
    rows, width = x.shape
    f32, b16 = jnp.float32, jnp.bfloat16
    vm = pl.BlockSpec(memory_space=pltpu.VMEM)
    hbm = pl.BlockSpec(memory_space=pl.ANY)
    flat = (rows, width)
    dma = pltpu.SemaphoreType.DMA
    return pl.pallas_call(
        both_layers_kernel,
        out_shape=[
            jax.ShapeDtypeStruct(flat, b16),
            jax.ShapeDtypeStruct(mats.shape, b16),
            jax.ShapeDtypeStruct(flat, b16),
            jax.ShapeDtypeStruct((2, 8, width), f32),
        ],
        in_specs=[hbm, vm, vm, vm, vm, vm],
        out_specs=[vm, hbm, vm, vm],
        scratch_shapes=[
            pltpu.VMEM((SLOTS, width, width), b16),
            pltpu.VMEM((2, 3) + flat, b16),
            pltpu.VMEM((2, HEADS, rows, rows), b16),
            pltpu.VMEM((2,) + flat, b16),
            pltpu.VMEM((2,) + flat, f32),
            pltpu.VMEM((2,) + flat, f32),
            pltpu.VMEM(flat, b16),
            pltpu.VMEM(flat, b16),
            pltpu.VMEM(flat, b16),
            pltpu.VMEM((rows, rows), f32),
            pltpu.VMEM((3,) + flat, b16),
            pltpu.VMEM((GROUP, rows, rows), b16),
            pltpu.VMEM((width, rows), b16),
            pltpu.VMEM((2, 3 * WIN, width), b16),
            dma((len(plan_loads()),)),
            dma((2, 6, 2)),
        ],
        compiler_params=pltpu.CompilerParams(
            vmem_limit_bytes=63 * 2**20,
        ),
        name="both_layers",
    )(mats, x, vec, segc, segr, cot)


def give_back(s, d, me, peers, sendbuf, returned, local_sem, send_sem, recv_sem):
    total = 2 * peers
    keep = pltpu.make_async_copy(sendbuf.at[s, d], returned.at[me], local_sem)
    keep.start()

    def give(step, carry):
        other = lax.rem(me + step, total)
        sec, dp = other // peers, lax.rem(other, peers)
        pltpu.make_async_remote_copy(
            sendbuf.at[sec, dp], returned.at[me], send_sem, recv_sem,
            device_id=(sec, dp), device_id_type=MESH,
        ).start()
        return carry

    lax.fori_loop(1, total, give, 0)

    def finish():
        keep.wait()
        bulk_copy(returned, total - 1, send_sem, recv_sem).wait_recv()
        bulk_copy(returned, total - 1, send_sem, recv_sem).wait_send()

    return finish


def rs_kernel(parts,zn,g_ref,v_ref,dx_ref,y_ref,place_ref,picks_ref,o_ref,vo_ref,res_ref,land,buf,obuf,vland,strips32,sendbuf,returned,*rest):
    nP=len(parts)
    lks=rest[:nP]
    ssem,rsem,cs,cr,lsem,osem,vsend,vrecv,tlocal,tsend,trecv=rest[nP:]
    s,d,z,y,c=coords()
    peers=4*zn
    total_dev=2*peers
    me=s*peers+d
    greet(total_dev,me,peers)
    vland[me]=v_ref[me]
    def small(step,carry):
        other=lax.rem(me+step,total_dev)
        pltpu.make_async_remote_copy(v_ref.at[other],vland.at[me],vsend,vrecv,device_id=(other//peers,lax.rem(other,peers)),device_id_type=MESH).start()
        return carry
    lax.fori_loop(1,total_dev,small,0)
    sib=(s,(z*2+y)*2+1-c)
    def where(it):
        s2=1-s if it[0] else s
        y2=1-y if it[1] else y
        return s2,z+it[2],y2
    def conds(it):
        cl=[]
        if it[2]<0: cl.append(z+it[2]>=0)
        if it[2]>0: cl.append(z+it[2]<=zn-1)
        return cl
    def guarded(cl,fn):
        if not cl: fn(); return
        e=cl[0]
        for q in cl[1:]: e=jnp.logical_and(e,q)
        pl.when(e)(fn)
    def slot_base(order):
        sizes={"x":2,"y":2,"z":zn}
        base={};cur=0
        for k,dim in enumerate(order):
            n=1
            for q in order[k+1:]: n*=sizes[q]
            if dim=="z": n*=2*zn
            base[dim]=cur; cur+=n
        return base,cur
    def slot(p,dim,side,dest):
        order=parts[p][2][::-1]
        base,_=slot_base(order)
        k=order.index(dim)
        v={"x":dest[0],"z":dest[1],"y":dest[2]}
        idx=0
        for q in order[k+1:]:
            idx=idx*(zn if q=="z" else 2)+v[q]
        if dim=="z": idx=(idx*zn+dest[1])*2+side
        return base[dim]+idx
    evs=[]
    for p in range(nP):
        for it in items():
            if abs(it[2])<=zn-1: evs.append((-hops(it),p,it))
    evs.sort(key=lambda e:e[0])
    seq=[(p,it) for _,p,it in evs]
    def core_dsc(p,it,mine):
        r0,rn,_=parts[p]
        s2,z2,y2=where(it)
        idx=(s2*zn+z2)*2+y2
        cc=c if mine else 1-c
        return pltpu.make_async_remote_copy(g_ref.at[s2,(z2*2+y2)*2+cc,pl.ds(r0,rn)],land.at[idx,pl.ds(r0,rn)],cs.at[p,idx],cr.at[p,idx],device_id=sib,device_id_type=MESH)
    for p,it in seq:
        guarded(conds(it),lambda p=p,it=it: core_dsc(p,it,False).start())
    for kind,ref in enumerate((dx_ref,y_ref)):
        cut_strips(place_ref[...],ref,strips32)
        sendbuf[kind]=strips32[...].astype(jnp.bfloat16)
    def load(i):
        p,it=seq[i]
        r0,rn,_=parts[p]
        s2,z2,y2=where(it)
        return pltpu.make_async_copy(g_ref.at[s2,(z2*2+y2)*2+c,pl.ds(r0,rn)],buf.at[i%NB,pl.ds(0,rn)],lsem.at[i%NB])
    NB=buf.shape[0]
    for i in range(min(NB-1,len(seq))):
        guarded(conds(seq[i][1]),lambda i=i: load(i).start())
    def contribs(p,it):
        order=parts[p][2][::-1]
        diff={"x":it[0],"y":it[1],"z":it[2]}
        out=[];nxt=None
        for dim in order:
            if dim=="z":
                if it[2]==0: out+=[("z",0,z>0),("z",1,z<zn-1)]
                elif it[2]>0: out.append(("z",0,z>0))
                else: out.append(("z",1,z<zn-1))
                if it[2]!=0: nxt="r" if it[2]>0 else "l"; break
            else:
                if diff[dim]: nxt=dim; break
                out.append((dim,0,None))
        return out,nxt
    semoff=[0]
    for p in range(nP): semoff.append(semoff[-1]+slot_base(parts[p][2][::-1])[1])
    def out_dsc(p,it,nxt):
        r0,rn,_=parts[p]
        dest=where(it)
        s2,z2,y2=dest
        idx=(s2*zn+z2)*2+y2
        dim="z" if nxt in "lr" else nxt
        side=1 if nxt=="l" else 0
        sl=slot(p,dim,side,dest)
        dev={"x":(1-s,d),"y":(s,(z*2+1-y)*2+c),"l":(s,d-4),"r":(s,d+4)}[nxt]
        return pltpu.make_async_remote_copy(land.at[idx,pl.ds(r0,rn)],lks[p].at[sl],ssem.at[p,idx],rsem.at[semoff[p]+sl],device_id=dev,device_id_type=MESH)
    def settle():
        rest_of=vland.at[pl.ds(0,total_dev-1)]
        bulk=pltpu.make_async_remote_copy(rest_of,rest_of,vsend,vrecv,device_id=(0,0),device_id_type=MESH)
        bulk.wait_recv()
        bulk.wait_send()
        vo_ref[...]=jnp.sum(vland[...],axis=0)
        back()
        for batch in range(2):
            strips32[...]=returned[batch*peers:(batch+1)*peers].astype(jnp.float32)
            join_strips(picks_ref[batch],strips32,res_ref.at[batch])
    for i,(p,it) in enumerate(seq):
        r0,rn,_=parts[p]
        if i==len(seq)*GIVE_NUM//GIVE_DEN: back=give_back(s,d,me,peers,sendbuf,returned,tlocal,tsend,trecv)
        if i==len(seq)*SETTLE_NUM//SETTLE_DEN: settle()
        if i+NB-1<len(seq):
            guarded(conds(seq[i+NB-1][1]),lambda i=i: load(i+NB-1).start())
        def ev(i=i,p=p,it=it,r0=r0,rn=rn):
            dest=where(it)
            s2,z2,y2=dest
            idx=(s2*zn+z2)*2+y2
            con,nxt=contribs(p,it)
            lk=lks[p]
            load(i).wait()
            core_dsc(p,it,True).wait_recv()
            plain=[x for x in con if x[2] is None]
            cond=[x for x in con if x[2] is not None]
            def rdsc(dim,side):
                sl=slot(p,dim,side,dest)
                return pltpu.make_async_remote_copy(lk.at[sl],lk.at[sl],ssem.at[p,idx],rsem.at[semoff[p]+sl],device_id=sib,device_id_type=MESH),sl
            for dim,side,_ in plain: rdsc(dim,side)[0].wait_recv()
            for dim,side,cnd in cond:
                pl.when(cnd)(lambda dim=dim,side=side: rdsc(dim,side)[0].wait_recv())
            if not cond: variants=[(None,plain)]
            elif len(cond)==1:
                variants=[(cond[0][2],plain+cond),(jnp.logical_not(cond[0][2]),plain)]
            else:
                a,b=cond
                variants=[(jnp.logical_and(a[2],b[2]),plain+cond),(jnp.logical_and(a[2],jnp.logical_not(b[2])),plain+[a]),
                          (jnp.logical_and(jnp.logical_not(a[2]),b[2]),plain+[b])]
            def total(lst):
                slots=[slot(p,dim,side,dest) for dim,side,_ in lst]
                CH=16
                def body(k,_):
                    ro=pl.multiple_of(k*CH,CH)
                    acc=buf[i%NB,pl.ds(ro,CH),:].astype(jnp.float32)+land[idx,pl.ds(r0+ro,CH),:].astype(jnp.float32)
                    for sl in slots: acc=acc+lk[sl,pl.ds(ro,CH),:].astype(jnp.float32)
                    if nxt is None: obuf[pl.ds(r0+ro,CH),:]=acc
                    else: land[idx,pl.ds(r0+ro,CH),:]=acc.astype(jnp.bfloat16)
                    return 0
                lax.fori_loop(0,rn//CH,body,0)
            for cnd,lst in variants:
                if cnd is None: total(lst)
                else: pl.when(cnd)(lambda lst=lst: total(lst))
            if nxt is not None: out_dsc(p,it,nxt).start()
            else: pltpu.make_async_copy(obuf.at[pl.ds(r0,rn)],o_ref.at[pl.ds(r0,rn)],osem.at[p]).start()
        guarded(conds(it),ev)
    for p,it in seq:
        def fin(p=p,it=it):
            core_dsc(p,it,False).wait_send()
            nxt=contribs(p,it)[1]
            if nxt is not None: out_dsc(p,it,nxt).wait_send()
        guarded(conds(it),fin)
    for p,(r0,rn,_) in enumerate(parts):
        pltpu.make_async_copy(obuf.at[pl.ds(r0,rn)],o_ref.at[pl.ds(r0,rn)],osem.at[p]).wait()


def slot_count(order,zn):
    sizes={"x":2,"y":2,"z":zn};cur=0
    for k,dim in enumerate(order):
        n=1
        for q in order[k+1:]: n*=sizes[q]
        if dim=="z": n*=2*zn
        cur+=n
    return cur
def rs(g,v,dx,y,place,picks,block,parts,zn,cid=1,nb=4):
    n=len(parts)
    cnt=[slot_count(p[2][::-1],zn) for p in parts]
    mx=max(p[1] for p in parts)
    return pl.pallas_call(functools.partial(rs_kernel,parts,zn),
        out_shape=[jax.ShapeDtypeStruct((480,1280),jnp.float32),jax.ShapeDtypeStruct(v.shape[1:],jnp.float32),
            jax.ShapeDtypeStruct((2,)+dx.shape,jnp.bfloat16)],
        in_specs=[pl.BlockSpec(memory_space=pl.ANY)]+[pl.BlockSpec(memory_space=pltpu.VMEM)]*5,
        out_specs=[pl.BlockSpec(memory_space=pl.ANY)]+[pl.BlockSpec(memory_space=pltpu.VMEM)]*2,
        scratch_shapes=[pltpu.VMEM((4*zn,480,1280),jnp.bfloat16),pltpu.VMEM((nb,mx,1280),jnp.bfloat16),pltpu.VMEM((480,1280),jnp.float32),pltpu.VMEM(v.shape,jnp.float32),
            pltpu.VMEM((4*zn,)+block,jnp.float32),pltpu.VMEM((2,4*zn)+block,jnp.bfloat16),pltpu.VMEM((8*zn,)+block,jnp.bfloat16)]
          +[pltpu.VMEM((cnt[p],parts[p][1],1280),jnp.bfloat16) for p in range(n)]
          +[pltpu.SemaphoreType.DMA((n,4*zn)),pltpu.SemaphoreType.DMA((sum(cnt),)),
          pltpu.SemaphoreType.DMA((n,4*zn)),pltpu.SemaphoreType.DMA((n,4*zn)),pltpu.SemaphoreType.DMA((nb,)),pltpu.SemaphoreType.DMA((n,))]+[pltpu.SemaphoreType.DMA]*5,
        compiler_params=pltpu.CompilerParams(collective_id=cid,has_side_effects=True,vmem_limit_bytes=62*2**20))(g,v,dx,y,place,picks)


def as_row(column):
    rows = column.shape[0]
    return jnp.broadcast_to(column, (rows, 128)).T[0:1, :]


def as_column(row):
    size = row.shape[1]
    return jnp.broadcast_to(row, (128, size)).T[:, 0:1]


def ones_where(flag):
    return jnp.where(flag, 1.0, 0.0)


def gather_events(parts,zn,place,own,w_ref,ssem,rsem,cs,cr):
    s,d,z,y,c=place
    KIND={"x":0,"y":1,"l":2,"r":3}
    def where(it):
        s2=1-s if it[0] else s
        y2=1-y if it[1] else y
        z2=z+it[2]
        return s2,z2,y2
    def dsc(p,it,kind):
        r0,rn,order=parts[p]
        s2,z2,y2=where(it)
        idx=s2*(2*zn)+z2*2+y2
        is_own=it==(0,0,0)
        src=own.at[pl.ds(r0,rn)] if is_own else w_ref.at[s2,(z2*2+y2)*2+c,pl.ds(r0,rn)]
        dst=w_ref.at[s2,(z2*2+y2)*2+c,pl.ds(r0,rn)]
        if kind=="core":
            dev=(s,(z*2+y)*2+1-c)
            return pltpu.make_async_remote_copy(src,dst,cs.at[p,idx],cr.at[p,idx],device_id=dev,device_id_type=MESH)
        dev={"x":(1-s,d),"y":(s,(z*2+1-y)*2+c),"l":(s,d-4),"r":(s,d+4)}[kind]
        return pltpu.make_async_remote_copy(src,dst,ssem.at[KIND[kind],p,idx],rsem.at[p,idx],device_id=dev,device_id_type=MESH)
    def cdsc(p,it):
        r0,rn,order=parts[p]
        s2,z2,y2=where(it)
        idx=s2*(2*zn)+z2*2+y2
        dst=w_ref.at[s2,(z2*2+y2)*2+1-c,pl.ds(r0,rn)]
        return pltpu.make_async_remote_copy(dst,dst,cs.at[p,idx],cr.at[p,idx],device_id=(s,(z*2+y)*2+1-c),device_id_type=MESH)
    def conds(it,kind):
        cs_=[]
        if it[2]<0: cs_.append(z+it[2]>=0)
        if it[2]>0: cs_.append(z+it[2]<=zn-1)
        if kind=="l": cs_.append(z>0)
        if kind=="r": cs_.append(z<zn-1)
        return cs_
    def guarded(cl,fn):
        if not cl: fn(); return
        e=cl[0]
        for q in cl[1:]: e=jnp.logical_and(e,q)
        pl.when(e)(fn)
    def sends(p,it):
        order=parts[p][2]
        a=arrival(order,it)
        ks=[]
        if a is not None and order[a]=="z": ks.append("l" if it[2]>0 else "r")
        for dim in order[(a+1) if a is not None else 0:]:
            ks += ["r","l"] if dim=="z" else [dim]
        ks.append("core")
        return ks
    evs=[]
    for p in range(len(parts)):
        for it in items():
            if abs(it[2])<zn: evs.append((hops(it),p,it))
    evs.sort(key=lambda e:e[0])
    first=[]
    later=[]
    for h,p,it in evs:
        def ev(p=p,it=it):
            if it!=(0,0,0): dsc(p,it,"x").wait_recv()
            for k in sends(p,it):
                guarded(conds((0,0,0),k), lambda k=k: dsc(p,it,k).start())
        (later if h else first).append(lambda it=it,ev=ev: guarded(conds(it,None),ev))
    def finish():
        for _,p,it in evs:
            def fin(p=p,it=it):
                cdsc(p,it).wait_recv()
                for k in sends(p,it):
                    guarded(conds((0,0,0),k), lambda k=k: dsc(p,it,k).wait_send())
            guarded(conds(it,None),fin)
    return first,later,finish


def enter_kernel(
    parts, zn, mats_ref, packet_ref, deal_ref, tokens_ref,
    w_ref, shared_ref, x_ref, cot_ref, picks_ref, place_ref,
    own, wide_rows, strips32, sendbuf, landed, order,
    own_sem, lsem, ssem, rsem, cs, cr, psend, precv, tsend, trecv,
):
    s, d, z, y, c = coords()
    peers = 4 * zn
    total = 2 * peers
    me = s * peers + d
    batches, rows, width = tokens_ref.shape
    f32, b16 = jnp.float32, jnp.bfloat16
    cast_in = pltpu.make_async_copy(mats_ref, wide_rows, own_sem)
    cast_in.start()
    greet(total, me, peers)
    shared_ref[me] = packet_ref[...]

    def tell(step, carry):
        other = lax.rem(me + step, total)
        pltpu.make_async_remote_copy(
            packet_ref, shared_ref.at[me], psend, precv,
            device_id=(other // peers, lax.rem(other, peers)), device_id_type=MESH,
        ).start()
        return carry

    lax.fori_loop(1, total, tell, 0)
    cast_in.wait()
    own[...] = wide_rows[...].astype(b16)
    lc = pltpu.make_async_copy(own, w_ref.at[s, d], lsem)
    lc.start()
    start_events, rest_events, finish = gather_events(
        parts, zn, (s, d, z, y, c), own, w_ref, ssem, rsem, cs, cr
    )
    for event in start_events:
        event()
    sub = lax.broadcasted_iota(jnp.int32, (rows, rows), 0).astype(f32)
    lane = lax.broadcasted_iota(jnp.int32, (rows, rows), 1).astype(f32)
    mine_row = jnp.where(s == 0, deal_ref[0:1, :], deal_ref[1:2, :])
    mine_col = as_column(mine_row)
    rank_col = jnp.sum(ones_where(mine_row < mine_col), axis=1, keepdims=True)
    order[...] = ones_where(lane == rank_col).astype(b16)
    rank_row = jnp.sum(ones_where(mine_col < mine_row), axis=0, keepdims=True)
    place_ref[...] = ones_where(sub == rank_row).astype(b16)
    rest = shared_ref.at[pl.ds(0, total - 1)]
    bulk = pltpu.make_async_remote_copy(
        rest, rest, psend, precv, device_id=(0, 0), device_id_type=MESH
    )
    bulk.wait_recv()
    index_col = lax.broadcasted_iota(jnp.int32, (rows, 1), 0).astype(f32)
    ids_col = index_col + (d * rows).astype(f32)
    for batch in range(batches):

        def look(block, found):
            known = shared_ref[s * peers + block]
            for line in range(rows // 128):
                at = batch * (rows // 128) + line
                found = jnp.where(ids_col == known[at : at + 1, :], block.astype(f32), found)
            return found

        found = lax.fori_loop(0, peers, look, jnp.zeros((rows, 128), f32))
        key_col = jnp.sum(found, axis=1, keepdims=True) * rows + index_col
        key_row = as_row(key_col)
        rank_row = jnp.sum(ones_where(key_col < key_row), axis=0, keepdims=True)
        rank_col = jnp.sum(ones_where(key_row < key_col), axis=1, keepdims=True)
        picks_ref[batch] = ones_where(lane == rank_col).astype(b16)
        pick = ones_where(sub == rank_row).astype(b16)
        cut_strips(pick, tokens_ref.at[batch], strips32)
        sendbuf[batch] = strips32[...].astype(b16)

    landed[me] = sendbuf[s, d]

    early = len(rest_events) * HAND_NUM // HAND_DEN
    for event in rest_events[:early]:
        event()

    def give(step, carry):
        other = lax.rem(me + step, total)
        sec, dp = other // peers, lax.rem(other, peers)
        pltpu.make_async_remote_copy(
            sendbuf.at[sec, dp], landed.at[me], tsend, trecv.at[s],
            device_id=(sec, dp), device_id_type=MESH,
        ).start()
        return carry

    lax.fori_loop(1, total, give, 0)
    def take(kind, out_ref):
        pl.when(s == kind)(
            lambda: bulk_copy(landed, peers - 1, tsend, trecv.at[kind]).wait_recv()
        )
        pl.when(s != kind)(lambda: bulk_copy(landed, peers, tsend, trecv.at[kind]).wait_recv())
        strips32[...] = landed[pl.ds(kind * peers, peers)].astype(f32)
        join_strips(order[...], strips32, out_ref)

    middle = len(rest_events) * TAKE_NUM // TAKE_DEN
    for event in rest_events[early:middle]:
        event()
    take(0, x_ref)
    take(1, cot_ref)
    for event in rest_events[middle:]:
        event()
    finish()
    lc.wait()
    bulk.wait_send()
    most = landed.at[pl.ds(0, total - 1)]
    pltpu.make_async_remote_copy(
        most, most, tsend, trecv.at[0], device_id=(0, 0), device_id_type=MESH
    ).wait_send()


def enter(mats, packet, deal, tokens, parts, zn):
    n = len(parts)
    peers = 4 * zn
    batches, rows, width = tokens.shape
    strip_rows = rows // peers * (width // 128)
    f32, b16 = jnp.float32, jnp.bfloat16
    vm = pl.BlockSpec(memory_space=pltpu.VMEM)
    hbm = pl.BlockSpec(memory_space=pl.ANY)
    dma = pltpu.SemaphoreType.DMA
    return pl.pallas_call(
        functools.partial(enter_kernel, parts, zn),
        out_shape=[
            jax.ShapeDtypeStruct((2, peers) + mats.shape, b16),
            jax.ShapeDtypeStruct((2 * peers,) + packet.shape, f32),
            jax.ShapeDtypeStruct((rows, width), b16),
            jax.ShapeDtypeStruct((rows, width), b16),
            jax.ShapeDtypeStruct((batches, rows, rows), b16),
            jax.ShapeDtypeStruct((rows, rows), b16),
        ],
        in_specs=[hbm, vm, vm, vm],
        out_specs=[hbm, vm, vm, vm, vm, vm],
        scratch_shapes=[
            pltpu.VMEM(mats.shape, b16),
            pltpu.VMEM(mats.shape, f32),
            pltpu.VMEM((peers, strip_rows, 128), f32),
            pltpu.VMEM((batches, peers, strip_rows, 128), b16),
            pltpu.VMEM((2 * peers, strip_rows, 128), b16),
            pltpu.VMEM((rows, rows), b16),
            dma, dma, dma((4, n, peers)), dma((n, peers)), dma((n, peers)), dma((n, peers)),
            dma, dma, dma, dma((2,)),
        ],
        compiler_params=pltpu.CompilerParams(
            collective_id=0, has_side_effects=True, vmem_limit_bytes=VMEM_LIMIT
        ),
        name="enter",
    )(mats, packet, deal, tokens)


def one_hot(rank):
    rows = rank.shape[0]
    return (rank[None, :] == jnp.arange(rows, dtype=jnp.int32)[:, None]).astype(jnp.bfloat16)


def rank_of(key):
    return jnp.sum((key[None, :] < key[:, None]).astype(jnp.int32), axis=1)


def padded(flat):
    lead, size = flat.shape
    full = -(-size // 1024) * 1024
    return jnp.pad(flat, ((0, 0), (0, full - size))).reshape(lead, full // 128, 128)


def enter_plain(own, packet, deal, tokens, peers):
    section = lax.axis_index("section")
    batches, rows, width = tokens.shape
    per_peer = rows // peers
    shared = lax.all_gather(packet, BOTH, axis=0)
    low = own.astype(jnp.bfloat16)
    mats = lax.all_gather(low, BOTH, axis=0, tiled=True).reshape((2, peers) + own.shape)
    flat = shared.reshape(2, peers, -1)[:, :, : batches * rows]
    dealt = jnp.where(section == 0, flat[0], flat[1]).astype(jnp.int32).reshape(peers, batches, rows)
    own_rows = lax.axis_index("dp") * rows + jnp.arange(rows, dtype=jnp.int32)
    blocks = jnp.arange(peers, dtype=jnp.int32)
    picks = []
    sends = []
    for batch in range(batches):
        hit = dealt[:, batch][None, :, :] == own_rows[:, None, None]
        target = jnp.sum(jnp.where(hit, blocks[None, :, None], 0), axis=(1, 2))
        pick = one_hot(rank_of(target * rows + jnp.arange(rows, dtype=jnp.int32)))
        picks.append(pick.T)
        sends.append(nn(pick, tokens[batch]).astype(jnp.bfloat16))
    outgoing = jnp.stack(sends).reshape(2 * peers, per_peer, width)
    arrived = lax.all_to_all(outgoing, BOTH, split_axis=0, concat_axis=0, tiled=True)
    arrived = arrived.reshape(2, rows, width)
    place = one_hot(rank_of(jnp.where(section == 0, deal[0], deal[1])))
    x, cot = (tn(place, arrived[kind]).astype(jnp.bfloat16) for kind in range(2))
    return mats, shared, x, cot, jnp.stack(picks), place


def leave_plain(terms, small, down, final, place, picks, peers):
    sections, _, rows, width = terms.shape
    terms = terms.reshape(sections * peers * rows, width)
    total = lax.psum_scatter(terms, BOTH, scatter_dimension=0, tiled=True).astype(jnp.float32)
    small = lax.psum_scatter(small, BOTH, scatter_dimension=0, tiled=True)[0]
    back = jnp.stack([nn(place, down), nn(place, final)]).astype(jnp.bfloat16)
    count = down.shape[0]
    back = back.reshape(2 * peers, count // peers, width)
    back = lax.all_to_all(back, BOTH, split_axis=0, concat_axis=0, tiled=True)
    back = back.reshape(-1, count, width)
    results = jnp.stack([nn(picks[batch], back[batch]) for batch in range(back.shape[0])])
    return total, small, results.astype(jnp.bfloat16)


def local(entering, deal, seq_lens, mats, gains, biases):
    section = lax.axis_index("section")
    peers = lax.axis_size("dp")
    arrival = entering[0]
    batches, rows, width = arrival.shape
    per = 2 * width // peers
    vecs = jnp.concatenate([gains[0], biases[0]]).astype(jnp.bfloat16).astype(jnp.float32)
    packet = jnp.concatenate([deal.reshape(-1).astype(jnp.float32), vecs])
    packet = padded(packet[None])[0]
    packet = jnp.pad(packet, ((0, -packet.shape[0] % 8), (0, 0)))
    args = (mats[0], packet, deal.astype(jnp.float32), arrival)
    direct = peers == 16
    entered = enter(*args, GATHER_PARTS, peers // 4) if direct else enter_plain(*args, peers)
    all_mats, shared, tokens, cotangent, picks, place = entered
    shared = shared.reshape(2, peers, -1)
    small = shared[:, :, batches * rows : batches * rows + 2 * per].reshape(2, peers, 2, per)
    small = jnp.swapaxes(small, 1, 2).reshape(2, 4, width)
    small = jnp.pad(small, ((0, 0), (0, 4), (0, 0)))
    all_mats = all_mats.reshape(2, 6 * width, width)
    lens = jnp.where(section == 0, seq_lens[0, 0], seq_lens[1, 0])
    ends = jnp.cumsum(lens)
    positions = jnp.arange(rows, dtype=jnp.int32)
    segment = jnp.sum((positions[:, None] >= ends[None, :]).astype(jnp.int32), axis=1)
    segc, segr = segment[:, None], segment[None]
    final, terms, down, vec_grads = both_layers(
        all_mats, tokens, small, segc, segr, cotangent
    )
    terms = terms.reshape(2, peers, -1, width)
    vec_terms = vec_grads[:, :4].reshape(2, 2, peers, per)
    vec_terms = padded(jnp.swapaxes(vec_terms, 1, 2).reshape(2 * peers, 2 * per))
    block = (rows // peers * (width // 128), 128)
    if direct:
        shard_mats, vec_total, results = rs(
            terms, vec_terms, down, final, place, picks, block, SCATTER_PARTS, peers // 4
        )
    else:
        shard_mats, vec_total, results = leave_plain(
            terms, vec_terms, down, final, place, picks, peers
        )
    vec_total = vec_total.reshape(-1)
    return (
        results[None],
        shard_mats[None],
        vec_total[None, :per],
        vec_total[None, per : 2 * per],
    )


def solution(mesh):
    in_specs = (
        P("section", None, "dp", None),
        P(None, "dp"),
        P(None, "dp", None),
        P("section", "dp", None),
        P("section", "dp"),
        P("section", "dp"),
    )
    out_specs = (
        P("section", None, "dp", None),
        P("section", "dp", None),
        P("section", "dp"),
        P("section", "dp"),
    )
    return jax.shard_map(local, mesh=mesh, in_specs=in_specs, out_specs=out_specs, check_vma=False)
```

```python
import functools

import jax
import jax.numpy as jnp
from jax import lax
from jax.experimental import pallas as pl
from jax.experimental.pallas import tpu as pltpu
from jax.sharding import PartitionSpec as P

HEADS = 16
EPS = 1e-06
NEG = -1000000000.0
BOTH = ("section", "dp")
MESH = pl.DeviceIdType.MESH
GATHER_PARTS = ((0, 112, "zxy"), (112, 112, "zyx"), (224, 128, "xzy"), (352, 128, "yzx"))
SCATTER_PARTS = ((0, 112, "zxy"), (112, 112, "zyx"), (224, 128, "xzy"), (352, 128, "yzx"))
TAKE_NUM, TAKE_DEN = 3, 4
SETTLE_NUM, SETTLE_DEN = 7, 8
GIVE_NUM, GIVE_DEN = 0, 1
HAND_NUM, HAND_DEN = 0, 1


WIN = 256
QB = 128
GROUP = 4
LOG2E = 1.4426950408889634
LN2 = 0.6931471805599453
GC = 0.7978845608028654
GA = 0.044715
VMEM_LIMIT = 62 * 2**20


def nn(left, right):
    return jnp.dot(left, right, preferred_element_type=jnp.float32)


def nt(left, right):
    return lax.dot_general(
        left, right, (((1,), (1,)), ((), ())), preferred_element_type=jnp.float32
    )


def tn(left, right):
    return lax.dot_general(
        left, right, (((0,), (0,)), ((), ())), preferred_element_type=jnp.float32
    )


def head_window(head, depth, width):
    start = jnp.minimum((head * depth) // 128, (width - WIN) // 128) * 128
    start = pl.multiple_of(start, 128)
    lane = lax.broadcasted_iota(jnp.int32, (1, WIN), 1) + (start - head * depth)
    return start, (lane >= 0) & (lane < depth)


def norm_rows(value, gain):
    return value * lax.rsqrt(jnp.mean(value * value, axis=-1, keepdims=True) + EPS) * gain


def norm_back(value, gain, down):
    inv = lax.rsqrt(jnp.mean(value * value, axis=-1, keepdims=True) + EPS)
    unit = value * inv
    scaled = down * gain
    lean = jnp.mean(scaled * unit, axis=-1, keepdims=True)
    return inv * (scaled - unit * lean), jnp.sum(down * unit, axis=0, keepdims=True)


def signal_all(total, me, peers):
    barrier = pltpu.get_barrier_semaphore()

    def one(step, carry):
        other = lax.rem(me + step, total)
        pl.semaphore_signal(
            barrier, inc=1, device_id=(other // peers, lax.rem(other, peers)), device_id_type=MESH
        )
        return carry

    lax.fori_loop(1, total, one, 0)


def wait_all(total):
    pl.semaphore_wait(pltpu.get_barrier_semaphore(), total - 1)


def greet(total, me, peers):
    signal_all(total, me, peers)
    wait_all(total)


def cut_strips(pick, source, strips32):
    peers = strips32.shape[0]
    strips = source.shape[-1] // 128
    each = strips32.shape[1] // strips
    for strip in range(strips):
        part = nn(pick, source[:, strip * 128 : (strip + 1) * 128])
        strips32[:, strip * each : (strip + 1) * each, :] = part.reshape(peers, each, 128)


def join_strips(order, strips32, out_ref):
    peers = strips32.shape[0]
    strips = out_ref.shape[-1] // 128
    each = strips32.shape[1] // strips
    for strip in range(strips):
        part = strips32[:, strip * each : (strip + 1) * each, :].reshape(peers * each, 128)
        part = nn(order, part.astype(jnp.bfloat16)).astype(jnp.bfloat16)
        out_ref[:, strip * 128 : (strip + 1) * 128] = part


def bulk_copy(ref, count, send_sem, recv_sem):
    some = ref.at[pl.ds(0, count)]
    return pltpu.make_async_remote_copy(
        some, some, send_sem, recv_sem, device_id=(0, 0), device_id_type=MESH
    )


def coords():
    s=lax.axis_index("section"); d=lax.axis_index("dp")
    return s,d,d//4,(d//2)%2,d%2

def items():
    out=[]
    for bx in (0,1):
        for by in (0,1):
            for dz in (0,-1,1,-2,2,-3,3):
                out.append((bx,by,dz))
    return out
def hops(it): return it[0]+it[1]+abs(it[2])
def arrival(order,it):
    diff={"x":it[0]!=0,"y":it[1]!=0,"z":it[2]!=0}
    last=None
    for k,dim in enumerate(order):
        if diff[dim]: last=k
    return last

def neighbours(s,d,z,y,c,zn):
    return [(None,(1-s,d)),(None,(s,(z*2+1-y)*2+c)),(None,(s,(z*2+y)*2+1-c)),(z>0,(s,d-4)),(z<zn-1,(s,d+4))]


SLOTS = 4
USES = (
    [(0, index) for index in range(6)] + [(1, index) for index in range(6)]
    + [(1, index) for index in (5, 4, 3, 2, 1, 0)] + [(0, index) for index in (5, 4, 3, 2, 1, 0)]
)


def plan_loads():
    def next_use(what, since):
        return next((t for t in range(since, len(USES)) if USES[t] == what), len(USES))

    held = [None] * SLOTS
    loads = []
    for done in range(-1, len(USES)):
        for t in range(done + 1, len(USES)):
            if USES[t] in held:
                continue
            away = [next_use(what, done + 1) if what else len(USES) + 1 for what in held]
            slot = max(range(SLOTS), key=lambda k: away[k])
            if away[slot] <= t:
                break
            held[slot] = USES[t]
            loads.append((done, t, slot))
    return loads


def both_layers_kernel(*refs):
    mats_ref, x_ref, vec_ref, lens_ref, cot_ref = refs[:5]
    y_ref, grads_ref, dx_ref, dvec_ref = refs[5:9]
    (
        held, qkvs, probs, atts, mids, us, between, act, low, mask, dqkv, dscore, turned,
    stage, sems, out_sems,
    ) = refs[9:]
    rows, width = x_ref.shape
    depth = width // HEADS
    scale = depth ** (-0.5)
    f32, b16 = jnp.float32, jnp.bfloat16
    tiles = [slice(c, c + WIN) for c in range(0, width, WIN)]
    loads = plan_loads()
    pending = {}

    def load(number):
        done, use, slot = loads[number]
        layer, index = USES[use]
        return pltpu.make_async_copy(
            mats_ref.at[layer, pl.ds(index * width, width)], held.at[slot], sems.at[number]
        )

    def after(done):
        for number, (when, use, slot) in enumerate(loads):
            if when == done:
                load(number).start()
                pending[slot] = number

    def acquire(use):
        number = max(
            k for k, (when, first, slot) in enumerate(loads) if USES[first] == USES[use] and first <= use
        )
        slot = loads[number][2]
        if pending.get(slot) == number:
            load(number).wait()
            pending.pop(slot)
        return held.at[slot]

    after(-1)
    batch = lax.axis_index("section")
    row = lax.broadcasted_iota(jnp.int32, (rows, 1), 0)
    col = lax.broadcasted_iota(jnp.int32, (1, rows), 1)
    end = jnp.int32(0)
    row_part, col_part = jnp.zeros((rows, 1), jnp.int32), jnp.zeros((1, rows), jnp.int32)
    for place in range(lens_ref.shape[1]):
        end = end + lens_ref[batch, place]
        row_part = row_part + jnp.where(row >= end, 1, 0)
        col_part = col_part + jnp.where(col >= end, 1, 0)
    mask[...] = jnp.where((row_part == col_part) & (col <= row), 3e38, NEG)

    def forward(layer, source, out_ref):
        qkv, prob, att, mid, u = (ref.at[layer] for ref in (qkvs, probs, atts, mids, us))
        gain_one, gain_two = vec_ref[layer, 0:1, :], vec_ref[layer, 1:2, :]
        bias_one, bias_two = vec_ref[layer, 2:3, :], vec_ref[layer, 3:4, :]
        use = 6 * layer
        low[...] = norm_rows(source[...].astype(f32), gain_one).astype(b16)
        for index in range(3):
            weight = acquire(use + index)
            for cols in tiles:
                part = nn(low[...], weight[:, cols])
                if index == 0:
                    part = part * (scale * LOG2E)
                qkv[index, :, cols] = part.astype(b16)
            after(use + index)

        def head_group(group, carry):
            blocks = range(rows // QB)
            heres = [slice(block * QB, (block + 1) * QB) for block in blocks]
            uptos = [slice(0, (block + 1) * QB) for block in blocks]
            work = []
            for k in range(GROUP):
                head = group * GROUP + k
                start, lanes = head_window(head, depth, width)
                work += [(head, pl.ds(start, WIN), lanes, heres[b], uptos[b]) for b in blocks]
            scores = [nt(jnp.where(lanes, qkv[0, here, cols], 0), qkv[1, upto, cols]) for head, cols, lanes, here, upto in work]
            scores = [jnp.minimum(score, mask[w[3], w[4]]) for score, w in zip(scores, work)]
            tops = [jnp.max(score, axis=-1, keepdims=True) for score in scores]
            expds = [jnp.exp2(score - top) for score, top in zip(scores, tops)]
            sums = [1.0 / jnp.sum(e, axis=-1, keepdims=True) for e in expds]
            softs = [(e * r).astype(jnp.bfloat16) for e, r in zip(expds, sums)]
            for soft, (head, cols, lanes, here, upto) in zip(softs, work):
                prob[head, here, upto] = soft
            mixes = [nn(soft, qkv[2, w[4], w[1]]).astype(jnp.bfloat16) for soft, w in zip(softs, work)]
            for mixed, (head, cols, lanes, here, upto) in zip(mixes, work):
                att[here, cols] = jnp.where(lanes, mixed, att[here, cols])
            return carry
        lax.fori_loop(0, HEADS // GROUP, head_group, 0)
        weight = acquire(use + 3)
        for cols in tiles:
            mid[:, cols] = source[:, cols].astype(f32) + nn(att[...], weight[:, cols])
        after(use + 3)
        low[...] = norm_rows(mid[...], gain_two).astype(b16)
        weight = acquire(use + 4)
        for cols in tiles:
            pre = nn(low[...], weight[:, cols]) + bias_one[:, cols]
            u[:, cols] = pre
            bent = 0.5 * pre * (1.0 + jnp.tanh(GC * (pre + GA * (pre * pre * pre))))
            act[:, cols] = bent.astype(b16)
        after(use + 4)
        weight = acquire(use + 5)
        for cols in tiles:
            out = mid[:, cols] + (nn(act[...], weight[:, cols]) + bias_two[:, cols])
            out_ref[:, cols] = out.astype(b16)
        after(use + 5)

    pieces = (tiles[:3], tiles[3:])
    in_slot = [None, None]

    def put(layer, index, slot):
        first = pieces[slot][0].start
        count = pieces[slot][-1].stop - first
        return pltpu.make_async_copy(
            stage.at[slot, pl.ds(0, count)],
            grads_ref.at[layer, pl.ds(index * width + first, count)],
            out_sems.at[layer, index, slot],
        )

    def weight_grad(layer, index, left_t, right):
        for slot, piece in enumerate(pieces):
            if in_slot[slot] is not None:
                put(*in_slot[slot], slot).wait()
            for cols in piece:
                at = slice(cols.start - piece[0].start, cols.stop - piece[0].start)
                stage[slot, at, :] = nn(left_t(cols), right).astype(b16)
            put(layer, index, slot).start()
            in_slot[slot] = (layer, index)

    def backward(layer, source, dy_ref, out_ref, use):
        qkv, prob, att, mid, u = (ref.at[layer] for ref in (qkvs, probs, atts, mids, us))
        wide, dmid = u, mid
        gain_one, gain_two = vec_ref[layer, 0:1, :], vec_ref[layer, 1:2, :]
        dvec_ref[layer, 3:4, :] = jnp.sum(dy_ref[...].astype(f32), axis=0, keepdims=True)
        weight = acquire(use)
        for cols in tiles:
            pre = u[:, cols]
            square = pre * pre
            bent = jnp.tanh(GC * (pre + GA * (square * pre)))
            half = 0.5 * (1.0 + bent)
            act[:, cols] = (pre * half).astype(b16)
            slope = half + (0.5 * GC) * pre * (1.0 - bent * bent) * (1.0 + (3.0 * GA) * square)
            down = (nt(dy_ref[...], weight[cols, :]) * slope).astype(b16)
            low[:, cols] = down
            dvec_ref[layer, 2:3, cols] = jnp.sum(down.astype(f32), axis=0, keepdims=True)
        after(use)
        weight_grad(layer, 5, lambda cols: act[:, cols].T, dy_ref[...])
        weight = acquire(use + 1)
        for cols in tiles:
            wide[:, cols] = nt(low[...], weight[cols, :])
        after(use + 1)
        act[...] = norm_rows(mid[...], gain_two).astype(b16)
        weight_grad(layer, 4, lambda cols: act[:, cols].T, low[...])
        part, gain_sum = norm_back(mid[...], gain_two, wide[...])
        dvec_ref[layer, 1:2, :] = gain_sum
        total = dy_ref[...].astype(f32) + part
        dmid[...] = total
        low[...] = total.astype(b16)
        weight_grad(layer, 3, lambda cols: att[:, cols].T, low[...])
        weight = acquire(use + 2)
        for cols in tiles:
            act[:, cols] = nt(low[...], weight[cols, :]).astype(b16)
        after(use + 2)

        def head_group(group, carry):
            blocks = range(rows // QB)
            heres = [slice(block * QB, (block + 1) * QB) for block in blocks]
            uptos = [slice(0, (block + 1) * QB) for block in blocks]
            sinces = [slice(block * QB, rows) for block in blocks]
            work = []
            for k in range(GROUP):
                head = group * GROUP + k
                start, lanes = head_window(head, depth, width)
                work += [(head, pl.ds(start, WIN), lanes, heres[b], uptos[b], sinces[b], k) for b in blocks]
            dprobs = [nt(jnp.where(w[2], act[w[3], w[1]], 0), qkv[2, w[4], w[1]]) for w in work]
            softs = [prob[w[0], w[3], w[4]].astype(f32) for w in work]
            leans = [jnp.sum(dp * soft, axis=-1, keepdims=True) for dp, soft in zip(dprobs, softs)]
            dss = [(soft * (dp - lean)).astype(b16) for dp, soft, lean in zip(dprobs, softs, leans)]
            for ds, w in zip(dss, work):
                dscore[w[6], w[3], w[4]] = ds
            dvs = [tn(prob[w[0], w[5], w[3]], act[w[5], w[1]]).astype(b16) for w in work]
            dqs = [(nn(ds, qkv[1, w[4], w[1]]) * scale).astype(b16) for ds, w in zip(dss, work)]
            dks = [(tn(dscore[w[6], w[5], w[3]], qkv[0, w[5], w[1]]) * LN2).astype(b16) for w in work]
            for dq, dk, dv, w in zip(dqs, dks, dvs, work):
                for index, value in enumerate((dq, dk, dv)):
                    dqkv[index, w[3], w[1]] = jnp.where(w[2], value, dqkv[index, w[3], w[1]])
            return carry
        lax.fori_loop(0, HEADS // GROUP, head_group, 0)
        low[...] = norm_rows(source[...].astype(f32), gain_one).astype(b16)
        for cols in tiles:
            turned[cols, :] = low[:, cols].T
        for index in (2, 1, 0):
            weight_grad(layer, index, lambda cols: turned[cols, :], dqkv[index])
        w_value, w_key, w_query = acquire(use + 3), acquire(use + 4), acquire(use + 5)
        for cols in tiles:
            wide[:, cols] = (
                nt(dqkv[0], w_query[cols, :]) + nt(dqkv[1], w_key[cols, :]) + nt(dqkv[2], w_value[cols, :])
            )
        for k in (3, 4, 5):
            after(use + k)
        part, gain_sum = norm_back(source[...].astype(f32), gain_one, wide[...])
        dvec_ref[layer, 0:1, :] = gain_sum
        dvec_ref[layer, 4:8, :] = jnp.zeros_like(dvec_ref[layer, 4:8, :])
        out_ref[...] = (dmid[...] + part).astype(b16)

    forward(0, x_ref, between)
    forward(1, between, y_ref)
    backward(1, between, cot_ref, dx_ref, 12)
    backward(0, x_ref, dx_ref, dx_ref, 18)
    for slot in range(2):
        put(*in_slot[slot], slot).wait()


def both_layers(mats, x, vec, lens, cot):
    rows, width = x.shape
    f32, b16 = jnp.float32, jnp.bfloat16
    vm = pl.BlockSpec(memory_space=pltpu.VMEM)
    hbm = pl.BlockSpec(memory_space=pl.ANY)
    flat = (rows, width)
    dma = pltpu.SemaphoreType.DMA
    return pl.pallas_call(
        both_layers_kernel,
        out_shape=[
            jax.ShapeDtypeStruct(flat, b16),
            jax.ShapeDtypeStruct(mats.shape, b16),
            jax.ShapeDtypeStruct(flat, b16),
            jax.ShapeDtypeStruct((2, 8, width), f32),
        ],
        in_specs=[hbm, vm, vm, pl.BlockSpec(memory_space=pltpu.SMEM), vm],
        out_specs=[vm, hbm, vm, vm],
        scratch_shapes=[
            pltpu.VMEM((SLOTS, width, width), b16),
            pltpu.VMEM((2, 3) + flat, b16),
            pltpu.VMEM((2, HEADS, rows, rows), b16),
            pltpu.VMEM((2,) + flat, b16),
            pltpu.VMEM((2,) + flat, f32),
            pltpu.VMEM((2,) + flat, f32),
            pltpu.VMEM(flat, b16),
            pltpu.VMEM(flat, b16),
            pltpu.VMEM(flat, b16),
            pltpu.VMEM((rows, rows), f32),
            pltpu.VMEM((3,) + flat, b16),
            pltpu.VMEM((GROUP, rows, rows), b16),
            pltpu.VMEM((width, rows), b16),
            pltpu.VMEM((2, 3 * WIN, width), b16),
            dma((len(plan_loads()),)),
            dma((2, 6, 2)),
        ],
        compiler_params=pltpu.CompilerParams(
            vmem_limit_bytes=63 * 2**20,
        ),
        name="both_layers",
    )(mats, x, vec, lens, cot)


def give_back(s, d, me, peers, sendbuf, returned, local_sem, send_sem, recv_sem):
    total = 2 * peers
    keep = pltpu.make_async_copy(sendbuf.at[s, d], returned.at[me], local_sem)
    keep.start()

    def give(step, carry):
        other = lax.rem(me + step, total)
        sec, dp = other // peers, lax.rem(other, peers)
        pltpu.make_async_remote_copy(
            sendbuf.at[sec, dp], returned.at[me], send_sem, recv_sem,
            device_id=(sec, dp), device_id_type=MESH,
        ).start()
        return carry

    lax.fori_loop(1, total, give, 0)

    def finish():
        keep.wait()
        bulk_copy(returned, total - 1, send_sem, recv_sem).wait_recv()
        bulk_copy(returned, total - 1, send_sem, recv_sem).wait_send()

    return finish


def rs_kernel(parts,zn,g_ref,v_ref,dx_ref,y_ref,place_ref,picks_ref,o_ref,vo_ref,res_ref,land,buf,obuf,vland,strips32,sendbuf,returned,*rest):
    nP=len(parts)
    lks=rest[:nP]
    ssem,rsem,cs,cr,lsem,osem,vsend,vrecv,tlocal,tsend,trecv=rest[nP:]
    s,d,z,y,c=coords()
    peers=4*zn
    total_dev=2*peers
    me=s*peers+d
    greet(total_dev,me,peers)
    vland[me]=v_ref[me]
    def small(step,carry):
        other=lax.rem(me+step,total_dev)
        pltpu.make_async_remote_copy(v_ref.at[other],vland.at[me],vsend,vrecv,device_id=(other//peers,lax.rem(other,peers)),device_id_type=MESH).start()
        return carry
    lax.fori_loop(1,total_dev,small,0)
    sib=(s,(z*2+y)*2+1-c)
    def where(it):
        s2=1-s if it[0] else s
        y2=1-y if it[1] else y
        return s2,z+it[2],y2
    def conds(it):
        cl=[]
        if it[2]<0: cl.append(z+it[2]>=0)
        if it[2]>0: cl.append(z+it[2]<=zn-1)
        return cl
    def guarded(cl,fn):
        if not cl: fn(); return
        e=cl[0]
        for q in cl[1:]: e=jnp.logical_and(e,q)
        pl.when(e)(fn)
    def slot_base(order):
        sizes={"x":2,"y":2,"z":zn}
        base={};cur=0
        for k,dim in enumerate(order):
            n=1
            for q in order[k+1:]: n*=sizes[q]
            if dim=="z": n*=2*zn
            base[dim]=cur; cur+=n
        return base,cur
    def slot(p,dim,side,dest):
        order=parts[p][2][::-1]
        base,_=slot_base(order)
        k=order.index(dim)
        v={"x":dest[0],"z":dest[1],"y":dest[2]}
        idx=0
        for q in order[k+1:]:
            idx=idx*(zn if q=="z" else 2)+v[q]
        if dim=="z": idx=(idx*zn+dest[1])*2+side
        return base[dim]+idx
    evs=[]
    for p in range(nP):
        for it in items():
            if abs(it[2])<=zn-1: evs.append((-hops(it),p,it))
    evs.sort(key=lambda e:e[0])
    seq=[(p,it) for _,p,it in evs]
    def core_dsc(p,it,mine):
        r0,rn,_=parts[p]
        s2,z2,y2=where(it)
        idx=(s2*zn+z2)*2+y2
        cc=c if mine else 1-c
        return pltpu.make_async_remote_copy(g_ref.at[s2,(z2*2+y2)*2+cc,pl.ds(r0,rn)],land.at[idx,pl.ds(r0,rn)],cs.at[p,idx],cr.at[p,idx],device_id=sib,device_id_type=MESH)
    for p,it in seq:
        guarded(conds(it),lambda p=p,it=it: core_dsc(p,it,False).start())
    for kind,ref in enumerate((dx_ref,y_ref)):
        cut_strips(place_ref[...],ref,strips32)
        sendbuf[kind]=strips32[...].astype(jnp.bfloat16)
    def load(i):
        p,it=seq[i]
        r0,rn,_=parts[p]
        s2,z2,y2=where(it)
        return pltpu.make_async_copy(g_ref.at[s2,(z2*2+y2)*2+c,pl.ds(r0,rn)],buf.at[i%NB,pl.ds(0,rn)],lsem.at[i%NB])
    NB=buf.shape[0]
    for i in range(min(NB-1,len(seq))):
        guarded(conds(seq[i][1]),lambda i=i: load(i).start())
    def contribs(p,it):
        order=parts[p][2][::-1]
        diff={"x":it[0],"y":it[1],"z":it[2]}
        out=[];nxt=None
        for dim in order:
            if dim=="z":
                if it[2]==0: out+=[("z",0,z>0),("z",1,z<zn-1)]
                elif it[2]>0: out.append(("z",0,z>0))
                else: out.append(("z",1,z<zn-1))
                if it[2]!=0: nxt="r" if it[2]>0 else "l"; break
            else:
                if diff[dim]: nxt=dim; break
                out.append((dim,0,None))
        return out,nxt
    semoff=[0]
    for p in range(nP): semoff.append(semoff[-1]+slot_base(parts[p][2][::-1])[1])
    def out_dsc(p,it,nxt):
        r0,rn,_=parts[p]
        dest=where(it)
        s2,z2,y2=dest
        idx=(s2*zn+z2)*2+y2
        dim="z" if nxt in "lr" else nxt
        side=1 if nxt=="l" else 0
        sl=slot(p,dim,side,dest)
        dev={"x":(1-s,d),"y":(s,(z*2+1-y)*2+c),"l":(s,d-4),"r":(s,d+4)}[nxt]
        return pltpu.make_async_remote_copy(land.at[idx,pl.ds(r0,rn)],lks[p].at[sl],ssem.at[p,idx],rsem.at[semoff[p]+sl],device_id=dev,device_id_type=MESH)
    def settle():
        rest_of=vland.at[pl.ds(0,total_dev-1)]
        bulk=pltpu.make_async_remote_copy(rest_of,rest_of,vsend,vrecv,device_id=(0,0),device_id_type=MESH)
        bulk.wait_recv()
        bulk.wait_send()
        vo_ref[...]=jnp.sum(vland[...],axis=0)
        back()
        for batch in range(2):
            strips32[...]=returned[batch*peers:(batch+1)*peers].astype(jnp.float32)
            join_strips(picks_ref[batch],strips32,res_ref.at[batch])
    for i,(p,it) in enumerate(seq):
        r0,rn,_=parts[p]
        if i==len(seq)*GIVE_NUM//GIVE_DEN: back=give_back(s,d,me,peers,sendbuf,returned,tlocal,tsend,trecv)
        if i==len(seq)*SETTLE_NUM//SETTLE_DEN: settle()
        if i+NB-1<len(seq):
            guarded(conds(seq[i+NB-1][1]),lambda i=i: load(i+NB-1).start())
        def ev(i=i,p=p,it=it,r0=r0,rn=rn):
            dest=where(it)
            s2,z2,y2=dest
            idx=(s2*zn+z2)*2+y2
            con,nxt=contribs(p,it)
            lk=lks[p]
            load(i).wait()
            core_dsc(p,it,True).wait_recv()
            plain=[x for x in con if x[2] is None]
            cond=[x for x in con if x[2] is not None]
            def rdsc(dim,side):
                sl=slot(p,dim,side,dest)
                return pltpu.make_async_remote_copy(lk.at[sl],lk.at[sl],ssem.at[p,idx],rsem.at[semoff[p]+sl],device_id=sib,device_id_type=MESH),sl
            for dim,side,_ in plain: rdsc(dim,side)[0].wait_recv()
            for dim,side,cnd in cond:
                pl.when(cnd)(lambda dim=dim,side=side: rdsc(dim,side)[0].wait_recv())
            if not cond: variants=[(None,plain)]
            elif len(cond)==1:
                variants=[(cond[0][2],plain+cond),(jnp.logical_not(cond[0][2]),plain)]
            else:
                a,b=cond
                variants=[(jnp.logical_and(a[2],b[2]),plain+cond),(jnp.logical_and(a[2],jnp.logical_not(b[2])),plain+[a]),
                          (jnp.logical_and(jnp.logical_not(a[2]),b[2]),plain+[b])]
            def total(lst):
                slots=[slot(p,dim,side,dest) for dim,side,_ in lst]
                CH=16
                def body(k,_):
                    ro=pl.multiple_of(k*CH,CH)
                    acc=buf[i%NB,pl.ds(ro,CH),:].astype(jnp.float32)+land[idx,pl.ds(r0+ro,CH),:].astype(jnp.float32)
                    for sl in slots: acc=acc+lk[sl,pl.ds(ro,CH),:].astype(jnp.float32)
                    if nxt is None: obuf[pl.ds(r0+ro,CH),:]=acc
                    else: land[idx,pl.ds(r0+ro,CH),:]=acc.astype(jnp.bfloat16)
                    return 0
                lax.fori_loop(0,rn//CH,body,0)
            for cnd,lst in variants:
                if cnd is None: total(lst)
                else: pl.when(cnd)(lambda lst=lst: total(lst))
            if nxt is not None: out_dsc(p,it,nxt).start()
            else: pltpu.make_async_copy(obuf.at[pl.ds(r0,rn)],o_ref.at[pl.ds(r0,rn)],osem.at[p]).start()
        guarded(conds(it),ev)
    for p,it in seq:
        def fin(p=p,it=it):
            core_dsc(p,it,False).wait_send()
            nxt=contribs(p,it)[1]
            if nxt is not None: out_dsc(p,it,nxt).wait_send()
        guarded(conds(it),fin)
    for p,(r0,rn,_) in enumerate(parts):
        pltpu.make_async_copy(obuf.at[pl.ds(r0,rn)],o_ref.at[pl.ds(r0,rn)],osem.at[p]).wait()


def slot_count(order,zn):
    sizes={"x":2,"y":2,"z":zn};cur=0
    for k,dim in enumerate(order):
        n=1
        for q in order[k+1:]: n*=sizes[q]
        if dim=="z": n*=2*zn
        cur+=n
    return cur
def rs(g,v,dx,y,place,picks,block,parts,zn,cid=1,nb=4):
    n=len(parts)
    cnt=[slot_count(p[2][::-1],zn) for p in parts]
    mx=max(p[1] for p in parts)
    return pl.pallas_call(functools.partial(rs_kernel,parts,zn),
        out_shape=[jax.ShapeDtypeStruct((480,1280),jnp.float32),jax.ShapeDtypeStruct(v.shape[1:],jnp.float32),
            jax.ShapeDtypeStruct((2,)+dx.shape,jnp.bfloat16)],
        in_specs=[pl.BlockSpec(memory_space=pl.ANY)]+[pl.BlockSpec(memory_space=pltpu.VMEM)]*5,
        out_specs=[pl.BlockSpec(memory_space=pl.ANY)]+[pl.BlockSpec(memory_space=pltpu.VMEM)]*2,
        scratch_shapes=[pltpu.VMEM((4*zn,480,1280),jnp.bfloat16),pltpu.VMEM((nb,mx,1280),jnp.bfloat16),pltpu.VMEM((480,1280),jnp.float32),pltpu.VMEM(v.shape,jnp.float32),
            pltpu.VMEM((4*zn,)+block,jnp.float32),pltpu.VMEM((2,4*zn)+block,jnp.bfloat16),pltpu.VMEM((8*zn,)+block,jnp.bfloat16)]
          +[pltpu.VMEM((cnt[p],parts[p][1],1280),jnp.bfloat16) for p in range(n)]
          +[pltpu.SemaphoreType.DMA((n,4*zn)),pltpu.SemaphoreType.DMA((sum(cnt),)),
          pltpu.SemaphoreType.DMA((n,4*zn)),pltpu.SemaphoreType.DMA((n,4*zn)),pltpu.SemaphoreType.DMA((nb,)),pltpu.SemaphoreType.DMA((n,))]+[pltpu.SemaphoreType.DMA]*5,
        compiler_params=pltpu.CompilerParams(collective_id=cid,has_side_effects=True,vmem_limit_bytes=62*2**20))(g,v,dx,y,place,picks)


def as_row(column):
    rows = column.shape[0]
    return jnp.broadcast_to(column, (rows, 128)).T[0:1, :]


def as_column(row):
    size = row.shape[1]
    return jnp.broadcast_to(row, (128, size)).T[:, 0:1]


def ones_where(flag):
    return jnp.where(flag, 1.0, 0.0)


def gather_events(parts,zn,place,own,w_ref,ssem,rsem,cs,cr):
    s,d,z,y,c=place
    KIND={"x":0,"y":1,"l":2,"r":3}
    def where(it):
        s2=1-s if it[0] else s
        y2=1-y if it[1] else y
        z2=z+it[2]
        return s2,z2,y2
    def dsc(p,it,kind):
        r0,rn,order=parts[p]
        s2,z2,y2=where(it)
        idx=s2*(2*zn)+z2*2+y2
        is_own=it==(0,0,0)
        src=own.at[pl.ds(r0,rn)] if is_own else w_ref.at[s2,(z2*2+y2)*2+c,pl.ds(r0,rn)]
        dst=w_ref.at[s2,(z2*2+y2)*2+c,pl.ds(r0,rn)]
        if kind=="core":
            dev=(s,(z*2+y)*2+1-c)
            return pltpu.make_async_remote_copy(src,dst,cs.at[p,idx],cr.at[p,idx],device_id=dev,device_id_type=MESH)
        dev={"x":(1-s,d),"y":(s,(z*2+1-y)*2+c),"l":(s,d-4),"r":(s,d+4)}[kind]
        return pltpu.make_async_remote_copy(src,dst,ssem.at[KIND[kind],p,idx],rsem.at[p,idx],device_id=dev,device_id_type=MESH)
    def cdsc(p,it):
        r0,rn,order=parts[p]
        s2,z2,y2=where(it)
        idx=s2*(2*zn)+z2*2+y2
        dst=w_ref.at[s2,(z2*2+y2)*2+1-c,pl.ds(r0,rn)]
        return pltpu.make_async_remote_copy(dst,dst,cs.at[p,idx],cr.at[p,idx],device_id=(s,(z*2+y)*2+1-c),device_id_type=MESH)
    def conds(it,kind):
        cs_=[]
        if it[2]<0: cs_.append(z+it[2]>=0)
        if it[2]>0: cs_.append(z+it[2]<=zn-1)
        if kind=="l": cs_.append(z>0)
        if kind=="r": cs_.append(z<zn-1)
        return cs_
    def guarded(cl,fn):
        if not cl: fn(); return
        e=cl[0]
        for q in cl[1:]: e=jnp.logical_and(e,q)
        pl.when(e)(fn)
    def sends(p,it):
        order=parts[p][2]
        a=arrival(order,it)
        ks=[]
        if a is not None and order[a]=="z": ks.append("l" if it[2]>0 else "r")
        for dim in order[(a+1) if a is not None else 0:]:
            ks += ["r","l"] if dim=="z" else [dim]
        ks.append("core")
        return ks
    evs=[]
    for p in range(len(parts)):
        for it in items():
            if abs(it[2])<zn: evs.append((hops(it),p,it))
    evs.sort(key=lambda e:e[0])
    first=[]
    later=[]
    for h,p,it in evs:
        def ev(p=p,it=it):
            if it!=(0,0,0): dsc(p,it,"x").wait_recv()
            for k in sends(p,it):
                guarded(conds((0,0,0),k), lambda k=k: dsc(p,it,k).start())
        (later if h else first).append(lambda it=it,ev=ev: guarded(conds(it,None),ev))
    def finish():
        for _,p,it in evs:
            def fin(p=p,it=it):
                cdsc(p,it).wait_recv()
                for k in sends(p,it):
                    guarded(conds((0,0,0),k), lambda k=k: dsc(p,it,k).wait_send())
            guarded(conds(it,None),fin)
    return first,later,finish


def enter_kernel(
    parts, zn, mats_ref, deal_in, vecs_ref, tokens_ref,
    w_ref, shared_ref, x_ref, cot_ref, picks_ref, place_ref,
    packet_ref, deal_ref, own, wide_rows, strips32, sendbuf, landed, order,
    own_sem, lsem, ssem, rsem, cs, cr, psend, precv, tsend, trecv,
):
    s, d, z, y, c = coords()
    peers = 4 * zn
    total = 2 * peers
    me = s * peers + d
    batches, rows, width = tokens_ref.shape
    f32, b16 = jnp.float32, jnp.bfloat16
    cast_in = pltpu.make_async_copy(mats_ref, wide_rows, own_sem)
    cast_in.start()
    signal_all(total, me, peers)
    deal_ref[...] = deal_in[...].astype(f32)
    lines = rows // 128
    for batch in range(batches):
        for line in range(lines):
            at = batch * lines + line
            packet_ref[at : at + 1, :] = deal_ref[batch : batch + 1, line * 128 : (line + 1) * 128]
    packet_ref[batches * lines :, :] = vecs_ref[...]
    wait_all(total)
    shared_ref[me] = packet_ref[...]

    def tell(step, carry):
        other = lax.rem(me + step, total)
        pltpu.make_async_remote_copy(
            packet_ref, shared_ref.at[me], psend, precv,
            device_id=(other // peers, lax.rem(other, peers)), device_id_type=MESH,
        ).start()
        return carry

    lax.fori_loop(1, total, tell, 0)
    cast_in.wait()
    own[...] = wide_rows[...].astype(b16)
    lc = pltpu.make_async_copy(own, w_ref.at[s, d], lsem)
    lc.start()
    start_events, rest_events, finish = gather_events(
        parts, zn, (s, d, z, y, c), own, w_ref, ssem, rsem, cs, cr
    )
    for event in start_events:
        event()
    sub = lax.broadcasted_iota(jnp.int32, (rows, rows), 0).astype(f32)
    lane = lax.broadcasted_iota(jnp.int32, (rows, rows), 1).astype(f32)
    mine_row = jnp.where(s == 0, deal_ref[0:1, :], deal_ref[1:2, :])
    mine_col = as_column(mine_row)
    rank_col = jnp.sum(ones_where(mine_row < mine_col), axis=1, keepdims=True)
    order[...] = ones_where(lane == rank_col).astype(b16)
    rank_row = jnp.sum(ones_where(mine_col < mine_row), axis=0, keepdims=True)
    place_ref[...] = ones_where(sub == rank_row).astype(b16)
    rest = shared_ref.at[pl.ds(0, total - 1)]
    bulk = pltpu.make_async_remote_copy(
        rest, rest, psend, precv, device_id=(0, 0), device_id_type=MESH
    )
    bulk.wait_recv()
    index_col = lax.broadcasted_iota(jnp.int32, (rows, 1), 0).astype(f32)
    ids_col = index_col + (d * rows).astype(f32)
    for batch in range(batches):

        def look(block, found):
            known = shared_ref[s * peers + block]
            for line in range(rows // 128):
                at = batch * (rows // 128) + line
                found = jnp.where(ids_col == known[at : at + 1, :], block.astype(f32), found)
            return found

        found = lax.fori_loop(0, peers, look, jnp.zeros((rows, 128), f32))
        key_col = jnp.sum(found, axis=1, keepdims=True) * rows + index_col
        key_row = as_row(key_col)
        rank_row = jnp.sum(ones_where(key_col < key_row), axis=0, keepdims=True)
        rank_col = jnp.sum(ones_where(key_row < key_col), axis=1, keepdims=True)
        picks_ref[batch] = ones_where(lane == rank_col).astype(b16)
        pick = ones_where(sub == rank_row).astype(b16)
        cut_strips(pick, tokens_ref.at[batch], strips32)
        sendbuf[batch] = strips32[...].astype(b16)

    landed[me] = sendbuf[s, d]

    early = len(rest_events) * HAND_NUM // HAND_DEN
    for event in rest_events[:early]:
        event()

    def give(step, carry):
        other = lax.rem(me + step, total)
        sec, dp = other // peers, lax.rem(other, peers)
        pltpu.make_async_remote_copy(
            sendbuf.at[sec, dp], landed.at[me], tsend, trecv.at[s],
            device_id=(sec, dp), device_id_type=MESH,
        ).start()
        return carry

    lax.fori_loop(1, total, give, 0)
    def take(kind, out_ref):
        pl.when(s == kind)(
            lambda: bulk_copy(landed, peers - 1, tsend, trecv.at[kind]).wait_recv()
        )
        pl.when(s != kind)(lambda: bulk_copy(landed, peers, tsend, trecv.at[kind]).wait_recv())
        strips32[...] = landed[pl.ds(kind * peers, peers)].astype(f32)
        join_strips(order[...], strips32, out_ref)

    middle = len(rest_events) * TAKE_NUM // TAKE_DEN
    for event in rest_events[early:middle]:
        event()
    take(0, x_ref)
    take(1, cot_ref)
    for event in rest_events[middle:]:
        event()
    finish()
    lc.wait()
    bulk.wait_send()
    most = landed.at[pl.ds(0, total - 1)]
    pltpu.make_async_remote_copy(
        most, most, tsend, trecv.at[0], device_id=(0, 0), device_id_type=MESH
    ).wait_send()


def enter(mats, deal, vecs, tokens, parts, zn):
    n = len(parts)
    peers = 4 * zn
    batches, rows, width = tokens.shape
    packet = (batches * (rows // 128) + vecs.shape[0], 128)
    strip_rows = rows // peers * (width // 128)
    f32, b16 = jnp.float32, jnp.bfloat16
    vm = pl.BlockSpec(memory_space=pltpu.VMEM)
    hbm = pl.BlockSpec(memory_space=pl.ANY)
    dma = pltpu.SemaphoreType.DMA
    return pl.pallas_call(
        functools.partial(enter_kernel, parts, zn),
        out_shape=[
            jax.ShapeDtypeStruct((2, peers) + mats.shape, b16),
            jax.ShapeDtypeStruct((2 * peers,) + packet, f32),
            jax.ShapeDtypeStruct((rows, width), b16),
            jax.ShapeDtypeStruct((rows, width), b16),
            jax.ShapeDtypeStruct((batches, rows, rows), b16),
            jax.ShapeDtypeStruct((rows, rows), b16),
        ],
        in_specs=[hbm, vm, vm, vm],
        out_specs=[hbm, vm, vm, vm, vm, vm],
        scratch_shapes=[
            pltpu.VMEM(packet, f32),
            pltpu.VMEM(deal.shape, f32),
            pltpu.VMEM(mats.shape, b16),
            pltpu.VMEM(mats.shape, f32),
            pltpu.VMEM((peers, strip_rows, 128), f32),
            pltpu.VMEM((batches, peers, strip_rows, 128), b16),
            pltpu.VMEM((2 * peers, strip_rows, 128), b16),
            pltpu.VMEM((rows, rows), b16),
            dma, dma, dma((4, n, peers)), dma((n, peers)), dma((n, peers)), dma((n, peers)),
            dma, dma, dma, dma((2,)),
        ],
        compiler_params=pltpu.CompilerParams(
            collective_id=0, has_side_effects=True, vmem_limit_bytes=VMEM_LIMIT
        ),
        name="enter",
    )(mats, deal, vecs, tokens)


def one_hot(rank):
    rows = rank.shape[0]
    return (rank[None, :] == jnp.arange(rows, dtype=jnp.int32)[:, None]).astype(jnp.bfloat16)


def rank_of(key):
    return jnp.sum((key[None, :] < key[:, None]).astype(jnp.int32), axis=1)


def padded(flat):
    lead, size = flat.shape
    full = -(-size // 1024) * 1024
    return jnp.pad(flat, ((0, 0), (0, full - size))).reshape(lead, full // 128, 128)


def enter_plain(own, packet, deal, tokens, peers):
    section = lax.axis_index("section")
    batches, rows, width = tokens.shape
    per_peer = rows // peers
    shared = lax.all_gather(packet, BOTH, axis=0)
    low = own.astype(jnp.bfloat16)
    mats = lax.all_gather(low, BOTH, axis=0, tiled=True).reshape((2, peers) + own.shape)
    flat = shared.reshape(2, peers, -1)[:, :, : batches * rows]
    dealt = jnp.where(section == 0, flat[0], flat[1]).astype(jnp.int32).reshape(peers, batches, rows)
    own_rows = lax.axis_index("dp") * rows + jnp.arange(rows, dtype=jnp.int32)
    blocks = jnp.arange(peers, dtype=jnp.int32)
    picks = []
    sends = []
    for batch in range(batches):
        hit = dealt[:, batch][None, :, :] == own_rows[:, None, None]
        target = jnp.sum(jnp.where(hit, blocks[None, :, None], 0), axis=(1, 2))
        pick = one_hot(rank_of(target * rows + jnp.arange(rows, dtype=jnp.int32)))
        picks.append(pick.T)
        sends.append(nn(pick, tokens[batch]).astype(jnp.bfloat16))
    outgoing = jnp.stack(sends).reshape(2 * peers, per_peer, width)
    arrived = lax.all_to_all(outgoing, BOTH, split_axis=0, concat_axis=0, tiled=True)
    arrived = arrived.reshape(2, rows, width)
    place = one_hot(rank_of(jnp.where(section == 0, deal[0], deal[1])))
    x, cot = (tn(place, arrived[kind]).astype(jnp.bfloat16) for kind in range(2))
    return mats, shared, x, cot, jnp.stack(picks), place


def leave_plain(terms, small, down, final, place, picks, peers):
    sections, _, rows, width = terms.shape
    terms = terms.reshape(sections * peers * rows, width)
    total = lax.psum_scatter(terms, BOTH, scatter_dimension=0, tiled=True).astype(jnp.float32)
    small = lax.psum_scatter(small, BOTH, scatter_dimension=0, tiled=True)[0]
    back = jnp.stack([nn(place, down), nn(place, final)]).astype(jnp.bfloat16)
    count = down.shape[0]
    back = back.reshape(2 * peers, count // peers, width)
    back = lax.all_to_all(back, BOTH, split_axis=0, concat_axis=0, tiled=True)
    back = back.reshape(-1, count, width)
    results = jnp.stack([nn(picks[batch], back[batch]) for batch in range(back.shape[0])])
    return total, small, results.astype(jnp.bfloat16)


def local(entering, deal, seq_lens, mats, gains, biases):
    section = lax.axis_index("section")
    peers = lax.axis_size("dp")
    arrival = entering[0]
    batches, rows, width = arrival.shape
    per = 2 * width // peers
    direct = peers == 16
    vecs = jnp.concatenate([gains[0], biases[0]]).astype(jnp.bfloat16).astype(jnp.float32)
    known = batches * rows
    if direct:
        lines = known // 128
        full = -(-(lines * 128 + vecs.shape[0]) // 1024) * 8 - lines
        vecs = jnp.pad(vecs, (0, full * 128 - vecs.shape[0])).reshape(full, 128)
        entered = enter(mats[0], deal, vecs, arrival, GATHER_PARTS, peers // 4)
    else:
        packet = jnp.concatenate([deal.reshape(-1).astype(jnp.float32), vecs])
        packet = padded(packet[None])[0]
        entered = enter_plain(mats[0], packet, deal, arrival, peers)
    all_mats, shared, tokens, cotangent, picks, place = entered
    shared = shared.reshape(2, peers, -1)
    small = shared[:, :, batches * rows : batches * rows + 2 * per].reshape(2, peers, 2, per)
    small = jnp.swapaxes(small, 1, 2).reshape(2, 4, width)
    small = jnp.pad(small, ((0, 0), (0, 4), (0, 0)))
    all_mats = all_mats.reshape(2, 6 * width, width)
    final, terms, down, vec_grads = both_layers(
        all_mats, tokens, small, seq_lens[:, 0, :], cotangent
    )
    terms = terms.reshape(2, peers, -1, width)
    vec_terms = vec_grads[:, :4].reshape(2, 2, peers, per)
    vec_terms = padded(jnp.swapaxes(vec_terms, 1, 2).reshape(2 * peers, 2 * per))
    block = (rows // peers * (width // 128), 128)
    if direct:
        shard_mats, vec_total, results = rs(
            terms, vec_terms, down, final, place, picks, block, SCATTER_PARTS, peers // 4
        )
    else:
        shard_mats, vec_total, results = leave_plain(
            terms, vec_terms, down, final, place, picks, peers
        )
    vec_total = vec_total.reshape(-1)
    return (
        results[None],
        shard_mats[None],
        vec_total[None, :per],
        vec_total[None, per : 2 * per],
    )


def solution(mesh):
    in_specs = (
        P("section", None, "dp", None),
        P(None, "dp"),
        P(None, "dp", None),
        P("section", "dp", None),
        P("section", "dp"),
        P("section", "dp"),
    )
    out_specs = (
        P("section", None, "dp", None),
        P("section", "dp", None),
        P("section", "dp"),
        P("section", "dp"),
    )
    return jax.shard_map(local, mesh=mesh, in_specs=in_specs, out_specs=out_specs, check_vma=False)
```

```python
import functools

import jax
import jax.numpy as jnp
from jax import lax
from jax.experimental import pallas as pl
from jax.experimental.pallas import tpu as pltpu
from jax.sharding import PartitionSpec as P

HEADS = 16
EPS = 1e-06
NEG = -1000000000.0
BOTH = ("section", "dp")
MESH = pl.DeviceIdType.MESH
GATHER_PARTS = ((0, 112, "zxy"), (112, 112, "zyx"), (224, 128, "xzy"), (352, 128, "yzx"))
SCATTER_PARTS = ((0, 112, "zxy"), (112, 112, "zyx"), (224, 128, "xzy"), (352, 128, "yzx"))
TAKE_NUM, TAKE_DEN = 3, 4
SETTLE_NUM, SETTLE_DEN = 7, 8
GIVE_NUM, GIVE_DEN = 0, 1
HAND_NUM, HAND_DEN = 0, 1


WIN = 256
QB = 128
GROUP = 4
LOG2E = 1.4426950408889634
LN2 = 0.6931471805599453
GC = 0.7978845608028654
GA = 0.044715
VMEM_LIMIT = 62 * 2**20


def nn(left, right):
    return jnp.dot(left, right, preferred_element_type=jnp.float32)


def nt(left, right):
    return lax.dot_general(
        left, right, (((1,), (1,)), ((), ())), preferred_element_type=jnp.float32
    )


def tn(left, right):
    return lax.dot_general(
        left, right, (((0,), (0,)), ((), ())), preferred_element_type=jnp.float32
    )


def head_window(head, depth, width):
    start = jnp.minimum((head * depth) // 128, (width - WIN) // 128) * 128
    start = pl.multiple_of(start, 128)
    lane = lax.broadcasted_iota(jnp.int32, (1, WIN), 1) + (start - head * depth)
    return start, (lane >= 0) & (lane < depth)


def norm_rows(value, gain):
    return value * lax.rsqrt(jnp.mean(value * value, axis=-1, keepdims=True) + EPS) * gain


def norm_back(value, gain, down):
    inv = lax.rsqrt(jnp.mean(value * value, axis=-1, keepdims=True) + EPS)
    unit = value * inv
    scaled = down * gain
    lean = jnp.mean(scaled * unit, axis=-1, keepdims=True)
    return inv * (scaled - unit * lean), jnp.sum(down * unit, axis=0, keepdims=True)


def signal_all(total, me, peers):
    barrier = pltpu.get_barrier_semaphore()

    def one(step, carry):
        other = lax.rem(me + step, total)
        pl.semaphore_signal(
            barrier, inc=1, device_id=(other // peers, lax.rem(other, peers)), device_id_type=MESH
        )
        return carry

    lax.fori_loop(1, total, one, 0)


def wait_all(total):
    pl.semaphore_wait(pltpu.get_barrier_semaphore(), total - 1)


def greet(total, me, peers):
    signal_all(total, me, peers)
    wait_all(total)


def cut_strips(pick, source, strips32):
    peers = strips32.shape[0]
    strips = source.shape[-1] // 128
    each = strips32.shape[1] // strips
    for strip in range(strips):
        part = nn(pick, source[:, strip * 128 : (strip + 1) * 128])
        strips32[:, strip * each : (strip + 1) * each, :] = part.reshape(peers, each, 128)


def join_strips(order, strips32, out_ref):
    peers = strips32.shape[0]
    strips = out_ref.shape[-1] // 128
    each = strips32.shape[1] // strips
    for strip in range(strips):
        part = strips32[:, strip * each : (strip + 1) * each, :].reshape(peers * each, 128)
        part = nn(order, part.astype(jnp.bfloat16)).astype(jnp.bfloat16)
        out_ref[:, strip * 128 : (strip + 1) * 128] = part


def bulk_copy(ref, count, send_sem, recv_sem):
    some = ref.at[pl.ds(0, count)]
    return pltpu.make_async_remote_copy(
        some, some, send_sem, recv_sem, device_id=(0, 0), device_id_type=MESH
    )


def coords():
    s=lax.axis_index("section"); d=lax.axis_index("dp")
    return s,d,d//4,(d//2)%2,d%2

def items():
    out=[]
    for bx in (0,1):
        for by in (0,1):
            for dz in (0,-1,1,-2,2,-3,3):
                out.append((bx,by,dz))
    return out
def hops(it): return it[0]+it[1]+abs(it[2])
def arrival(order,it):
    diff={"x":it[0]!=0,"y":it[1]!=0,"z":it[2]!=0}
    last=None
    for k,dim in enumerate(order):
        if diff[dim]: last=k
    return last

def neighbours(s,d,z,y,c,zn):
    return [(None,(1-s,d)),(None,(s,(z*2+1-y)*2+c)),(None,(s,(z*2+y)*2+1-c)),(z>0,(s,d-4)),(z<zn-1,(s,d+4))]


SLOTS = 4
USES = (
    [(0, index) for index in range(6)] + [(1, index) for index in range(6)]
    + [(1, index) for index in (5, 4, 3, 2, 1, 0)] + [(0, index) for index in (5, 4, 3, 2, 1, 0)]
)


def plan_loads():
    def next_use(what, since):
        return next((t for t in range(since, len(USES)) if USES[t] == what), len(USES))

    held = [None] * SLOTS
    loads = []
    for done in range(-1, len(USES)):
        for t in range(done + 1, len(USES)):
            if USES[t] in held:
                continue
            away = [next_use(what, done + 1) if what else len(USES) + 1 for what in held]
            slot = max(range(SLOTS), key=lambda k: away[k])
            if away[slot] <= t:
                break
            held[slot] = USES[t]
            loads.append((done, t, slot))
    return loads


def both_layers_kernel(*refs):
    mats_ref, x_ref, vec_ref, lens_ref, cot_ref = refs[:5]
    y_ref, grads_ref, dx_ref, dvec_ref = refs[5:9]
    (
        held, qkvs, probs, atts, mids, us, between, act, low, mask, dqkv, dscore, turned,
    stage, sems, out_sems,
    ) = refs[9:]
    rows, width = x_ref.shape
    depth = width // HEADS
    scale = depth ** (-0.5)
    f32, b16 = jnp.float32, jnp.bfloat16
    tiles = [slice(c, c + WIN) for c in range(0, width, WIN)]
    loads = plan_loads()
    pending = {}

    def load(number):
        done, use, slot = loads[number]
        layer, index = USES[use]
        return pltpu.make_async_copy(
            mats_ref.at[layer, pl.ds(index * width, width)], held.at[slot], sems.at[number]
        )

    def after(done):
        for number, (when, use, slot) in enumerate(loads):
            if when == done:
                load(number).start()
                pending[slot] = number

    def acquire(use):
        number = max(
            k for k, (when, first, slot) in enumerate(loads) if USES[first] == USES[use] and first <= use
        )
        slot = loads[number][2]
        if pending.get(slot) == number:
            load(number).wait()
            pending.pop(slot)
        return held.at[slot]

    after(-1)
    batch = lax.axis_index("section")
    row = lax.broadcasted_iota(jnp.int32, (rows, 1), 0)
    col = lax.broadcasted_iota(jnp.int32, (1, rows), 1)
    end = jnp.int32(0)
    row_part, col_part = jnp.zeros((rows, 1), jnp.int32), jnp.zeros((1, rows), jnp.int32)
    for place in range(lens_ref.shape[1]):
        end = end + lens_ref[batch, place]
        row_part = row_part + jnp.where(row >= end, 1, 0)
        col_part = col_part + jnp.where(col >= end, 1, 0)
    mask[...] = jnp.where((row_part == col_part) & (col <= row), 3e38, NEG)

    def forward(layer, source, out_ref):
        qkv, prob, att, mid, u = (ref.at[layer] for ref in (qkvs, probs, atts, mids, us))
        gain_one, gain_two = vec_ref[layer, 0:1, :], vec_ref[layer, 1:2, :]
        bias_one, bias_two = vec_ref[layer, 2:3, :], vec_ref[layer, 3:4, :]
        use = 6 * layer
        low[...] = norm_rows(source[...].astype(f32), gain_one).astype(b16)
        for index in range(3):
            weight = acquire(use + index)
            for cols in tiles:
                part = nn(low[...], weight[:, cols])
                if index == 0:
                    part = part * (scale * LOG2E)
                qkv[index, :, cols] = part.astype(b16)
            after(use + index)

        def head_group(group, carry):
            blocks = range(rows // QB)
            heres = [slice(block * QB, (block + 1) * QB) for block in blocks]
            uptos = [slice(0, (block + 1) * QB) for block in blocks]
            work = []
            for k in range(GROUP):
                head = group * GROUP + k
                start, lanes = head_window(head, depth, width)
                work += [(head, pl.ds(start, WIN), lanes, heres[b], uptos[b]) for b in blocks]
            scores = [nt(jnp.where(lanes, qkv[0, here, cols], 0), qkv[1, upto, cols]) for head, cols, lanes, here, upto in work]
            scores = [jnp.minimum(score, mask[w[3], w[4]]) for score, w in zip(scores, work)]
            tops = [jnp.max(score, axis=-1, keepdims=True) for score in scores]
            expds = [jnp.exp2(score - top) for score, top in zip(scores, tops)]
            sums = [1.0 / jnp.sum(e, axis=-1, keepdims=True) for e in expds]
            softs = [(e * r).astype(jnp.bfloat16) for e, r in zip(expds, sums)]
            for soft, (head, cols, lanes, here, upto) in zip(softs, work):
                prob[head, here, upto] = soft
            mixes = [nn(soft, qkv[2, w[4], w[1]]).astype(jnp.bfloat16) for soft, w in zip(softs, work)]
            for mixed, (head, cols, lanes, here, upto) in zip(mixes, work):
                att[here, cols] = jnp.where(lanes, mixed, att[here, cols])
            return carry
        lax.fori_loop(0, HEADS // GROUP, head_group, 0)
        weight = acquire(use + 3)
        for cols in tiles:
            mid[:, cols] = source[:, cols].astype(f32) + nn(att[...], weight[:, cols])
        after(use + 3)
        low[...] = norm_rows(mid[...], gain_two).astype(b16)
        weight = acquire(use + 4)
        for cols in tiles:
            pre = nn(low[...], weight[:, cols]) + bias_one[:, cols]
            u[:, cols] = pre
            bent = 0.5 * pre * (1.0 + jnp.tanh(GC * (pre + GA * (pre * pre * pre))))
            act[:, cols] = bent.astype(b16)
        after(use + 4)
        weight = acquire(use + 5)
        for cols in tiles:
            out = mid[:, cols] + (nn(act[...], weight[:, cols]) + bias_two[:, cols])
            out_ref[:, cols] = out.astype(b16)
        after(use + 5)

    pieces = (tiles[:3], tiles[3:])
    in_slot = [None, None]

    def put(layer, index, slot):
        first = pieces[slot][0].start
        count = pieces[slot][-1].stop - first
        return pltpu.make_async_copy(
            stage.at[slot, pl.ds(0, count)],
            grads_ref.at[layer, pl.ds(index * width + first, count)],
            out_sems.at[layer, index, slot],
        )

    def weight_grad(layer, index, left_t, right):
        for slot, piece in enumerate(pieces):
            if in_slot[slot] is not None:
                put(*in_slot[slot], slot).wait()
            for cols in piece:
                at = slice(cols.start - piece[0].start, cols.stop - piece[0].start)
                stage[slot, at, :] = nn(left_t(cols), right).astype(b16)
            put(layer, index, slot).start()
            in_slot[slot] = (layer, index)

    def backward(layer, source, dy_ref, out_ref, use):
        qkv, prob, att, mid, u = (ref.at[layer] for ref in (qkvs, probs, atts, mids, us))
        wide, dmid = u, mid
        gain_one, gain_two = vec_ref[layer, 0:1, :], vec_ref[layer, 1:2, :]
        dvec_ref[layer, 3:4, :] = jnp.sum(dy_ref[...].astype(f32), axis=0, keepdims=True)
        weight = acquire(use)
        for cols in tiles:
            pre = u[:, cols]
            square = pre * pre
            bent = jnp.tanh(GC * (pre + GA * (square * pre)))
            half = 0.5 * (1.0 + bent)
            act[:, cols] = (pre * half).astype(b16)
            slope = half + (0.5 * GC) * pre * (1.0 - bent * bent) * (1.0 + (3.0 * GA) * square)
            down = (nt(dy_ref[...], weight[cols, :]) * slope).astype(b16)
            low[:, cols] = down
            dvec_ref[layer, 2:3, cols] = jnp.sum(down.astype(f32), axis=0, keepdims=True)
        after(use)
        weight_grad(layer, 5, lambda cols: act[:, cols].T, dy_ref[...])
        weight = acquire(use + 1)
        for cols in tiles:
            wide[:, cols] = nt(low[...], weight[cols, :])
        after(use + 1)
        act[...] = norm_rows(mid[...], gain_two).astype(b16)
        weight_grad(layer, 4, lambda cols: act[:, cols].T, low[...])
        part, gain_sum = norm_back(mid[...], gain_two, wide[...])
        dvec_ref[layer, 1:2, :] = gain_sum
        total = dy_ref[...].astype(f32) + part
        dmid[...] = total
        low[...] = total.astype(b16)
        weight_grad(layer, 3, lambda cols: att[:, cols].T, low[...])
        weight = acquire(use + 2)
        for cols in tiles:
            act[:, cols] = nt(low[...], weight[cols, :]).astype(b16)
        after(use + 2)

        def head_group(group, carry):
            blocks = range(rows // QB)
            heres = [slice(block * QB, (block + 1) * QB) for block in blocks]
            uptos = [slice(0, (block + 1) * QB) for block in blocks]
            sinces = [slice(block * QB, rows) for block in blocks]
            work = []
            for k in range(GROUP):
                head = group * GROUP + k
                start, lanes = head_window(head, depth, width)
                work += [(head, pl.ds(start, WIN), lanes, heres[b], uptos[b], sinces[b], k) for b in blocks]
            dprobs = [nt(jnp.where(w[2], act[w[3], w[1]], 0), qkv[2, w[4], w[1]]) for w in work]
            softs = [prob[w[0], w[3], w[4]].astype(f32) for w in work]
            leans = [jnp.sum(dp * soft, axis=-1, keepdims=True) for dp, soft in zip(dprobs, softs)]
            dss = [(soft * (dp - lean)).astype(b16) for dp, soft, lean in zip(dprobs, softs, leans)]
            for ds, w in zip(dss, work):
                dscore[w[6], w[3], w[4]] = ds
            dvs = [tn(prob[w[0], w[5], w[3]], act[w[5], w[1]]).astype(b16) for w in work]
            dqs = [(nn(ds, qkv[1, w[4], w[1]]) * scale).astype(b16) for ds, w in zip(dss, work)]
            dks = [(tn(dscore[w[6], w[5], w[3]], qkv[0, w[5], w[1]]) * LN2).astype(b16) for w in work]
            for dq, dk, dv, w in zip(dqs, dks, dvs, work):
                for index, value in enumerate((dq, dk, dv)):
                    dqkv[index, w[3], w[1]] = jnp.where(w[2], value, dqkv[index, w[3], w[1]])
            return carry
        lax.fori_loop(0, HEADS // GROUP, head_group, 0)
        low[...] = norm_rows(source[...].astype(f32), gain_one).astype(b16)
        for cols in tiles:
            turned[cols, :] = low[:, cols].T
        for index in (2, 1, 0):
            weight_grad(layer, index, lambda cols: turned[cols, :], dqkv[index])
        w_value, w_key, w_query = acquire(use + 3), acquire(use + 4), acquire(use + 5)
        for cols in tiles:
            wide[:, cols] = (
                nt(dqkv[0], w_query[cols, :]) + nt(dqkv[1], w_key[cols, :]) + nt(dqkv[2], w_value[cols, :])
            )
        for k in (3, 4, 5):
            after(use + k)
        part, gain_sum = norm_back(source[...].astype(f32), gain_one, wide[...])
        dvec_ref[layer, 0:1, :] = gain_sum
        dvec_ref[layer, 4:8, :] = jnp.zeros_like(dvec_ref[layer, 4:8, :])
        out_ref[...] = (dmid[...] + part).astype(b16)

    forward(0, x_ref, between)
    forward(1, between, y_ref)
    backward(1, between, cot_ref, dx_ref, 12)
    backward(0, x_ref, dx_ref, dx_ref, 18)
    for slot in range(2):
        put(*in_slot[slot], slot).wait()


def both_layers(mats, x, vec, lens, cot):
    rows, width = x.shape
    f32, b16 = jnp.float32, jnp.bfloat16
    vm = pl.BlockSpec(memory_space=pltpu.VMEM)
    hbm = pl.BlockSpec(memory_space=pl.ANY)
    flat = (rows, width)
    dma = pltpu.SemaphoreType.DMA
    return pl.pallas_call(
        both_layers_kernel,
        out_shape=[
            jax.ShapeDtypeStruct(flat, b16),
            jax.ShapeDtypeStruct(mats.shape, b16),
            jax.ShapeDtypeStruct(flat, b16),
            jax.ShapeDtypeStruct((2, 8, width), f32),
        ],
        in_specs=[hbm, vm, vm, pl.BlockSpec(memory_space=pltpu.SMEM), vm],
        out_specs=[vm, hbm, vm, vm],
        scratch_shapes=[
            pltpu.VMEM((SLOTS, width, width), b16),
            pltpu.VMEM((2, 3) + flat, b16),
            pltpu.VMEM((2, HEADS, rows, rows), b16),
            pltpu.VMEM((2,) + flat, b16),
            pltpu.VMEM((2,) + flat, f32),
            pltpu.VMEM((2,) + flat, f32),
            pltpu.VMEM(flat, b16),
            pltpu.VMEM(flat, b16),
            pltpu.VMEM(flat, b16),
            pltpu.VMEM((rows, rows), f32),
            pltpu.VMEM((3,) + flat, b16),
            pltpu.VMEM((GROUP, rows, rows), b16),
            pltpu.VMEM((width, rows), b16),
            pltpu.VMEM((2, 3 * WIN, width), b16),
            dma((len(plan_loads()),)),
            dma((2, 6, 2)),
        ],
        compiler_params=pltpu.CompilerParams(
            vmem_limit_bytes=63 * 2**20,
        ),
        name="both_layers",
    )(mats, x, vec, lens, cot)


def give_back(s, d, me, peers, sendbuf, returned, local_sem, send_sem, recv_sem):
    total = 2 * peers
    keep = pltpu.make_async_copy(sendbuf.at[s, d], returned.at[me], local_sem)
    keep.start()

    def give(step, carry):
        other = lax.rem(me + step, total)
        sec, dp = other // peers, lax.rem(other, peers)
        pltpu.make_async_remote_copy(
            sendbuf.at[sec, dp], returned.at[me], send_sem, recv_sem,
            device_id=(sec, dp), device_id_type=MESH,
        ).start()
        return carry

    lax.fori_loop(1, total, give, 0)

    def finish():
        keep.wait()
        bulk_copy(returned, total - 1, send_sem, recv_sem).wait_recv()
        bulk_copy(returned, total - 1, send_sem, recv_sem).wait_send()

    return finish


def rs_kernel(parts,zn,g_ref,v_ref,dx_ref,y_ref,place_ref,picks_ref,o_ref,vo_ref,res_ref,land,buf,obuf,vland,strips32,sendbuf,returned,*rest):
    nP=len(parts)
    lks=rest[:nP]
    ssem,rsem,cs,cr,lsem,osem,vsend,vrecv,tlocal,tsend,trecv=rest[nP:]
    s,d,z,y,c=coords()
    peers=4*zn
    total_dev=2*peers
    me=s*peers+d
    greet(total_dev,me,peers)
    vland[me]=v_ref[me]
    def small(step,carry):
        other=lax.rem(me+step,total_dev)
        pltpu.make_async_remote_copy(v_ref.at[other],vland.at[me],vsend,vrecv,device_id=(other//peers,lax.rem(other,peers)),device_id_type=MESH).start()
        return carry
    lax.fori_loop(1,total_dev,small,0)
    sib=(s,(z*2+y)*2+1-c)
    def where(it):
        s2=1-s if it[0] else s
        y2=1-y if it[1] else y
        return s2,z+it[2],y2
    def conds(it):
        cl=[]
        if it[2]<0: cl.append(z+it[2]>=0)
        if it[2]>0: cl.append(z+it[2]<=zn-1)
        return cl
    def guarded(cl,fn):
        if not cl: fn(); return
        e=cl[0]
        for q in cl[1:]: e=jnp.logical_and(e,q)
        pl.when(e)(fn)
    def slot_base(order):
        sizes={"x":2,"y":2,"z":zn}
        base={};cur=0
        for k,dim in enumerate(order):
            n=1
            for q in order[k+1:]: n*=sizes[q]
            if dim=="z": n*=2*zn
            base[dim]=cur; cur+=n
        return base,cur
    def slot(p,dim,side,dest):
        order=parts[p][2][::-1]
        base,_=slot_base(order)
        k=order.index(dim)
        v={"x":dest[0],"z":dest[1],"y":dest[2]}
        idx=0
        for q in order[k+1:]:
            idx=idx*(zn if q=="z" else 2)+v[q]
        if dim=="z": idx=(idx*zn+dest[1])*2+side
        return base[dim]+idx
    evs=[]
    for p in range(nP):
        for it in items():
            if abs(it[2])<=zn-1: evs.append((-hops(it),p,it))
    evs.sort(key=lambda e:e[0])
    seq=[(p,it) for _,p,it in evs]
    def core_dsc(p,it,mine):
        r0,rn,_=parts[p]
        s2,z2,y2=where(it)
        idx=(s2*zn+z2)*2+y2
        cc=c if mine else 1-c
        return pltpu.make_async_remote_copy(g_ref.at[s2,(z2*2+y2)*2+cc,pl.ds(r0,rn)],land.at[idx,pl.ds(r0,rn)],cs.at[p,idx],cr.at[p,idx],device_id=sib,device_id_type=MESH)
    for p,it in seq:
        guarded(conds(it),lambda p=p,it=it: core_dsc(p,it,False).start())
    for kind,ref in enumerate((dx_ref,y_ref)):
        cut_strips(place_ref[...],ref,strips32)
        sendbuf[kind]=strips32[...].astype(jnp.bfloat16)
    def load(i):
        p,it=seq[i]
        r0,rn,_=parts[p]
        s2,z2,y2=where(it)
        return pltpu.make_async_copy(g_ref.at[s2,(z2*2+y2)*2+c,pl.ds(r0,rn)],buf.at[i%NB,pl.ds(0,rn)],lsem.at[i%NB])
    NB=buf.shape[0]
    for i in range(min(NB-1,len(seq))):
        guarded(conds(seq[i][1]),lambda i=i: load(i).start())
    def contribs(p,it):
        order=parts[p][2][::-1]
        diff={"x":it[0],"y":it[1],"z":it[2]}
        out=[];nxt=None
        for dim in order:
            if dim=="z":
                if it[2]==0: out+=[("z",0,z>0),("z",1,z<zn-1)]
                elif it[2]>0: out.append(("z",0,z>0))
                else: out.append(("z",1,z<zn-1))
                if it[2]!=0: nxt="r" if it[2]>0 else "l"; break
            else:
                if diff[dim]: nxt=dim; break
                out.append((dim,0,None))
        return out,nxt
    semoff=[0]
    for p in range(nP): semoff.append(semoff[-1]+slot_base(parts[p][2][::-1])[1])
    def out_dsc(p,it,nxt):
        r0,rn,_=parts[p]
        dest=where(it)
        s2,z2,y2=dest
        idx=(s2*zn+z2)*2+y2
        dim="z" if nxt in "lr" else nxt
        side=1 if nxt=="l" else 0
        sl=slot(p,dim,side,dest)
        dev={"x":(1-s,d),"y":(s,(z*2+1-y)*2+c),"l":(s,d-4),"r":(s,d+4)}[nxt]
        return pltpu.make_async_remote_copy(land.at[idx,pl.ds(r0,rn)],lks[p].at[sl],ssem.at[p,idx],rsem.at[semoff[p]+sl],device_id=dev,device_id_type=MESH)
    def settle():
        rest_of=vland.at[pl.ds(0,total_dev-1)]
        bulk=pltpu.make_async_remote_copy(rest_of,rest_of,vsend,vrecv,device_id=(0,0),device_id_type=MESH)
        bulk.wait_recv()
        bulk.wait_send()
        vo_ref[...]=jnp.sum(vland[...],axis=0)
        back()
        for batch in range(2):
            strips32[...]=returned[batch*peers:(batch+1)*peers].astype(jnp.float32)
            join_strips(picks_ref[batch],strips32,res_ref.at[batch])
    for i,(p,it) in enumerate(seq):
        r0,rn,_=parts[p]
        if i==len(seq)*GIVE_NUM//GIVE_DEN: back=give_back(s,d,me,peers,sendbuf,returned,tlocal,tsend,trecv)
        if i==len(seq)*SETTLE_NUM//SETTLE_DEN: settle()
        if i+NB-1<len(seq):
            guarded(conds(seq[i+NB-1][1]),lambda i=i: load(i+NB-1).start())
        def ev(i=i,p=p,it=it,r0=r0,rn=rn):
            dest=where(it)
            s2,z2,y2=dest
            idx=(s2*zn+z2)*2+y2
            con,nxt=contribs(p,it)
            lk=lks[p]
            load(i).wait()
            core_dsc(p,it,True).wait_recv()
            plain=[x for x in con if x[2] is None]
            cond=[x for x in con if x[2] is not None]
            def rdsc(dim,side):
                sl=slot(p,dim,side,dest)
                return pltpu.make_async_remote_copy(lk.at[sl],lk.at[sl],ssem.at[p,idx],rsem.at[semoff[p]+sl],device_id=sib,device_id_type=MESH),sl
            for dim,side,_ in plain: rdsc(dim,side)[0].wait_recv()
            for dim,side,cnd in cond:
                pl.when(cnd)(lambda dim=dim,side=side: rdsc(dim,side)[0].wait_recv())
            if not cond: variants=[(None,plain)]
            elif len(cond)==1:
                variants=[(cond[0][2],plain+cond),(jnp.logical_not(cond[0][2]),plain)]
            else:
                a,b=cond
                variants=[(jnp.logical_and(a[2],b[2]),plain+cond),(jnp.logical_and(a[2],jnp.logical_not(b[2])),plain+[a]),
                          (jnp.logical_and(jnp.logical_not(a[2]),b[2]),plain+[b])]
            def total(lst):
                slots=[slot(p,dim,side,dest) for dim,side,_ in lst]
                CH=32 if rn%32==0 else 16
                def body(k,_):
                    ro=pl.multiple_of(k*CH,CH)
                    acc=buf[i%NB,pl.ds(ro,CH),:].astype(jnp.float32)+land[idx,pl.ds(r0+ro,CH),:].astype(jnp.float32)
                    for sl in slots: acc=acc+lk[sl,pl.ds(ro,CH),:].astype(jnp.float32)
                    if nxt is None: obuf[pl.ds(r0+ro,CH),:]=acc
                    else: land[idx,pl.ds(r0+ro,CH),:]=acc.astype(jnp.bfloat16)
                    return 0
                lax.fori_loop(0,rn//CH,body,0)
            for cnd,lst in variants:
                if cnd is None: total(lst)
                else: pl.when(cnd)(lambda lst=lst: total(lst))
            if nxt is not None: out_dsc(p,it,nxt).start()
            else: pltpu.make_async_copy(obuf.at[pl.ds(r0,rn)],o_ref.at[pl.ds(r0,rn)],osem.at[p]).start()
        guarded(conds(it),ev)
    for p,it in seq:
        def fin(p=p,it=it):
            core_dsc(p,it,False).wait_send()
            nxt=contribs(p,it)[1]
            if nxt is not None: out_dsc(p,it,nxt).wait_send()
        guarded(conds(it),fin)
    for p,(r0,rn,_) in enumerate(parts):
        pltpu.make_async_copy(obuf.at[pl.ds(r0,rn)],o_ref.at[pl.ds(r0,rn)],osem.at[p]).wait()


def slot_count(order,zn):
    sizes={"x":2,"y":2,"z":zn};cur=0
    for k,dim in enumerate(order):
        n=1
        for q in order[k+1:]: n*=sizes[q]
        if dim=="z": n*=2*zn
        cur+=n
    return cur
def rs(g,v,dx,y,place,picks,block,parts,zn,cid=1,nb=4):
    n=len(parts)
    cnt=[slot_count(p[2][::-1],zn) for p in parts]
    mx=max(p[1] for p in parts)
    return pl.pallas_call(functools.partial(rs_kernel,parts,zn),
        out_shape=[jax.ShapeDtypeStruct((480,1280),jnp.float32),jax.ShapeDtypeStruct(v.shape[1:],jnp.float32),
            jax.ShapeDtypeStruct((2,)+dx.shape,jnp.bfloat16)],
        in_specs=[pl.BlockSpec(memory_space=pl.ANY)]+[pl.BlockSpec(memory_space=pltpu.VMEM)]*5,
        out_specs=[pl.BlockSpec(memory_space=pl.ANY)]+[pl.BlockSpec(memory_space=pltpu.VMEM)]*2,
        scratch_shapes=[pltpu.VMEM((4*zn,480,1280),jnp.bfloat16),pltpu.VMEM((nb,mx,1280),jnp.bfloat16),pltpu.VMEM((480,1280),jnp.float32),pltpu.VMEM(v.shape,jnp.float32),
            pltpu.VMEM((4*zn,)+block,jnp.float32),pltpu.VMEM((2,4*zn)+block,jnp.bfloat16),pltpu.VMEM((8*zn,)+block,jnp.bfloat16)]
          +[pltpu.VMEM((cnt[p],parts[p][1],1280),jnp.bfloat16) for p in range(n)]
          +[pltpu.SemaphoreType.DMA((n,4*zn)),pltpu.SemaphoreType.DMA((sum(cnt),)),
          pltpu.SemaphoreType.DMA((n,4*zn)),pltpu.SemaphoreType.DMA((n,4*zn)),pltpu.SemaphoreType.DMA((nb,)),pltpu.SemaphoreType.DMA((n,))]+[pltpu.SemaphoreType.DMA]*5,
        compiler_params=pltpu.CompilerParams(collective_id=cid,has_side_effects=True,vmem_limit_bytes=62*2**20))(g,v,dx,y,place,picks)


def as_row(column):
    rows = column.shape[0]
    return jnp.broadcast_to(column, (rows, 128)).T[0:1, :]


def as_column(row):
    size = row.shape[1]
    return jnp.broadcast_to(row, (128, size)).T[:, 0:1]


def ones_where(flag):
    return jnp.where(flag, 1.0, 0.0)


def gather_events(parts,zn,place,own,w_ref,ssem,rsem,cs,cr):
    s,d,z,y,c=place
    KIND={"x":0,"y":1,"l":2,"r":3}
    def where(it):
        s2=1-s if it[0] else s
        y2=1-y if it[1] else y
        z2=z+it[2]
        return s2,z2,y2
    def dsc(p,it,kind):
        r0,rn,order=parts[p]
        s2,z2,y2=where(it)
        idx=s2*(2*zn)+z2*2+y2
        is_own=it==(0,0,0)
        src=own.at[pl.ds(r0,rn)] if is_own else w_ref.at[s2,(z2*2+y2)*2+c,pl.ds(r0,rn)]
        dst=w_ref.at[s2,(z2*2+y2)*2+c,pl.ds(r0,rn)]
        if kind=="core":
            dev=(s,(z*2+y)*2+1-c)
            return pltpu.make_async_remote_copy(src,dst,cs.at[p,idx],cr.at[p,idx],device_id=dev,device_id_type=MESH)
        dev={"x":(1-s,d),"y":(s,(z*2+1-y)*2+c),"l":(s,d-4),"r":(s,d+4)}[kind]
        return pltpu.make_async_remote_copy(src,dst,ssem.at[KIND[kind],p,idx],rsem.at[p,idx],device_id=dev,device_id_type=MESH)
    def cdsc(p,it):
        r0,rn,order=parts[p]
        s2,z2,y2=where(it)
        idx=s2*(2*zn)+z2*2+y2
        dst=w_ref.at[s2,(z2*2+y2)*2+1-c,pl.ds(r0,rn)]
        return pltpu.make_async_remote_copy(dst,dst,cs.at[p,idx],cr.at[p,idx],device_id=(s,(z*2+y)*2+1-c),device_id_type=MESH)
    def conds(it,kind):
        cs_=[]
        if it[2]<0: cs_.append(z+it[2]>=0)
        if it[2]>0: cs_.append(z+it[2]<=zn-1)
        if kind=="l": cs_.append(z>0)
        if kind=="r": cs_.append(z<zn-1)
        return cs_
    def guarded(cl,fn):
        if not cl: fn(); return
        e=cl[0]
        for q in cl[1:]: e=jnp.logical_and(e,q)
        pl.when(e)(fn)
    def sends(p,it):
        order=parts[p][2]
        a=arrival(order,it)
        ks=[]
        if a is not None and order[a]=="z": ks.append("l" if it[2]>0 else "r")
        for dim in order[(a+1) if a is not None else 0:]:
            ks += ["r","l"] if dim=="z" else [dim]
        ks.append("core")
        return ks
    evs=[]
    for p in range(len(parts)):
        for it in items():
            if abs(it[2])<zn: evs.append((hops(it),p,it))
    evs.sort(key=lambda e:e[0])
    first=[]
    later=[]
    for h,p,it in evs:
        def ev(p=p,it=it):
            if it!=(0,0,0): dsc(p,it,"x").wait_recv()
            for k in sends(p,it):
                guarded(conds((0,0,0),k), lambda k=k: dsc(p,it,k).start())
        (later if h else first).append(lambda it=it,ev=ev: guarded(conds(it,None),ev))
    def finish():
        for _,p,it in evs:
            def fin(p=p,it=it):
                cdsc(p,it).wait_recv()
                for k in sends(p,it):
                    guarded(conds((0,0,0),k), lambda k=k: dsc(p,it,k).wait_send())
            guarded(conds(it,None),fin)
    return first,later,finish


def enter_kernel(
    parts, zn, mats_ref, deal_in, vecs_ref, tokens_ref,
    w_ref, shared_ref, x_ref, cot_ref, picks_ref, place_ref,
    packet_ref, deal_ref, own, wide_rows, strips32, sendbuf, landed, order,
    own_sem, lsem, ssem, rsem, cs, cr, psend, precv, tsend, trecv,
):
    s, d, z, y, c = coords()
    peers = 4 * zn
    total = 2 * peers
    me = s * peers + d
    batches, rows, width = tokens_ref.shape
    f32, b16 = jnp.float32, jnp.bfloat16
    cast_in = pltpu.make_async_copy(mats_ref, wide_rows, own_sem)
    cast_in.start()
    signal_all(total, me, peers)
    deal_ref[...] = deal_in[...].astype(f32)
    lines = rows // 128
    for batch in range(batches):
        for line in range(lines):
            at = batch * lines + line
            packet_ref[at : at + 1, :] = deal_ref[batch : batch + 1, line * 128 : (line + 1) * 128]
    packet_ref[batches * lines :, :] = vecs_ref[...]
    wait_all(total)
    shared_ref[me] = packet_ref[...]

    def tell(step, carry):
        other = lax.rem(me + step, total)
        pltpu.make_async_remote_copy(
            packet_ref, shared_ref.at[me], psend, precv,
            device_id=(other // peers, lax.rem(other, peers)), device_id_type=MESH,
        ).start()
        return carry

    lax.fori_loop(1, total, tell, 0)
    cast_in.wait()
    own[...] = wide_rows[...].astype(b16)
    lc = pltpu.make_async_copy(own, w_ref.at[s, d], lsem)
    lc.start()
    start_events, rest_events, finish = gather_events(
        parts, zn, (s, d, z, y, c), own, w_ref, ssem, rsem, cs, cr
    )
    for event in start_events:
        event()
    sub = lax.broadcasted_iota(jnp.int32, (rows, rows), 0).astype(f32)
    lane = lax.broadcasted_iota(jnp.int32, (rows, rows), 1).astype(f32)
    mine_row = jnp.where(s == 0, deal_ref[0:1, :], deal_ref[1:2, :])
    mine_col = as_column(mine_row)
    rank_col = jnp.sum(ones_where(mine_row < mine_col), axis=1, keepdims=True)
    order[...] = ones_where(lane == rank_col).astype(b16)
    rank_row = jnp.sum(ones_where(mine_col < mine_row), axis=0, keepdims=True)
    place_ref[...] = ones_where(sub == rank_row).astype(b16)
    rest = shared_ref.at[pl.ds(0, total - 1)]
    bulk = pltpu.make_async_remote_copy(
        rest, rest, psend, precv, device_id=(0, 0), device_id_type=MESH
    )
    bulk.wait_recv()
    index_col = lax.broadcasted_iota(jnp.int32, (rows, 1), 0).astype(f32)
    ids_col = index_col + (d * rows).astype(f32)
    for batch in range(batches):

        def look(block, found):
            known = shared_ref[s * peers + block]
            for line in range(rows // 128):
                at = batch * (rows // 128) + line
                found = jnp.where(ids_col == known[at : at + 1, :], block.astype(f32), found)
            return found

        found = lax.fori_loop(0, peers, look, jnp.zeros((rows, 128), f32))
        key_col = jnp.sum(found, axis=1, keepdims=True) * rows + index_col
        key_row = as_row(key_col)
        rank_row = jnp.sum(ones_where(key_col < key_row), axis=0, keepdims=True)
        rank_col = jnp.sum(ones_where(key_row < key_col), axis=1, keepdims=True)
        picks_ref[batch] = ones_where(lane == rank_col).astype(b16)
        pick = ones_where(sub == rank_row).astype(b16)
        cut_strips(pick, tokens_ref.at[batch], strips32)
        sendbuf[batch] = strips32[...].astype(b16)

    landed[me] = sendbuf[s, d]

    early = len(rest_events) * HAND_NUM // HAND_DEN
    for event in rest_events[:early]:
        event()

    def give(step, carry):
        other = lax.rem(me + step, total)
        sec, dp = other // peers, lax.rem(other, peers)
        pltpu.make_async_remote_copy(
            sendbuf.at[sec, dp], landed.at[me], tsend, trecv.at[s],
            device_id=(sec, dp), device_id_type=MESH,
        ).start()
        return carry

    lax.fori_loop(1, total, give, 0)
    def take(kind, out_ref):
        pl.when(s == kind)(
            lambda: bulk_copy(landed, peers - 1, tsend, trecv.at[kind]).wait_recv()
        )
        pl.when(s != kind)(lambda: bulk_copy(landed, peers, tsend, trecv.at[kind]).wait_recv())
        strips32[...] = landed[pl.ds(kind * peers, peers)].astype(f32)
        join_strips(order[...], strips32, out_ref)

    middle = len(rest_events) * TAKE_NUM // TAKE_DEN
    for event in rest_events[early:middle]:
        event()
    take(0, x_ref)
    take(1, cot_ref)
    for event in rest_events[middle:]:
        event()
    finish()
    lc.wait()
    bulk.wait_send()
    most = landed.at[pl.ds(0, total - 1)]
    pltpu.make_async_remote_copy(
        most, most, tsend, trecv.at[0], device_id=(0, 0), device_id_type=MESH
    ).wait_send()


def enter(mats, deal, vecs, tokens, parts, zn):
    n = len(parts)
    peers = 4 * zn
    batches, rows, width = tokens.shape
    packet = (batches * (rows // 128) + vecs.shape[0], 128)
    strip_rows = rows // peers * (width // 128)
    f32, b16 = jnp.float32, jnp.bfloat16
    vm = pl.BlockSpec(memory_space=pltpu.VMEM)
    hbm = pl.BlockSpec(memory_space=pl.ANY)
    dma = pltpu.SemaphoreType.DMA
    return pl.pallas_call(
        functools.partial(enter_kernel, parts, zn),
        out_shape=[
            jax.ShapeDtypeStruct((2, peers) + mats.shape, b16),
            jax.ShapeDtypeStruct((2 * peers,) + packet, f32),
            jax.ShapeDtypeStruct((rows, width), b16),
            jax.ShapeDtypeStruct((rows, width), b16),
            jax.ShapeDtypeStruct((batches, rows, rows), b16),
            jax.ShapeDtypeStruct((rows, rows), b16),
        ],
        in_specs=[hbm, vm, vm, vm],
        out_specs=[hbm, vm, vm, vm, vm, vm],
        scratch_shapes=[
            pltpu.VMEM(packet, f32),
            pltpu.VMEM(deal.shape, f32),
            pltpu.VMEM(mats.shape, b16),
            pltpu.VMEM(mats.shape, f32),
            pltpu.VMEM((peers, strip_rows, 128), f32),
            pltpu.VMEM((batches, peers, strip_rows, 128), b16),
            pltpu.VMEM((2 * peers, strip_rows, 128), b16),
            pltpu.VMEM((rows, rows), b16),
            dma, dma, dma((4, n, peers)), dma((n, peers)), dma((n, peers)), dma((n, peers)),
            dma, dma, dma, dma((2,)),
        ],
        compiler_params=pltpu.CompilerParams(
            collective_id=0, has_side_effects=True, vmem_limit_bytes=VMEM_LIMIT
        ),
        name="enter",
    )(mats, deal, vecs, tokens)


def one_hot(rank):
    rows = rank.shape[0]
    return (rank[None, :] == jnp.arange(rows, dtype=jnp.int32)[:, None]).astype(jnp.bfloat16)


def rank_of(key):
    return jnp.sum((key[None, :] < key[:, None]).astype(jnp.int32), axis=1)


def padded(flat):
    lead, size = flat.shape
    full = -(-size // 1024) * 1024
    return jnp.pad(flat, ((0, 0), (0, full - size))).reshape(lead, full // 128, 128)


def enter_plain(own, packet, deal, tokens, peers):
    section = lax.axis_index("section")
    batches, rows, width = tokens.shape
    per_peer = rows // peers
    shared = lax.all_gather(packet, BOTH, axis=0)
    low = own.astype(jnp.bfloat16)
    mats = lax.all_gather(low, BOTH, axis=0, tiled=True).reshape((2, peers) + own.shape)
    flat = shared.reshape(2, peers, -1)[:, :, : batches * rows]
    dealt = jnp.where(section == 0, flat[0], flat[1]).astype(jnp.int32).reshape(peers, batches, rows)
    own_rows = lax.axis_index("dp") * rows + jnp.arange(rows, dtype=jnp.int32)
    blocks = jnp.arange(peers, dtype=jnp.int32)
    picks = []
    sends = []
    for batch in range(batches):
        hit = dealt[:, batch][None, :, :] == own_rows[:, None, None]
        target = jnp.sum(jnp.where(hit, blocks[None, :, None], 0), axis=(1, 2))
        pick = one_hot(rank_of(target * rows + jnp.arange(rows, dtype=jnp.int32)))
        picks.append(pick.T)
        sends.append(nn(pick, tokens[batch]).astype(jnp.bfloat16))
    outgoing = jnp.stack(sends).reshape(2 * peers, per_peer, width)
    arrived = lax.all_to_all(outgoing, BOTH, split_axis=0, concat_axis=0, tiled=True)
    arrived = arrived.reshape(2, rows, width)
    place = one_hot(rank_of(jnp.where(section == 0, deal[0], deal[1])))
    x, cot = (tn(place, arrived[kind]).astype(jnp.bfloat16) for kind in range(2))
    return mats, shared, x, cot, jnp.stack(picks), place


def leave_plain(terms, small, down, final, place, picks, peers):
    sections, _, rows, width = terms.shape
    terms = terms.reshape(sections * peers * rows, width)
    total = lax.psum_scatter(terms, BOTH, scatter_dimension=0, tiled=True).astype(jnp.float32)
    small = lax.psum_scatter(small, BOTH, scatter_dimension=0, tiled=True)[0]
    back = jnp.stack([nn(place, down), nn(place, final)]).astype(jnp.bfloat16)
    count = down.shape[0]
    back = back.reshape(2 * peers, count // peers, width)
    back = lax.all_to_all(back, BOTH, split_axis=0, concat_axis=0, tiled=True)
    back = back.reshape(-1, count, width)
    results = jnp.stack([nn(picks[batch], back[batch]) for batch in range(back.shape[0])])
    return total, small, results.astype(jnp.bfloat16)


def local(entering, deal, seq_lens, mats, gains, biases):
    section = lax.axis_index("section")
    peers = lax.axis_size("dp")
    arrival = entering[0]
    batches, rows, width = arrival.shape
    per = 2 * width // peers
    direct = peers == 16
    vecs = jnp.concatenate([gains[0], biases[0]]).astype(jnp.bfloat16).astype(jnp.float32)
    known = batches * rows
    if direct:
        lines = known // 128
        full = -(-(lines * 128 + vecs.shape[0]) // 1024) * 8 - lines
        vecs = jnp.pad(vecs, (0, full * 128 - vecs.shape[0])).reshape(full, 128)
        entered = enter(mats[0], deal, vecs, arrival, GATHER_PARTS, peers // 4)
    else:
        packet = jnp.concatenate([deal.reshape(-1).astype(jnp.float32), vecs])
        packet = padded(packet[None])[0]
        entered = enter_plain(mats[0], packet, deal, arrival, peers)
    all_mats, shared, tokens, cotangent, picks, place = entered
    shared = shared.reshape(2, peers, -1)
    small = shared[:, :, batches * rows : batches * rows + 2 * per].reshape(2, peers, 2, per)
    small = jnp.swapaxes(small, 1, 2).reshape(2, 4, width)
    small = jnp.pad(small, ((0, 0), (0, 4), (0, 0)))
    all_mats = all_mats.reshape(2, 6 * width, width)
    final, terms, down, vec_grads = both_layers(
        all_mats, tokens, small, seq_lens[:, 0, :], cotangent
    )
    terms = terms.reshape(2, peers, -1, width)
    vec_terms = vec_grads[:, :4].reshape(2, 2, peers, per)
    vec_terms = padded(jnp.swapaxes(vec_terms, 1, 2).reshape(2 * peers, 2 * per))
    block = (rows // peers * (width // 128), 128)
    if direct:
        shard_mats, vec_total, results = rs(
            terms, vec_terms, down, final, place, picks, block, SCATTER_PARTS, peers // 4
        )
    else:
        shard_mats, vec_total, results = leave_plain(
            terms, vec_terms, down, final, place, picks, peers
        )
    vec_total = vec_total.reshape(-1)
    return (
        results[None],
        shard_mats[None],
        vec_total[None, :per],
        vec_total[None, per : 2 * per],
    )


def solution(mesh):
    in_specs = (
        P("section", None, "dp", None),
        P(None, "dp"),
        P(None, "dp", None),
        P("section", "dp", None),
        P("section", "dp"),
        P("section", "dp"),
    )
    out_specs = (
        P("section", None, "dp", None),
        P("section", "dp", None),
        P("section", "dp"),
        P("section", "dp"),
    )
    return jax.shard_map(local, mesh=mesh, in_specs=in_specs, out_specs=out_specs, check_vma=False)
```
